32 devices in a mesh: seq: 4 (over y, x), chan: 8 (over z, core).
Axes of the slice: x: 2, y: 2, z: 4, core: 2. Of those that a mesh axis runs over, the one named last changes fastest.
Arguments:
- query_in: bfloat16 [1024, 4096], P('seq', 'chan'), may hold values from -6 to 6
- key_in: bfloat16 [1024, 4096], P('seq', 'chan'), may hold values from -6 to 6
- value_in: bfloat16 [1024, 4096], P('seq', 'chan'), may hold values from -6 to 6
- filter_taps: bfloat16 [256, 1024], P('chan', 'seq'), may hold values from -1.05 to 1.05, as said below
- skip_gain: float32 [4096], P('chan'), may hold values from 0.5 to 1.5
- out_weight: bfloat16 [4096, 4096], P('chan'), may hold values from -0.09375 to 0.09375
Outputs:
- mixed_out: bfloat16 [1024, 4096], P('seq', 'chan')
The draws below stay inside these ranges and needn't reach their ends.
Inputs may be any that keep to these rules, and one draw needn't show every extreme that they name: `filter_taps`: taps of every filter; the filters differ in how fast their taps fade with the lag.
All inputs are finite; a program needn't handle non-finite values.
Results may differ from the reference program's by a relative error of at most 0.0057.
Values may be sent and summed in bfloat16 or wider, within the bound.
No kernel may reach another device: no remote copies, remote signals or barrier semaphores. Data moves between devices by JAX's collectives and lax.ppermute only.
A program may use at most 64 MiB of HBM per device.

```python
import jax
import jax.numpy as jnp

D = 4096
GROUP_CH = 16
FILTER_GROUPS = 256
SEQUENCE_LENGTH = 1024


def draw_filter_taps(key, part):
    random_key_split = jax.random.split(jax.random.fold_in(key, 11), 6)
    token_positions = jnp.arange(SEQUENCE_LENGTH, dtype=jnp.float32)
    slow_share = 0.5
    slow_group = jax.random.uniform(random_key_split[0], (FILTER_GROUPS,)) < slow_share
    slow_rate = jnp.exp(jax.random.uniform(random_key_split[1], (FILTER_GROUPS,), minval=jnp.log(0.1), maxval=jnp.log(1.0))) / SEQUENCE_LENGTH
    fast_rate = jnp.exp(jax.random.uniform(random_key_split[2], (FILTER_GROUPS,), minval=jnp.log(1.0 / 50.0), maxval=jnp.log(1.0 / 30.0)))
    decay_rate = jnp.where(slow_group, slow_rate, fast_rate)
    decay_profile = jnp.exp(-decay_rate[:, None] * token_positions[None, :])
    spike_location = jax.random.randint(random_key_split[3], (FILTER_GROUPS, 2), 1, SEQUENCE_LENGTH).astype(jnp.float32)
    spike_multiplier = jax.random.uniform(random_key_split[4], (FILTER_GROUPS, 2), minval=0.55, maxval=0.8)
    spike_falloff = jnp.prod(jnp.where(token_positions[None, None, :] >= spike_location[:, :, None], spike_multiplier[:, :, None], 1.0), axis=1)
    decay_profile = decay_profile * spike_falloff
    rough_part = jnp.clip(jax.random.normal(random_key_split[5], (FILTER_GROUPS, SEQUENCE_LENGTH)), -4.0, 4.0)
    scale_inv = jnp.sqrt(jnp.sum(decay_profile * decay_profile, axis=1, keepdims=True))
    return (decay_profile * rough_part / scale_inv).astype(jnp.bfloat16)


def steps_of(key, dims, shards, least, high):
    def one(dim, shards_of):
        steps = jax.random.uniform(jax.random.fold_in(jax.random.fold_in(key, 6), dim), (shards_of,), jnp.float32, least / len(shards), high / len(shards))
        return jnp.repeat(jnp.exp(steps), dims[dim] // shards_of).reshape((-1,) + (1,) * (len(dims) - dim - 1))

    factor_of = one(*shards[0])
    for cut in shards[1:]:
        factor_of = factor_of * one(*cut)
    return factor_of


def noise(own_key, dims, spread, limit, cuts=(), kind=jnp.bfloat16):
    array = spread * jax.random.normal(own_key, dims, jnp.float32)
    if cuts:
        array = array * steps_of(own_key, dims, cuts, -0.22, 0.18)
    return jnp.clip(array, -limit, limit).astype(kind)


def setup_inputs(seed: int = 0) -> dict:
    key_of = jax.random.split(jax.random.key(seed), 7)
    query_in = noise(key_of[0], (SEQUENCE_LENGTH, D), 1.0, 6.0, ((0, 4), (1, 8)))
    key_in = noise(key_of[1], (SEQUENCE_LENGTH, D), 1.0, 6.0, ((0, 4), (1, 8)))
    value_in = noise(key_of[2], (SEQUENCE_LENGTH, D), 1.0, 6.0, ((0, 4), (1, 8)))
    filter_taps = draw_filter_taps(jax.random.fold_in(key_of[6], 71), 0)
    skip_gain = jnp.clip(0.5 + 1.0 * jax.random.uniform(key_of[4], (D,), jnp.float32) ** steps_of(key_of[4], (D,), ((0, 8),), -0.2, 0.2), 0.5, 1.5)
    out_weight = noise(key_of[5], (D, D), D ** -0.5, 0.09375, ((0, 8),))
    return dict(query_in=query_in, key_in=key_in, value_in=value_in, filter_taps=filter_taps, skip_gain=skip_gain, out_weight=out_weight)


def reference(query_in, key_in, value_in, filter_taps, skip_gain, out_weight):
    mixed_in = (key_in.astype(jnp.float32) * value_in.astype(jnp.float32)).astype(jnp.bfloat16)
    signal = mixed_in.astype(jnp.float32).T
    length = signal.shape[1]
    per_channel = jnp.repeat(filter_taps.astype(jnp.float32), GROUP_CH, axis=0)
    spectrum = jnp.fft.rfft(signal, n=2 * length, axis=1) * jnp.fft.rfft(per_channel, n=2 * length, axis=1)
    convolved = jnp.fft.irfft(spectrum, n=2 * length, axis=1)[:, :length].T
    gated = (query_in.astype(jnp.float32) * (convolved + skip_gain[None, :] * mixed_in.astype(jnp.float32))).astype(jnp.bfloat16)
    return jnp.dot(gated, out_weight, preferred_element_type=jnp.float32).astype(jnp.bfloat16)
```

```python
import functools
import math

import jax
import jax.numpy as jnp
from jax import lax
from jax.experimental import pallas as pl
from jax.experimental.pallas import tpu as pltpu
from jax.sharding import PartitionSpec as P

LANES = 128
BF16 = jnp.bfloat16
F32 = jnp.float32
VMEM_LIMIT = 16 * 1024 * 1024


def params():
    return pltpu.CompilerParams(vmem_limit_bytes=VMEM_LIMIT)


def in_hbm(*arrays):
    return [pltpu.with_memory_space_constraint(a, pltpu.HBM) for a in arrays]


def in_vmem(*arrays):
    return [pltpu.with_memory_space_constraint(a, pltpu.VMEM) for a in arrays]


def lanes_at(block):
    return pl.ds(pl.multiple_of(block * LANES, LANES), LANES)


def rows_at(block, size):
    return pl.ds(pl.multiple_of(block * size, size), size)


def product_kernel(n_seq, me_ref, key_hbm, value_hbm, taps_hbm, mixed_ref, *rest):
    packed_refs, (key_ref, value_ref, taps_ref, taps_f32, arrived) = rest[:n_seq], rest[n_seq:]
    rows = key_ref.shape[0]
    groups, span = taps_ref.shape
    part = groups // n_seq
    loads = [
        pltpu.make_async_copy(source, target, arrived.at[i])
        for i, (source, target) in enumerate(
            [(taps_hbm, taps_ref), (key_hbm, key_ref), (value_hbm, value_ref)]
        )
    ]
    for load in loads:
        load.start()
    loads[0].wait()
    taps_f32[...] = taps_ref[...].astype(F32)
    for d in range(n_seq):
        own = taps_f32[rows_at(me_ref[0] ^ d, part), :]
        pieces = [own[:, k * LANES : (k + 1) * LANES] for k in range(span // LANES)]
        packed_refs[d][rows:, :] = jnp.concatenate(pieces, axis=0).astype(BF16)
    loads[1].wait()
    loads[2].wait()
    mixed_ref[...] = (key_ref[...].astype(F32) * value_ref[...].astype(F32)).astype(BF16)
    for d in range(n_seq):
        packed_refs[d][0:rows, :] = mixed_ref[:, lanes_at(me_ref[0] ^ d)]


def products(me, key_in, value_in, taps, n_seq):
    rows, width = key_in.shape
    groups, span = taps.shape
    tap_rows = (groups // n_seq) * (span // LANES)
    packed = jax.ShapeDtypeStruct((rows + tap_rows, LANES), BF16)
    return pl.pallas_call(
        functools.partial(product_kernel, n_seq),
        out_shape=[jax.ShapeDtypeStruct((rows, width), BF16)] + [packed] * n_seq,
        in_specs=[pl.BlockSpec(memory_space=pltpu.SMEM)] + [pl.BlockSpec(memory_space=pl.ANY)] * 3,
        out_specs=[pl.BlockSpec(memory_space=pltpu.VMEM)] * (n_seq + 1),
        scratch_shapes=[
            pltpu.VMEM((rows, width), BF16),
            pltpu.VMEM((rows, width), BF16),
            pltpu.VMEM((groups, span), BF16),
            pltpu.VMEM((groups, span), F32),
            pltpu.SemaphoreType.DMA((3,)),
        ],
        compiler_params=params(),
        name="products",
    )(me, *in_hbm(key_in, value_in, taps))


def conv_kernel(n_seq, rows, part, columns, me_ref, core_ref, weight_hbm, *refs):
    packed_refs = refs[:n_seq]
    out_refs = refs[n_seq : 2 * n_seq]
    weight_out, signal, tap_rows, lag_blocks, total, arrived = refs[2 * n_seq :]

    loads = []
    for i in range(weight_out.shape[1] // columns):
        source = weight_hbm.at[:, rows_at(2 * i + 1 - core_ref[0], columns)]
        target = weight_out.at[:, i * columns : (i + 1) * columns]
        loads.append(pltpu.make_async_copy(source, target, arrived.at[i]))
    for load in loads:
        load.start()

    per_shard = rows // LANES
    tiles = n_seq * per_shard
    group_width = LANES // part

    for d in range(n_seq):
        other = me_ref[0] ^ d
        signal[rows_at(other, rows), :] = packed_refs[d][0:rows, :]
        tap_rows[rows_at(other, part * per_shard), :] = packed_refs[d][rows:, :].astype(F32)

    from_lane = lax.broadcasted_iota(jnp.int32, (LANES, LANES), 0)
    to_lane = lax.broadcasted_iota(jnp.int32, (LANES, LANES), 1)
    flip = jnp.where((from_lane + to_lane) % LANES == 0, 1.0, 0.0).astype(BF16)
    tap_rows[...] = jnp.dot(tap_rows[...].astype(BF16), flip, preferred_element_type=F32)

    lower = to_lane <= from_lane
    zero_block = jnp.zeros((LANES, LANES), BF16)

    for g in range(part):
        lag_blocks[0:LANES, (2 * g + 1) * LANES : (2 * g + 2) * LANES] = zero_block
        before = jnp.zeros((LANES, LANES), F32)
        for k in range(tiles):
            row = tap_rows[k * part + g : k * part + g + 1, :]
            rolled = pltpu.roll(
                jnp.broadcast_to(row, (LANES, LANES)), 0, 1, stride=1, stride_axis=0
            )
            block = jnp.where(lower, rolled, before).astype(BF16)
            lag_blocks[k * LANES : (k + 1) * LANES, 2 * g * LANES : (2 * g + 1) * LANES] = block
            if k + 1 < tiles:
                lag_blocks[
                    (k + 1) * LANES : (k + 2) * LANES, (2 * g + 1) * LANES : (2 * g + 2) * LANES
                ] = block
            before = rolled

    step = 2 * LANES
    length = n_seq * rows
    lane_group = lax.broadcasted_iota(jnp.int32, (step, LANES), 1) // group_width
    total[...] = jnp.zeros_like(total)
    for first in range(0, length, 2 * step):
        left = signal[first : first + step, :]
        right = signal[first + step : first + 2 * step, :]
        masked = []
        for g in range(part):
            here = lane_group == g
            masked.append(
                jnp.concatenate(
                    [jnp.where(here, left, 0.0).astype(BF16), jnp.where(here, right, 0.0).astype(BF16)],
                    axis=1,
                )
            )
        both = jnp.dot(
            lag_blocks[0 : length - first, :],
            jnp.concatenate(masked, axis=0),
            preferred_element_type=F32,
        )
        total[first:length, :] += both[:, 0:LANES]
        total[first + step : length, :] += both[0 : length - first - step, LANES:]

    for d in range(n_seq):
        out_refs[d][...] = total[rows_at(me_ref[0] ^ d, rows), :].astype(BF16)
    for load in loads:
        load.wait()


def convolve(me, core, out_weight, packed, n_seq, rows, part, columns):
    tiles = n_seq * rows // LANES
    depth, total_columns = out_weight.shape
    chips = total_columns // (2 * columns)
    vmem = pl.BlockSpec(memory_space=pltpu.VMEM)
    smem = pl.BlockSpec(memory_space=pltpu.SMEM)
    return pl.pallas_call(
        functools.partial(conv_kernel, n_seq, rows, part, columns),
        out_shape=[jax.ShapeDtypeStruct((rows, LANES), BF16)] * n_seq
        + [jax.ShapeDtypeStruct((depth, chips * columns), out_weight.dtype)],
        in_specs=[smem, smem, pl.BlockSpec(memory_space=pl.ANY)] + [vmem] * n_seq,
        out_specs=[vmem] * (n_seq + 1),
        scratch_shapes=[
            pltpu.VMEM((n_seq * rows, LANES), BF16),
            pltpu.VMEM((tiles * part, LANES), F32),
            pltpu.VMEM((n_seq * rows, 2 * LANES * part), BF16),
            pltpu.VMEM((n_seq * rows, LANES), F32),
            pltpu.SemaphoreType.DMA((chips,)),
        ],
        compiler_params=params(),
        name="convolve",
    )(me, core, *in_hbm(out_weight), *packed)


def gate_kernel(n_seq, me_ref, query_ref, mixed_ref, skip_ref, *refs):
    conv_refs, out_ref = refs[:n_seq], refs[n_seq]
    for d in range(n_seq):
        lanes = lanes_at(me_ref[0] ^ d)
        direct = skip_ref[:, lanes] * mixed_ref[:, lanes].astype(F32)
        out_ref[:, lanes] = (
            query_ref[:, lanes].astype(F32) * (conv_refs[d][...].astype(F32) + direct)
        ).astype(BF16)


def gate(me, query_in, mixed_in, skip_gain, parts):
    vmem = pl.BlockSpec(memory_space=pltpu.VMEM)
    return pl.pallas_call(
        functools.partial(gate_kernel, len(parts)),
        out_shape=jax.ShapeDtypeStruct(query_in.shape, BF16),
        in_specs=[pl.BlockSpec(memory_space=pltpu.SMEM)] + [vmem] * (3 + len(parts)),
        out_specs=vmem,
        compiler_params=params(),
        name="gate",
    )(me, query_in, mixed_in, skip_gain.reshape(1, -1), *parts)


def load_block(weight_hbm, block, target, arrived):
    columns = target.shape[1]
    load = pltpu.make_async_copy(weight_hbm.at[:, rows_at(block, columns)], target, arrived)
    load.start()
    return load


def half_kernel(where_ref, own_ref, weight_hbm, out_ref, weight, arrived):
    load_block(weight_hbm, where_ref[0], weight, arrived).wait()
    out_ref[...] = jnp.dot(own_ref[...], weight[...], preferred_element_type=F32)


def add_half_kernel(chip_ref, half_ref, other_ref, weight_ref, out_ref):
    there = rows_at(chip_ref[0], out_ref.shape[1])
    out_ref[...] = (
        half_ref[...]
        + jnp.dot(other_ref[...], weight_ref[:, there], preferred_element_type=F32)
    ).astype(out_ref.dtype)


def two_kernel(where_ref, own_ref, other_ref, weight_hbm, other_weight, *refs):
    out_refs, weight, arrived = refs[:-2], refs[-2], refs[-1]
    columns = weight.shape[2]
    loads = [
        load_block(weight_hbm, where_ref[i], weight.at[i], arrived.at[i])
        for i in range(len(out_refs))
    ]
    n = len(out_refs)
    for i in range(n):
        there = rows_at(where_ref[n + i], columns)
        late = jnp.dot(other_ref[...], other_weight[:, there], preferred_element_type=F32)
        loads[i].wait()
        out_refs[i][...] = (
            late + jnp.dot(own_ref[...], weight[i], preferred_element_type=F32)
        ).astype(BF16)


def base_kernel(
    where_ref, own_ref, other_ref, weight_hbm, other_weight, pair_ref, first_ref, out_ref, weight, arrived
):
    columns = weight.shape[1]
    load = load_block(weight_hbm, where_ref[0], weight, arrived)
    there = rows_at(where_ref[1], columns)
    late = jnp.dot(other_ref[...], other_weight[:, there], preferred_element_type=F32)
    load.wait()
    base = (
        late
        + jnp.dot(own_ref[...], weight[...], preferred_element_type=F32)
        + pair_ref[...].astype(F32)
    )

    @pl.when(where_ref[2] == 1)
    def _():
        out_ref[...] = base + first_ref[...].astype(F32)

    @pl.when(where_ref[2] == 0)
    def _():
        out_ref[...] = base


def run_kernel(kernel, name, out_shape, scratch, scalars, *arrays, hbm=()):
    specs, given = [pl.BlockSpec(memory_space=pltpu.SMEM)] * (len(scalars) > 0), []
    if scalars:
        given.append(jnp.stack(scalars).astype(jnp.int32))
    for i, array in enumerate(arrays):
        space = pl.ANY if i in hbm else pltpu.VMEM
        specs.append(pl.BlockSpec(memory_space=space))
        given += in_hbm(array) if i in hbm else [array]
    vmem = pl.BlockSpec(memory_space=pltpu.VMEM)
    return pl.pallas_call(
        kernel,
        out_shape=out_shape,
        in_specs=specs,
        out_specs=[vmem] * len(out_shape) if isinstance(out_shape, list) else vmem,
        scratch_shapes=scratch,
        compiler_params=params(),
        name=name,
    )(*given)


def forward_kernel(own_ref, arrived_ref, out_ref):
    out_ref[...] = (own_ref[...].astype(F32) + arrived_ref[...].astype(F32)).astype(BF16)


def final_kernel(end_ref, base_ref, ends_hbm, middle_hbm, out_ref, last_ref, arrived):
    @pl.when(end_ref[0] == 1)
    def _():
        pltpu.make_async_copy(ends_hbm, last_ref, arrived).start()

    @pl.when(end_ref[0] == 0)
    def _():
        pltpu.make_async_copy(middle_hbm, last_ref, arrived).start()

    pltpu.make_async_copy(middle_hbm, last_ref, arrived).wait()
    out_ref[...] = (base_ref[...] + last_ref[...].astype(F32)).astype(BF16)


def finish(at_end, base, ends, middle):
    vmem = pl.BlockSpec(memory_space=pltpu.VMEM)
    anywhere = pl.BlockSpec(memory_space=pl.ANY)
    return pl.pallas_call(
        final_kernel,
        out_shape=jax.ShapeDtypeStruct(base.shape, BF16),
        in_specs=[pl.BlockSpec(memory_space=pltpu.SMEM), vmem, anywhere, anywhere],
        out_specs=vmem,
        scratch_shapes=[pltpu.VMEM(base.shape, BF16), pltpu.SemaphoreType.DMA(())],
        compiler_params=params(),
        name="final",
    )(at_end, base, ends, middle)


def fast_body(n_seq, n_chan, query_in, key_in, value_in, filter_taps, skip_gain, out_weight):
    rows, width = query_in.shape
    groups = filter_taps.shape[0]
    part = groups // n_seq
    columns = out_weight.shape[1] // n_chan
    seq = lax.axis_index("seq").astype(jnp.int32)
    chan = lax.axis_index("chan").astype(jnp.int32)
    chip, core = chan // 2, chan % 2
    me = seq.reshape(1)

    def over_seq(value, d):
        return lax.ppermute(value, "seq", [(i, i ^ d) for i in range(n_seq)])

    def over_chips(value, moves):
        return lax.ppermute(
            value, "chan", [(2 * a + c, 2 * b + c) for a, b in moves for c in range(2)]
        )

    def other_core(value):
        return lax.ppermute(value, "chan", [(i, i ^ 1) for i in range(n_chan)])

    mixed_in, *packed = products(me, key_in, value_in, filter_taps, n_seq)
    arrived = [packed[0]] + [over_seq(packed[d], d) for d in range(1, n_seq)]
    *convolved, for_other = convolve(
        me, core.reshape(1), out_weight, arrived, n_seq, rows, part, columns
    )
    returned = [convolved[0]] + [over_seq(convolved[d], d) for d in range(1, n_seq)]
    other_weight = other_core(for_other)
    gated = gate(me, query_in, mixed_in, skip_gain, returned)
    gated_other = other_core(gated)

    block = jax.ShapeDtypeStruct((rows, columns), BF16)
    block_f32 = jax.ShapeDtypeStruct((rows, columns), F32)
    one_weight = [pltpu.VMEM((width, columns), BF16), pltpu.SemaphoreType.DMA(())]
    two_weights = [pltpu.VMEM((2, width, columns), BF16), pltpu.SemaphoreType.DMA((2,))]

    def at(target):
        return 2 * target + core

    half = run_kernel(
        half_kernel, "half", block_f32, one_weight, [at(chip ^ 2)], gated, out_weight, hbm=(1,)
    )
    by_two = run_kernel(
        add_half_kernel, "by_two", block, [], [chip ^ 2], half, gated_other, other_weight
    )
    first = over_chips(by_two, [(0, 1), (3, 2), (1, 3), (2, 0)])
    by_three, by_one = run_kernel(
        two_kernel,
        "by_three_and_one",
        [block, block],
        two_weights,
        [at(chip ^ 3), at(chip ^ 1), chip ^ 3, chip ^ 1],
        gated,
        gated_other,
        out_weight,
        other_weight,
        hbm=(2,),
    )
    ends = over_chips(by_three, [(0, 3), (3, 0)])
    pair = over_chips(by_one, [(0, 1), (1, 0), (2, 3), (3, 2)])
    summed = run_kernel(forward_kernel, "forward", block, [], [], by_three, first)
    middle = over_chips(summed, [(1, 2), (2, 1)])
    at_end = ((chip == 0) | (chip == 3)).astype(jnp.int32)
    base = run_kernel(
        base_kernel,
        "base",
        block_f32,
        one_weight,
        [at(chip), chip, at_end],
        gated,
        gated_other,
        out_weight,
        other_weight,
        pair,
        first,
        hbm=(2,),
    )
    return finish(at_end.reshape(1), base, ends, middle)


def window_matrix(window, tile_size):
    reversed_window = window[:, ::-1]
    extended = jnp.concatenate(
        [reversed_window, jnp.zeros((window.shape[0], 1), window.dtype)], axis=1
    )
    repeated = jnp.tile(extended, (1, tile_size))[:, : tile_size * (2 * tile_size - 1)]
    return repeated.reshape(window.shape[0], tile_size, 2 * tile_size - 1)[:, :, tile_size - 1 :]


def accumulate(running, segment, tap_table, own_start):
    row_count, chan_width = running.shape
    group_count = tap_table.shape[0]
    tap_span = tap_table.shape[1] // 2
    group_width = chan_width // group_count
    block_rows = min(segment.shape[0], row_count)
    tile_size = math.gcd(math.gcd(block_rows, row_count), 128)
    out_tiles = row_count // tile_size
    in_tiles = block_rows // tile_size

    def one_block(step_index, current):
        block_start = step_index * block_rows
        in_blocks = lax.dynamic_slice_in_dim(segment, step_index * block_rows, block_rows, 0)
        in_blocks = in_blocks.reshape(in_tiles, tile_size, group_count, group_width)

        def add_block(previous):
            out_blocks = previous.reshape(out_tiles, tile_size, group_count, group_width)
            offset = own_start - block_start
            for lag_step in range(1 - in_tiles, out_tiles):
                tap_first = offset + lag_step * tile_size - (tile_size - 1) + tap_span
                window = lax.dynamic_slice_in_dim(tap_table, tap_first, 2 * tile_size - 1, 1)
                matrix = window_matrix(window, tile_size)
                first_out = max(0, lag_step)
                last_out = min(out_tiles, in_tiles + lag_step)
                addend = jnp.einsum(
                    "gij,qjgc->qigc",
                    matrix,
                    in_blocks[first_out - lag_step : last_out - lag_step],
                    preferred_element_type=jnp.float32,
                )
                out_blocks = out_blocks.at[first_out:last_out].add(addend)
            return out_blocks.reshape(previous.shape)

        def keep_same(previous):
            return previous

        needed = (block_start < own_start + row_count) & (block_start >= 0)
        return lax.cond(needed, add_block, keep_same, current)

    return lax.fori_loop(0, segment.shape[0] // block_rows, one_block, running)


def general_body(query_in, key_in, value_in, filter_taps, skip_gain, out_weight):
    row_count, chan_width = query_in.shape
    mixed_in = (key_in.astype(jnp.float32) * value_in.astype(jnp.float32)).astype(jnp.bfloat16)
    all_taps = lax.all_gather(filter_taps, "seq", axis=1, tiled=True)
    tap_table = jnp.concatenate([jnp.zeros_like(all_taps), all_taps], axis=1)
    seq_index = lax.axis_index("seq")
    own_start = seq_index * row_count
    zero_sum = jnp.zeros((row_count, chan_width), jnp.float32)
    convolved = accumulate(
        zero_sum, lax.all_gather(mixed_in, "seq", axis=0, tiled=True), tap_table, own_start
    )
    gated = (
        query_in.astype(jnp.float32)
        * (convolved + skip_gain[None, :] * mixed_in.astype(jnp.float32))
    ).astype(jnp.bfloat16)
    columns = lax.all_to_all(out_weight, "chan", split_axis=1, concat_axis=0, tiled=True)
    result = jnp.dot(
        lax.all_gather(gated, "chan", axis=1, tiled=True),
        columns,
        preferred_element_type=jnp.float32,
    )
    return result.astype(jnp.bfloat16)


def solution(mesh):
    n_seq, n_chan = mesh.shape["seq"], mesh.shape["chan"]

    def body(query_in, key_in, value_in, filter_taps, skip_gain, out_weight):
        rows, width = query_in.shape
        groups, span = filter_taps.shape
        part = groups // n_seq
        fits = (
            n_chan == 8
            and n_seq & (n_seq - 1) == 0
            and width == n_seq * LANES
            and part * n_seq == groups
            and part % 8 == 0
            and (part * (rows // LANES)) % 16 == 0
            and rows % (2 * LANES) == 0
            and (n_seq * rows) % (4 * LANES) == 0
            and span == rows
            and out_weight.shape[1] % (n_chan * LANES) == 0
        )
        run = functools.partial(fast_body, n_seq, n_chan) if fits else general_body
        return run(query_in, key_in, value_in, filter_taps, skip_gain, out_weight)

    placed = (
        P("seq", "chan"),
        P("seq", "chan"),
        P("seq", "chan"),
        P("chan", "seq"),
        P("chan"),
        P("chan", None),
    )
    return jax.shard_map(
        body, mesh=mesh, in_specs=placed, out_specs=P("seq", "chan"), check_vma=False
    )
```

```python
import functools
import math

import jax
import jax.numpy as jnp
from jax import lax
from jax.experimental import pallas as pl
from jax.experimental.pallas import tpu as pltpu
from jax.sharding import PartitionSpec as P

LANES = 128
BF16 = jnp.bfloat16
F32 = jnp.float32
VMEM_LIMIT = 16 * 1024 * 1024


def params():
    return pltpu.CompilerParams(vmem_limit_bytes=VMEM_LIMIT)


def in_hbm(*arrays):
    return [pltpu.with_memory_space_constraint(a, pltpu.HBM) for a in arrays]


def in_vmem(*arrays):
    return [pltpu.with_memory_space_constraint(a, pltpu.VMEM) for a in arrays]


def seq_place():
    return lax.axis_index("seq")


def chip_place():
    return lax.axis_index("chan") // 2


def core_place():
    return lax.axis_index("chan") % 2


def lanes_at(block):
    return pl.ds(pl.multiple_of(block * LANES, LANES), LANES)


def rows_at(block, size):
    return pl.ds(pl.multiple_of(block * size, size), size)


def product_kernel(n_seq, key_hbm, value_hbm, taps_hbm, query_hbm, skip_hbm, *refs):
    mixed_ref, query_ref, skip_ref, *packed_refs = refs[: n_seq + 3]
    key_ref, value_ref, taps_ref, taps_f32, arrived = refs[n_seq + 3 :]
    rows = key_ref.shape[0]
    groups, span = taps_ref.shape
    part = groups // n_seq
    loads = [
        pltpu.make_async_copy(source, target, arrived.at[i])
        for i, (source, target) in enumerate(
            [
                (taps_hbm, taps_ref),
                (key_hbm, key_ref),
                (value_hbm, value_ref),
                (query_hbm, query_ref),
                (skip_hbm, skip_ref),
            ]
        )
    ]
    for load in loads:
        load.start()
    loads[0].wait()
    taps_f32[...] = taps_ref[...].astype(F32)
    for d in range(n_seq):
        own = taps_f32[rows_at(seq_place() ^ d, part), :]
        pieces = [own[:, k * LANES : (k + 1) * LANES] for k in range(span // LANES)]
        packed_refs[d][rows:, :] = jnp.concatenate(pieces, axis=0).astype(BF16)
    loads[1].wait()
    loads[2].wait()
    mixed_ref[...] = (key_ref[...].astype(F32) * value_ref[...].astype(F32)).astype(BF16)
    for d in range(n_seq):
        packed_refs[d][0:rows, :] = mixed_ref[:, lanes_at(seq_place() ^ d)]
    loads[3].wait()
    loads[4].wait()


def products(key_in, value_in, taps, query_in, skip_gain, n_seq):
    rows, width = key_in.shape
    groups, span = taps.shape
    tap_rows = (groups // n_seq) * (span // LANES)
    here = jax.ShapeDtypeStruct((rows, width), BF16)
    packed = jax.ShapeDtypeStruct((rows + tap_rows, LANES), BF16)
    return pl.pallas_call(
        functools.partial(product_kernel, n_seq),
        out_shape=[here, here, jax.ShapeDtypeStruct((1, width), F32)] + [packed] * n_seq,
        in_specs=[pl.BlockSpec(memory_space=pl.ANY)] * 5,
        out_specs=[pl.BlockSpec(memory_space=pltpu.VMEM)] * (n_seq + 3),
        scratch_shapes=[
            pltpu.VMEM((rows, width), BF16),
            pltpu.VMEM((rows, width), BF16),
            pltpu.VMEM((groups, span), BF16),
            pltpu.VMEM((groups, span), F32),
            pltpu.SemaphoreType.DMA((5,)),
        ],
        compiler_params=params(),
        name="products",
    )(*in_hbm(key_in, value_in, taps, query_in, skip_gain.reshape(1, -1)))


def conv_kernel(n_seq, rows, part, *refs):
    packed_refs = refs[:n_seq]
    out_refs = refs[n_seq : 2 * n_seq]
    signal, tap_rows, lag_blocks, total = refs[2 * n_seq :]
    per_shard = rows // LANES
    tiles = n_seq * per_shard
    group_width = LANES // part

    for d in range(n_seq):
        other = seq_place() ^ d
        signal[rows_at(other, rows), :] = packed_refs[d][0:rows, :]
        tap_rows[rows_at(other, part * per_shard), :] = packed_refs[d][rows:, :].astype(F32)

    from_lane = lax.broadcasted_iota(jnp.int32, (LANES, LANES), 0)
    to_lane = lax.broadcasted_iota(jnp.int32, (LANES, LANES), 1)
    flip = jnp.where((from_lane + to_lane) % LANES == 0, 1.0, 0.0).astype(BF16)
    tap_rows[...] = jnp.dot(tap_rows[...].astype(BF16), flip, preferred_element_type=F32)

    lower = to_lane <= from_lane
    zero_block = jnp.zeros((LANES, LANES), BF16)

    for g in range(part):
        lag_blocks[0:LANES, (2 * g + 1) * LANES : (2 * g + 2) * LANES] = zero_block
        before = jnp.zeros((LANES, LANES), F32)
        for k in range(tiles):
            row = tap_rows[k * part + g : k * part + g + 1, :]
            rolled = pltpu.roll(
                jnp.broadcast_to(row, (LANES, LANES)), 0, 1, stride=1, stride_axis=0
            )
            block = jnp.where(lower, rolled, before).astype(BF16)
            lag_blocks[k * LANES : (k + 1) * LANES, 2 * g * LANES : (2 * g + 1) * LANES] = block
            if k + 1 < tiles:
                lag_blocks[
                    (k + 1) * LANES : (k + 2) * LANES, (2 * g + 1) * LANES : (2 * g + 2) * LANES
                ] = block
            before = rolled

    step = 2 * LANES
    length = n_seq * rows
    lane_group = lax.broadcasted_iota(jnp.int32, (step, LANES), 1) // group_width
    total[...] = jnp.zeros_like(total)
    for first in range(0, length, 2 * step):
        left = signal[first : first + step, :]
        right = signal[first + step : first + 2 * step, :]
        masked = []
        for g in range(part):
            here = lane_group == g
            masked.append(
                jnp.concatenate(
                    [jnp.where(here, left, 0.0).astype(BF16), jnp.where(here, right, 0.0).astype(BF16)],
                    axis=1,
                )
            )
        both = jnp.dot(
            lag_blocks[0 : length - first, :],
            jnp.concatenate(masked, axis=0),
            preferred_element_type=F32,
        )
        total[first:length, :] += both[:, 0:LANES]
        total[first + step : length, :] += both[0 : length - first - step, LANES:]

    for d in range(n_seq):
        out_refs[d][...] = total[rows_at(seq_place() ^ d, rows), :].astype(BF16)


def convolve(packed, n_seq, rows, part):
    tiles = n_seq * rows // LANES
    vmem = pl.BlockSpec(memory_space=pltpu.VMEM)
    return pl.pallas_call(
        functools.partial(conv_kernel, n_seq, rows, part),
        out_shape=[jax.ShapeDtypeStruct((rows, LANES), BF16)] * n_seq,
        in_specs=[vmem] * n_seq,
        out_specs=[vmem] * n_seq,
        scratch_shapes=[
            pltpu.VMEM((n_seq * rows, LANES), BF16),
            pltpu.VMEM((tiles * part, LANES), F32),
            pltpu.VMEM((n_seq * rows, 2 * LANES * part), BF16),
            pltpu.VMEM((n_seq * rows, LANES), F32),
        ],
        compiler_params=params(),
        name="convolve",
    )(*packed)


def gate_kernel(n_seq, query_ref, mixed_ref, skip_ref, *refs):
    conv_refs, out_ref = refs[:n_seq], refs[n_seq]
    for d in range(n_seq):
        lanes = lanes_at(seq_place() ^ d)
        direct = skip_ref[:, lanes] * mixed_ref[:, lanes].astype(F32)
        out_ref[:, lanes] = (
            query_ref[:, lanes].astype(F32) * (conv_refs[d][...].astype(F32) + direct)
        ).astype(BF16)


def gate(query_in, mixed_in, skip_gain, parts):
    vmem = pl.BlockSpec(memory_space=pltpu.VMEM)
    return pl.pallas_call(
        functools.partial(gate_kernel, len(parts)),
        out_shape=jax.ShapeDtypeStruct(query_in.shape, BF16),
        in_specs=[vmem] * (3 + len(parts)),
        out_specs=vmem,
        compiler_params=params(),
        name="gate",
    )(query_in, mixed_in, skip_gain, *parts)


def load_block(distance, weight_hbm, weight, arrived):
    block = rows_at(2 * (chip_place() ^ distance) + core_place(), weight.shape[1])
    load = pltpu.make_async_copy(weight_hbm.at[:, block], weight, arrived)
    load.start()
    return block, load


def half_kernel(own_ref, own_weight, out_ref, weight, arrived):
    load_block(2, own_weight, weight, arrived)[1].wait()
    out_ref[...] = jnp.dot(own_ref[...], weight[...], preferred_element_type=F32)


def add_half_kernel(half_ref, other_ref, other_weight, out_ref):
    block = rows_at(2 * (chip_place() ^ 2) + core_place(), out_ref.shape[1])
    late = jnp.dot(other_ref[...], other_weight[:, block], preferred_element_type=F32)
    out_ref[...] = (half_ref[...] + late).astype(BF16)


def both_halves(distance, own_ref, other_ref, own_weight, other_weight, weight, arrived):
    block, load = load_block(distance, own_weight, weight, arrived)
    late = jnp.dot(other_ref[...], other_weight[:, block], preferred_element_type=F32)
    load.wait()
    return late + jnp.dot(own_ref[...], weight[...], preferred_element_type=F32)


def block_kernel(distance, own_ref, other_ref, own_weight, other_weight, *refs):
    out_ref, weight, arrived = refs[-3:]
    out_ref[...] = both_halves(
        distance, own_ref, other_ref, own_weight, other_weight, weight, arrived
    ).astype(BF16)


def is_end():
    return (chip_place() == 0) | (chip_place() == 3)


def base_kernel(own_ref, other_ref, own_weight, other_weight, first_ref, *refs):
    early_refs, (out_ref, weight, arrived) = refs[:-3], refs[-3:]
    base = both_halves(0, own_ref, other_ref, own_weight, other_weight, weight, arrived)
    for early in early_refs:
        base += early[...].astype(F32)

    @pl.when(is_end())
    def _():
        out_ref[...] = base + first_ref[...].astype(F32)

    @pl.when(jnp.logical_not(is_end()))
    def _():
        out_ref[...] = base


def run_kernel(kernel, name, out_shape, scratch, *arrays, hbm=()):
    specs, given = [], []
    for i, array in enumerate(arrays):
        space = pl.ANY if i in hbm else pltpu.VMEM
        specs.append(pl.BlockSpec(memory_space=space))
        given += in_hbm(array) if i in hbm else [array]
    vmem = pl.BlockSpec(memory_space=pltpu.VMEM)
    return pl.pallas_call(
        kernel,
        out_shape=out_shape,
        in_specs=specs,
        out_specs=[vmem] * len(out_shape) if isinstance(out_shape, list) else vmem,
        scratch_shapes=scratch,
        compiler_params=params(),
        name=name,
    )(*given)


def forward_kernel(own_ref, arrived_ref, out_ref):
    @pl.when(is_end())
    def _():
        out_ref[...] = own_ref[...]

    @pl.when(jnp.logical_not(is_end()))
    def _():
        out_ref[...] = (own_ref[...].astype(F32) + arrived_ref[...].astype(F32)).astype(BF16)


def final_kernel(base_ref, pair_ref, mirror_ref, out_ref):
    arrived = pair_ref[...].astype(F32) + mirror_ref[...].astype(F32)
    out_ref[...] = (base_ref[...] + arrived).astype(BF16)


def fast_body(n_seq, n_chan, query_in, key_in, value_in, filter_taps, skip_gain, out_weight):
    rows, width = query_in.shape
    groups = filter_taps.shape[0]
    part = groups // n_seq
    columns = out_weight.shape[1] // n_chan
    def over_seq(value, d):
        return lax.ppermute(value, "seq", [(i, i ^ d) for i in range(n_seq)])

    def over_chips(value, moves):
        return lax.ppermute(
            value, "chan", [(2 * a + c, 2 * b + c) for a, b in moves for c in range(2)]
        )

    def other_core(value):
        return lax.ppermute(value, "chan", [(i, i ^ 1) for i in range(n_chan)])

    other_weight = other_core(out_weight)
    mixed_in, query, skip, *packed = products(
        key_in, value_in, filter_taps, query_in, skip_gain, n_seq
    )
    arrived = [packed[0]] + [over_seq(packed[d], d) for d in range(1, n_seq)]
    convolved = convolve(arrived, n_seq, rows, part)
    returned = [convolved[0]] + [over_seq(convolved[d], d) for d in range(1, n_seq)]
    gated = gate(query, mixed_in, skip, returned)
    gated_other = other_core(gated)

    block = jax.ShapeDtypeStruct((rows, columns), BF16)
    block_f32 = jax.ShapeDtypeStruct((rows, columns), F32)
    one_weight = [pltpu.VMEM((width, columns), BF16), pltpu.SemaphoreType.DMA(())]
    halves = (gated, gated_other, out_weight, other_weight)

    half = run_kernel(half_kernel, "half", block_f32, one_weight, gated, out_weight, hbm=(1,))
    by_two = run_kernel(add_half_kernel, "by_two", block, [], half, gated_other, other_weight)
    first = over_chips(by_two, [(0, 1), (3, 2), (1, 3), (2, 0)])
    by_one = run_kernel(
        functools.partial(block_kernel, 1), "by_one", block, one_weight, *halves, hbm=(2,)
    )
    pair = over_chips(by_one, [(0, 1), (1, 0), (2, 3), (3, 2)])
    by_three = run_kernel(
        functools.partial(block_kernel, 3), "by_three", block, one_weight, *halves, hbm=(2,)
    )
    summed = run_kernel(forward_kernel, "forward", block, [], by_three, first)
    mirror = over_chips(summed, [(0, 3), (3, 0), (1, 2), (2, 1)])
    base = run_kernel(base_kernel, "base", block_f32, one_weight, *halves, first, hbm=(2,))
    return run_kernel(final_kernel, "final", block, [], base, pair, mirror)


def window_matrix(window, tile_size):
    reversed_window = window[:, ::-1]
    extended = jnp.concatenate(
        [reversed_window, jnp.zeros((window.shape[0], 1), window.dtype)], axis=1
    )
    repeated = jnp.tile(extended, (1, tile_size))[:, : tile_size * (2 * tile_size - 1)]
    return repeated.reshape(window.shape[0], tile_size, 2 * tile_size - 1)[:, :, tile_size - 1 :]


def accumulate(running, segment, tap_table, own_start):
    row_count, chan_width = running.shape
    group_count = tap_table.shape[0]
    tap_span = tap_table.shape[1] // 2
    group_width = chan_width // group_count
    block_rows = min(segment.shape[0], row_count)
    tile_size = math.gcd(math.gcd(block_rows, row_count), 128)
    out_tiles = row_count // tile_size
    in_tiles = block_rows // tile_size

    def one_block(step_index, current):
        block_start = step_index * block_rows
        in_blocks = lax.dynamic_slice_in_dim(segment, step_index * block_rows, block_rows, 0)
        in_blocks = in_blocks.reshape(in_tiles, tile_size, group_count, group_width)

        def add_block(previous):
            out_blocks = previous.reshape(out_tiles, tile_size, group_count, group_width)
            offset = own_start - block_start
            for lag_step in range(1 - in_tiles, out_tiles):
                tap_first = offset + lag_step * tile_size - (tile_size - 1) + tap_span
                window = lax.dynamic_slice_in_dim(tap_table, tap_first, 2 * tile_size - 1, 1)
                matrix = window_matrix(window, tile_size)
                first_out = max(0, lag_step)
                last_out = min(out_tiles, in_tiles + lag_step)
                addend = jnp.einsum(
                    "gij,qjgc->qigc",
                    matrix,
                    in_blocks[first_out - lag_step : last_out - lag_step],
                    preferred_element_type=jnp.float32,
                )
                out_blocks = out_blocks.at[first_out:last_out].add(addend)
            return out_blocks.reshape(previous.shape)

        def keep_same(previous):
            return previous

        needed = (block_start < own_start + row_count) & (block_start >= 0)
        return lax.cond(needed, add_block, keep_same, current)

    return lax.fori_loop(0, segment.shape[0] // block_rows, one_block, running)


def general_body(query_in, key_in, value_in, filter_taps, skip_gain, out_weight):
    row_count, chan_width = query_in.shape
    mixed_in = (key_in.astype(jnp.float32) * value_in.astype(jnp.float32)).astype(jnp.bfloat16)
    all_taps = lax.all_gather(filter_taps, "seq", axis=1, tiled=True)
    tap_table = jnp.concatenate([jnp.zeros_like(all_taps), all_taps], axis=1)
    seq_index = lax.axis_index("seq")
    own_start = seq_index * row_count
    zero_sum = jnp.zeros((row_count, chan_width), jnp.float32)
    convolved = accumulate(
        zero_sum, lax.all_gather(mixed_in, "seq", axis=0, tiled=True), tap_table, own_start
    )
    gated = (
        query_in.astype(jnp.float32)
        * (convolved + skip_gain[None, :] * mixed_in.astype(jnp.float32))
    ).astype(jnp.bfloat16)
    columns = lax.all_to_all(out_weight, "chan", split_axis=1, concat_axis=0, tiled=True)
    result = jnp.dot(
        lax.all_gather(gated, "chan", axis=1, tiled=True),
        columns,
        preferred_element_type=jnp.float32,
    )
    return result.astype(jnp.bfloat16)


def solution(mesh):
    n_seq, n_chan = mesh.shape["seq"], mesh.shape["chan"]

    def body(query_in, key_in, value_in, filter_taps, skip_gain, out_weight):
        rows, width = query_in.shape
        groups, span = filter_taps.shape
        part = groups // n_seq
        fits = (
            n_chan == 8
            and n_seq & (n_seq - 1) == 0
            and width == n_seq * LANES
            and part * n_seq == groups
            and part % 8 == 0
            and (part * (rows // LANES)) % 16 == 0
            and rows % (2 * LANES) == 0
            and (n_seq * rows) % (4 * LANES) == 0
            and span == rows
            and out_weight.shape[1] % (n_chan * LANES) == 0
        )
        run = functools.partial(fast_body, n_seq, n_chan) if fits else general_body
        return run(query_in, key_in, value_in, filter_taps, skip_gain, out_weight)

    placed = (
        P("seq", "chan"),
        P("seq", "chan"),
        P("seq", "chan"),
        P("chan", "seq"),
        P("chan"),
        P("chan", None),
    )
    return jax.shard_map(
        body, mesh=mesh, in_specs=placed, out_specs=P("seq", "chan"), check_vma=False
    )
```

```python
import functools
import math

import jax
import jax.numpy as jnp
from jax import lax
from jax.experimental import pallas as pl
from jax.experimental.pallas import tpu as pltpu
from jax.sharding import PartitionSpec as P

LANES = 128
BF16 = jnp.bfloat16
F32 = jnp.float32
VMEM_LIMIT = 16 * 1024 * 1024


def params():
    return pltpu.CompilerParams(vmem_limit_bytes=VMEM_LIMIT)


def in_hbm(*arrays):
    return [pltpu.with_memory_space_constraint(a, pltpu.HBM) for a in arrays]


def in_vmem(*arrays):
    return [pltpu.with_memory_space_constraint(a, pltpu.VMEM) for a in arrays]


def far_first(n_seq):
    return sorted(range(n_seq), key=lambda d: -d.bit_count())


def seq_place():
    return lax.axis_index("seq")


def chip_place():
    return lax.axis_index("chan") // 2


def core_place():
    return lax.axis_index("chan") % 2


def lanes_at(block):
    return pl.ds(pl.multiple_of(block * LANES, LANES), LANES)


def rows_at(block, size):
    return pl.ds(pl.multiple_of(block * size, size), size)


def product_kernel(n_seq, key_hbm, value_hbm, taps_hbm, query_hbm, skip_hbm, *refs):
    mixed_ref, query_ref, skip_ref, *packed_refs = refs[: n_seq + 3]
    key_ref, value_ref, taps_ref, taps_f32, arrived = refs[n_seq + 3 :]
    rows = key_ref.shape[0]
    groups, span = taps_ref.shape
    part = groups // n_seq
    loads = [
        pltpu.make_async_copy(source, target, arrived.at[i])
        for i, (source, target) in enumerate(
            [
                (taps_hbm, taps_ref),
                (key_hbm, key_ref),
                (value_hbm, value_ref),
                (query_hbm, query_ref),
                (skip_hbm, skip_ref),
            ]
        )
    ]
    for load in loads:
        load.start()
    loads[0].wait()
    taps_f32[...] = taps_ref[...].astype(F32)
    for d in range(n_seq):
        own = taps_f32[rows_at(seq_place() ^ d, part), :]
        pieces = [own[:, k * LANES : (k + 1) * LANES] for k in range(span // LANES)]
        packed_refs[d][rows:, :] = jnp.concatenate(pieces, axis=0).astype(BF16)
    loads[1].wait()
    loads[2].wait()
    mixed_ref[...] = (key_ref[...].astype(F32) * value_ref[...].astype(F32)).astype(BF16)
    for d in range(n_seq):
        packed_refs[d][0:rows, :] = mixed_ref[:, lanes_at(seq_place() ^ d)]
    loads[3].wait()
    loads[4].wait()


def products(key_in, value_in, taps, query_in, skip_gain, n_seq):
    rows, width = key_in.shape
    groups, span = taps.shape
    tap_rows = (groups // n_seq) * (span // LANES)
    here = jax.ShapeDtypeStruct((rows, width), BF16)
    packed = jax.ShapeDtypeStruct((rows + tap_rows, LANES), BF16)
    return pl.pallas_call(
        functools.partial(product_kernel, n_seq),
        out_shape=[here, here, jax.ShapeDtypeStruct((1, width), F32)] + [packed] * n_seq,
        in_specs=[pl.BlockSpec(memory_space=pl.ANY)] * 5,
        out_specs=[pl.BlockSpec(memory_space=pltpu.VMEM)] * (n_seq + 3),
        scratch_shapes=[
            pltpu.VMEM((rows, width), BF16),
            pltpu.VMEM((rows, width), BF16),
            pltpu.VMEM((groups, span), BF16),
            pltpu.VMEM((groups, span), F32),
            pltpu.SemaphoreType.DMA((5,)),
        ],
        compiler_params=params(),
        name="products",
    )(*in_hbm(key_in, value_in, taps, query_in, skip_gain.reshape(1, -1)))


def conv_kernel(n_seq, rows, part, *refs):
    packed_refs = [refs[far_first(n_seq).index(d)] for d in range(n_seq)]
    out_refs = refs[n_seq : 2 * n_seq]
    signal, taps, total = refs[2 * n_seq :]
    per_shard = rows // LANES
    blocks = n_seq * per_shard
    group_width = LANES // part

    for d in range(n_seq):
        first = (seq_place() ^ d) * per_shard
        tap_rows = packed_refs[d][rows:, :].astype(F32)
        for k in range(per_shard):
            tokens = packed_refs[d][k * LANES : (k + 1) * LANES, :].astype(F32)
            signal[first + k] = tokens.T.astype(BF16)
            taps[first + k] = tap_rows[k * part : (k + 1) * part, :]

    below = lax.broadcasted_iota(jnp.int32, (LANES, LANES), 0)
    lane = lax.broadcasted_iota(jnp.int32, (LANES, LANES), 1)
    for g in range(part):
        here = slice(g * group_width, (g + 1) * group_width)
        before = jnp.zeros((LANES, LANES), F32)
        by_lag = []
        for e in range(blocks):
            rolled = pltpu.roll(
                jnp.broadcast_to(taps[e, g : g + 1, :], (LANES, LANES)), 0, 1, stride=1, stride_axis=0
            )
            by_lag.append(jnp.where(lane >= below, rolled, before).astype(BF16))
            before = rolled
        sums = [None] * blocks
        for e in range(0, blocks, 2):
            left = signal[0 : blocks - e, here, :].reshape((blocks - e) * group_width, LANES)
            both = jnp.dot(
                left, jnp.concatenate(by_lag[e : e + 2], axis=1), preferred_element_type=F32
            )
            for q in range(blocks - e):
                piece = both[q * group_width : (q + 1) * group_width, :]
                for k in range(2):
                    at = q + e + k
                    if at < blocks:
                        addend = piece[:, k * LANES : (k + 1) * LANES]
                        sums[at] = addend if sums[at] is None else sums[at] + addend
        for q in range(blocks):
            total[q, here, :] = sums[q]

    for d in range(n_seq):
        first = (seq_place() ^ d) * per_shard
        for k in range(per_shard):
            out_refs[d][k * LANES : (k + 1) * LANES, :] = total[first + k].T.astype(BF16)


def convolve(packed, n_seq, rows, part):
    blocks = n_seq * rows // LANES
    vmem = pl.BlockSpec(memory_space=pltpu.VMEM)
    return pl.pallas_call(
        functools.partial(conv_kernel, n_seq, rows, part),
        out_shape=[jax.ShapeDtypeStruct((rows, LANES), BF16)] * n_seq,
        in_specs=[vmem] * n_seq,
        out_specs=[vmem] * n_seq,
        scratch_shapes=[
            pltpu.VMEM((blocks, LANES, LANES), BF16),
            pltpu.VMEM((blocks, part, LANES), F32),
            pltpu.VMEM((blocks, LANES, LANES), F32),
        ],
        compiler_params=params(),
        name="convolve",
    )(*[packed[d] for d in far_first(n_seq)])


def gate_kernel(n_seq, query_ref, mixed_ref, skip_ref, *refs):
    conv_refs, out_ref = [refs[far_first(n_seq).index(d)] for d in range(n_seq)], refs[n_seq]
    for d in range(n_seq):
        lanes = lanes_at(seq_place() ^ d)
        direct = skip_ref[:, lanes] * mixed_ref[:, lanes].astype(F32)
        out_ref[:, lanes] = (
            query_ref[:, lanes].astype(F32) * (conv_refs[d][...].astype(F32) + direct)
        ).astype(BF16)


def gate(query_in, mixed_in, skip_gain, parts):
    vmem = pl.BlockSpec(memory_space=pltpu.VMEM)
    return pl.pallas_call(
        functools.partial(gate_kernel, len(parts)),
        out_shape=jax.ShapeDtypeStruct(query_in.shape, BF16),
        in_specs=[vmem] * (3 + len(parts)),
        out_specs=vmem,
        compiler_params=params(),
        name="gate",
    )(query_in, mixed_in, skip_gain, *[parts[d] for d in far_first(len(parts))])


def load_block(distance, weight_hbm, weight, arrived):
    block = rows_at(2 * (chip_place() ^ distance) + core_place(), weight.shape[1])
    load = pltpu.make_async_copy(weight_hbm.at[:, block], weight, arrived)
    load.start()
    return block, load


def half_kernel(own_ref, own_weight, out_ref, weight, arrived):
    load_block(2, own_weight, weight, arrived)[1].wait()
    out_ref[...] = jnp.dot(own_ref[...], weight[...], preferred_element_type=F32)


def add_half_kernel(half_ref, other_ref, other_weight, out_ref):
    block = rows_at(2 * (chip_place() ^ 2) + core_place(), out_ref.shape[1])
    late = jnp.dot(other_ref[...], other_weight[:, block], preferred_element_type=F32)
    out_ref[...] = (half_ref[...] + late).astype(BF16)


def both_halves(distance, own_ref, other_ref, own_weight, other_weight, weight, arrived):
    block, load = load_block(distance, own_weight, weight, arrived)
    late = jnp.dot(other_ref[...], other_weight[:, block], preferred_element_type=F32)
    load.wait()
    return late + jnp.dot(own_ref[...], weight[...], preferred_element_type=F32)


def block_kernel(distance, own_ref, other_ref, own_weight, other_weight, *refs):
    out_ref, weight, arrived = refs[-3:]
    out_ref[...] = both_halves(
        distance, own_ref, other_ref, own_weight, other_weight, weight, arrived
    ).astype(BF16)


def is_end():
    return (chip_place() == 0) | (chip_place() == 3)


def base_kernel(own_ref, other_ref, own_weight, other_weight, first_ref, *refs):
    early_refs, (out_ref, weight, arrived) = refs[:-3], refs[-3:]
    base = both_halves(0, own_ref, other_ref, own_weight, other_weight, weight, arrived)
    for early in early_refs:
        base += early[...].astype(F32)

    @pl.when(is_end())
    def _():
        out_ref[...] = base + first_ref[...].astype(F32)

    @pl.when(jnp.logical_not(is_end()))
    def _():
        out_ref[...] = base


def run_kernel(kernel, name, out_shape, scratch, *arrays, hbm=()):
    specs, given = [], []
    for i, array in enumerate(arrays):
        space = pl.ANY if i in hbm else pltpu.VMEM
        specs.append(pl.BlockSpec(memory_space=space))
        given += in_hbm(array) if i in hbm else [array]
    vmem = pl.BlockSpec(memory_space=pltpu.VMEM)
    return pl.pallas_call(
        kernel,
        out_shape=out_shape,
        in_specs=specs,
        out_specs=[vmem] * len(out_shape) if isinstance(out_shape, list) else vmem,
        scratch_shapes=scratch,
        compiler_params=params(),
        name=name,
    )(*given)


def forward_kernel(own_ref, arrived_ref, out_ref):
    @pl.when(is_end())
    def _():
        out_ref[...] = own_ref[...]

    @pl.when(jnp.logical_not(is_end()))
    def _():
        out_ref[...] = (own_ref[...].astype(F32) + arrived_ref[...].astype(F32)).astype(BF16)


def final_kernel(base_ref, pair_ref, mirror_ref, out_ref):
    arrived = pair_ref[...].astype(F32) + mirror_ref[...].astype(F32)
    out_ref[...] = (base_ref[...] + arrived).astype(BF16)


def fast_body(n_seq, n_chan, query_in, key_in, value_in, filter_taps, skip_gain, out_weight):
    rows, width = query_in.shape
    groups = filter_taps.shape[0]
    part = groups // n_seq
    columns = out_weight.shape[1] // n_chan
    def over_seq(value, d):
        return lax.ppermute(value, "seq", [(i, i ^ d) for i in range(n_seq)])

    def over_chips(value, moves):
        return lax.ppermute(
            value, "chan", [(2 * a + c, 2 * b + c) for a, b in moves for c in range(2)]
        )

    def other_core(value):
        return lax.ppermute(value, "chan", [(i, i ^ 1) for i in range(n_chan)])

    other_weight = other_core(out_weight)
    mixed_in, query, skip, *packed = products(
        key_in, value_in, filter_taps, query_in, skip_gain, n_seq
    )
    arrived = [packed[0]] + [over_seq(packed[d], d) for d in range(1, n_seq)]
    convolved = convolve(arrived, n_seq, rows, part)
    returned = [convolved[0]] + [over_seq(convolved[d], d) for d in range(1, n_seq)]
    gated = gate(query, mixed_in, skip, returned)
    gated_other = other_core(gated)

    block = jax.ShapeDtypeStruct((rows, columns), BF16)
    block_f32 = jax.ShapeDtypeStruct((rows, columns), F32)
    one_weight = [pltpu.VMEM((width, columns), BF16), pltpu.SemaphoreType.DMA(())]
    halves = (gated, gated_other, out_weight, other_weight)

    half = run_kernel(half_kernel, "half", block_f32, one_weight, gated, out_weight, hbm=(1,))
    by_two = run_kernel(add_half_kernel, "by_two", block, [], half, gated_other, other_weight)
    first = over_chips(by_two, [(0, 1), (3, 2), (1, 3), (2, 0)])
    by_one = run_kernel(
        functools.partial(block_kernel, 1), "by_one", block, one_weight, *halves, hbm=(2,)
    )
    pair = over_chips(by_one, [(0, 1), (1, 0), (2, 3), (3, 2)])
    by_three = run_kernel(
        functools.partial(block_kernel, 3), "by_three", block, one_weight, *halves, hbm=(2,)
    )
    summed = run_kernel(forward_kernel, "forward", block, [], by_three, first)
    mirror = over_chips(summed, [(0, 3), (3, 0), (1, 2), (2, 1)])
    base = run_kernel(base_kernel, "base", block_f32, one_weight, *halves, first, hbm=(2,))
    return run_kernel(final_kernel, "final", block, [], base, pair, mirror)


def window_matrix(window, tile_size):
    reversed_window = window[:, ::-1]
    extended = jnp.concatenate(
        [reversed_window, jnp.zeros((window.shape[0], 1), window.dtype)], axis=1
    )
    repeated = jnp.tile(extended, (1, tile_size))[:, : tile_size * (2 * tile_size - 1)]
    return repeated.reshape(window.shape[0], tile_size, 2 * tile_size - 1)[:, :, tile_size - 1 :]


def accumulate(running, segment, tap_table, own_start):
    row_count, chan_width = running.shape
    group_count = tap_table.shape[0]
    tap_span = tap_table.shape[1] // 2
    group_width = chan_width // group_count
    block_rows = min(segment.shape[0], row_count)
    tile_size = math.gcd(math.gcd(block_rows, row_count), 128)
    out_tiles = row_count // tile_size
    in_tiles = block_rows // tile_size

    def one_block(step_index, current):
        block_start = step_index * block_rows
        in_blocks = lax.dynamic_slice_in_dim(segment, step_index * block_rows, block_rows, 0)
        in_blocks = in_blocks.reshape(in_tiles, tile_size, group_count, group_width)

        def add_block(previous):
            out_blocks = previous.reshape(out_tiles, tile_size, group_count, group_width)
            offset = own_start - block_start
            for lag_step in range(1 - in_tiles, out_tiles):
                tap_first = offset + lag_step * tile_size - (tile_size - 1) + tap_span
                window = lax.dynamic_slice_in_dim(tap_table, tap_first, 2 * tile_size - 1, 1)
                matrix = window_matrix(window, tile_size)
                first_out = max(0, lag_step)
                last_out = min(out_tiles, in_tiles + lag_step)
                addend = jnp.einsum(
                    "gij,qjgc->qigc",
                    matrix,
                    in_blocks[first_out - lag_step : last_out - lag_step],
                    preferred_element_type=jnp.float32,
                )
                out_blocks = out_blocks.at[first_out:last_out].add(addend)
            return out_blocks.reshape(previous.shape)

        def keep_same(previous):
            return previous

        needed = (block_start < own_start + row_count) & (block_start >= 0)
        return lax.cond(needed, add_block, keep_same, current)

    return lax.fori_loop(0, segment.shape[0] // block_rows, one_block, running)


def general_body(query_in, key_in, value_in, filter_taps, skip_gain, out_weight):
    row_count, chan_width = query_in.shape
    mixed_in = (key_in.astype(jnp.float32) * value_in.astype(jnp.float32)).astype(jnp.bfloat16)
    all_taps = lax.all_gather(filter_taps, "seq", axis=1, tiled=True)
    tap_table = jnp.concatenate([jnp.zeros_like(all_taps), all_taps], axis=1)
    seq_index = lax.axis_index("seq")
    own_start = seq_index * row_count
    zero_sum = jnp.zeros((row_count, chan_width), jnp.float32)
    convolved = accumulate(
        zero_sum, lax.all_gather(mixed_in, "seq", axis=0, tiled=True), tap_table, own_start
    )
    gated = (
        query_in.astype(jnp.float32)
        * (convolved + skip_gain[None, :] * mixed_in.astype(jnp.float32))
    ).astype(jnp.bfloat16)
    columns = lax.all_to_all(out_weight, "chan", split_axis=1, concat_axis=0, tiled=True)
    result = jnp.dot(
        lax.all_gather(gated, "chan", axis=1, tiled=True),
        columns,
        preferred_element_type=jnp.float32,
    )
    return result.astype(jnp.bfloat16)


def solution(mesh):
    n_seq, n_chan = mesh.shape["seq"], mesh.shape["chan"]

    def body(query_in, key_in, value_in, filter_taps, skip_gain, out_weight):
        rows, width = query_in.shape
        groups, span = filter_taps.shape
        part = groups // n_seq
        fits = (
            n_chan == 8
            and n_seq & (n_seq - 1) == 0
            and width == n_seq * LANES
            and part * n_seq == groups
            and part % 8 == 0
            and (part * (rows // LANES)) % 16 == 0
            and rows % (2 * LANES) == 0
            and (n_seq * rows) % (4 * LANES) == 0
            and span == rows
            and out_weight.shape[1] % (n_chan * LANES) == 0
        )
        run = functools.partial(fast_body, n_seq, n_chan) if fits else general_body
        return run(query_in, key_in, value_in, filter_taps, skip_gain, out_weight)

    placed = (
        P("seq", "chan"),
        P("seq", "chan"),
        P("seq", "chan"),
        P("chan", "seq"),
        P("chan"),
        P("chan", None),
    )
    return jax.shard_map(
        body, mesh=mesh, in_specs=placed, out_specs=P("seq", "chan"), check_vma=False
    )
```

```python
import functools
import math

import jax
import jax.numpy as jnp
from jax import lax
from jax.experimental import pallas as pl
from jax.experimental.pallas import tpu as pltpu
from jax.sharding import PartitionSpec as P

LANES = 128
FWD = ((3, 1, 2, 0), (2, 3, 1, 0))
RET = ((3, 1, 2, 0), (2, 3, 1, 0))
BF16 = jnp.bfloat16
F32 = jnp.float32
VMEM_LIMIT = 16 * 1024 * 1024


def params():
    return pltpu.CompilerParams(vmem_limit_bytes=VMEM_LIMIT)


def in_hbm(*arrays):
    return [pltpu.with_memory_space_constraint(a, pltpu.HBM) for a in arrays]


def in_vmem(*arrays):
    return [pltpu.with_memory_space_constraint(a, pltpu.VMEM) for a in arrays]


def away(orders, k):
    return jnp.where(core_place() == 0, orders[0][k], orders[1][k])


def seq_place():
    return lax.axis_index("seq")


def chip_place():
    return lax.axis_index("chan") // 2


def core_place():
    return lax.axis_index("chan") % 2


def lanes_at(block):
    return pl.ds(pl.multiple_of(block * LANES, LANES), LANES)


def rows_at(block, size):
    return pl.ds(pl.multiple_of(block * size, size), size)


def product_kernel(n_seq, key_hbm, value_hbm, taps_hbm, query_hbm, skip_hbm, *refs):
    mixed_ref, query_ref, skip_ref, *packed_refs = refs[: n_seq + 3]
    key_ref, value_ref, taps_ref, taps_f32, arrived = refs[n_seq + 3 :]
    rows = key_ref.shape[0]
    groups, span = taps_ref.shape
    part = groups // n_seq
    loads = [
        pltpu.make_async_copy(source, target, arrived.at[i])
        for i, (source, target) in enumerate(
            [
                (taps_hbm, taps_ref),
                (key_hbm, key_ref),
                (value_hbm, value_ref),
                (query_hbm, query_ref),
                (skip_hbm, skip_ref),
            ]
        )
    ]
    for load in loads:
        load.start()
    loads[0].wait()
    taps_f32[...] = taps_ref[...].astype(F32)
    for slot, packed_ref in enumerate(packed_refs):
        own = taps_f32[rows_at(seq_place() ^ away(FWD, slot), part), :]
        pieces = [own[:, k * LANES : (k + 1) * LANES] for k in range(span // LANES)]
        packed_ref[rows:, :] = jnp.concatenate(pieces, axis=0).astype(BF16)
    loads[1].wait()
    loads[2].wait()
    mixed_ref[...] = (key_ref[...].astype(F32) * value_ref[...].astype(F32)).astype(BF16)
    for slot, packed_ref in enumerate(packed_refs):
        packed_ref[0:rows, :] = mixed_ref[:, lanes_at(seq_place() ^ away(FWD, slot))]
    loads[3].wait()
    loads[4].wait()


def products(key_in, value_in, taps, query_in, skip_gain, n_seq):
    rows, width = key_in.shape
    groups, span = taps.shape
    tap_rows = (groups // n_seq) * (span // LANES)
    here = jax.ShapeDtypeStruct((rows, width), BF16)
    packed = jax.ShapeDtypeStruct((rows + tap_rows, LANES), BF16)
    return pl.pallas_call(
        functools.partial(product_kernel, n_seq),
        out_shape=[here, here, jax.ShapeDtypeStruct((1, width), F32)] + [packed] * n_seq,
        in_specs=[pl.BlockSpec(memory_space=pl.ANY)] * 5,
        out_specs=[pl.BlockSpec(memory_space=pltpu.VMEM)] * (n_seq + 3),
        scratch_shapes=[
            pltpu.VMEM((rows, width), BF16),
            pltpu.VMEM((rows, width), BF16),
            pltpu.VMEM((groups, span), BF16),
            pltpu.VMEM((groups, span), F32),
            pltpu.SemaphoreType.DMA((5,)),
        ],
        compiler_params=params(),
        name="products",
    )(*in_hbm(key_in, value_in, taps, query_in, skip_gain.reshape(1, -1)))


def conv_kernel(n_seq, rows, part, *refs):
    packed_refs = refs[:n_seq]
    out_refs = refs[n_seq : 2 * n_seq]
    signal, taps, total = refs[2 * n_seq :]
    per_shard = rows // LANES
    blocks = n_seq * per_shard
    group_width = LANES // part

    for slot, packed_ref in enumerate(packed_refs):
        first = (seq_place() ^ away(FWD, slot)) * per_shard
        tap_rows = packed_ref[rows:, :].astype(F32)
        for k in range(per_shard):
            tokens = packed_ref[k * LANES : (k + 1) * LANES, :].astype(F32)
            signal[first + k] = tokens.T.astype(BF16)
            taps[first + k] = tap_rows[k * part : (k + 1) * part, :]

    below = lax.broadcasted_iota(jnp.int32, (LANES, LANES), 0)
    lane = lax.broadcasted_iota(jnp.int32, (LANES, LANES), 1)
    for g in range(part):
        here = slice(g * group_width, (g + 1) * group_width)
        before = jnp.zeros((LANES, LANES), F32)
        by_lag = []
        for e in range(blocks):
            rolled = pltpu.roll(
                jnp.broadcast_to(taps[e, g : g + 1, :], (LANES, LANES)), 0, 1, stride=1, stride_axis=0
            )
            by_lag.append(jnp.where(lane >= below, rolled, before).astype(BF16))
            before = rolled
        sums = [None] * blocks
        for e in range(0, blocks, 2):
            left = signal[0 : blocks - e, here, :].reshape((blocks - e) * group_width, LANES)
            both = jnp.dot(
                left, jnp.concatenate(by_lag[e : e + 2], axis=1), preferred_element_type=F32
            )
            for q in range(blocks - e):
                piece = both[q * group_width : (q + 1) * group_width, :]
                for k in range(2):
                    at = q + e + k
                    if at < blocks:
                        addend = piece[:, k * LANES : (k + 1) * LANES]
                        sums[at] = addend if sums[at] is None else sums[at] + addend
        for q in range(blocks):
            total[q, here, :] = sums[q]

    for slot, out_ref in enumerate(out_refs):
        first = (seq_place() ^ away(RET, slot)) * per_shard
        for k in range(per_shard):
            out_ref[k * LANES : (k + 1) * LANES, :] = total[first + k].T.astype(BF16)


def convolve(packed, n_seq, rows, part):
    blocks = n_seq * rows // LANES
    vmem = pl.BlockSpec(memory_space=pltpu.VMEM)
    return pl.pallas_call(
        functools.partial(conv_kernel, n_seq, rows, part),
        out_shape=[jax.ShapeDtypeStruct((rows, LANES), BF16)] * n_seq,
        in_specs=[vmem] * n_seq,
        out_specs=[vmem] * n_seq,
        scratch_shapes=[
            pltpu.VMEM((blocks, LANES, LANES), BF16),
            pltpu.VMEM((blocks, part, LANES), F32),
            pltpu.VMEM((blocks, LANES, LANES), F32),
        ],
        compiler_params=params(),
        name="convolve",
    )(*packed)


def gate_kernel(n_seq, query_ref, mixed_ref, skip_ref, *refs):
    conv_refs, out_ref = refs[:n_seq], refs[n_seq]
    for slot, conv_ref in enumerate(conv_refs):
        lanes = lanes_at(seq_place() ^ away(RET, slot))
        direct = skip_ref[:, lanes] * mixed_ref[:, lanes].astype(F32)
        out_ref[:, lanes] = (
            query_ref[:, lanes].astype(F32) * (conv_ref[...].astype(F32) + direct)
        ).astype(BF16)


def gate(query_in, mixed_in, skip_gain, parts):
    vmem = pl.BlockSpec(memory_space=pltpu.VMEM)
    return pl.pallas_call(
        functools.partial(gate_kernel, len(parts)),
        out_shape=jax.ShapeDtypeStruct(query_in.shape, BF16),
        in_specs=[vmem] * (3 + len(parts)),
        out_specs=vmem,
        compiler_params=params(),
        name="gate",
    )(query_in, mixed_in, skip_gain, *parts)


def load_block(distance, weight_hbm, weight, arrived):
    block = rows_at(2 * (chip_place() ^ distance) + core_place(), weight.shape[1])
    load = pltpu.make_async_copy(weight_hbm.at[:, block], weight, arrived)
    load.start()
    return block, load


def half_kernel(own_ref, own_weight, out_ref, weight, arrived):
    load_block(2, own_weight, weight, arrived)[1].wait()
    out_ref[...] = jnp.dot(own_ref[...], weight[...], preferred_element_type=F32)


def add_half_kernel(half_ref, other_ref, other_weight, out_ref):
    block = rows_at(2 * (chip_place() ^ 2) + core_place(), out_ref.shape[1])
    late = jnp.dot(other_ref[...], other_weight[:, block], preferred_element_type=F32)
    out_ref[...] = (half_ref[...] + late).astype(BF16)


def both_halves(distance, own_ref, other_ref, own_weight, other_weight, weight, arrived):
    block, load = load_block(distance, own_weight, weight, arrived)
    late = jnp.dot(other_ref[...], other_weight[:, block], preferred_element_type=F32)
    load.wait()
    return late + jnp.dot(own_ref[...], weight[...], preferred_element_type=F32)


def block_kernel(distance, own_ref, other_ref, own_weight, other_weight, *refs):
    out_ref, weight, arrived = refs[-3:]
    out_ref[...] = both_halves(
        distance, own_ref, other_ref, own_weight, other_weight, weight, arrived
    ).astype(BF16)


def is_end():
    return (chip_place() == 0) | (chip_place() == 3)


def base_kernel(own_ref, other_ref, own_weight, other_weight, first_ref, *refs):
    early_refs, (out_ref, weight, arrived) = refs[:-3], refs[-3:]
    base = both_halves(0, own_ref, other_ref, own_weight, other_weight, weight, arrived)
    for early in early_refs:
        base += early[...].astype(F32)

    @pl.when(is_end())
    def _():
        out_ref[...] = base + first_ref[...].astype(F32)

    @pl.when(jnp.logical_not(is_end()))
    def _():
        out_ref[...] = base


def run_kernel(kernel, name, out_shape, scratch, *arrays, hbm=()):
    specs, given = [], []
    for i, array in enumerate(arrays):
        space = pl.ANY if i in hbm else pltpu.VMEM
        specs.append(pl.BlockSpec(memory_space=space))
        given += in_hbm(array) if i in hbm else [array]
    vmem = pl.BlockSpec(memory_space=pltpu.VMEM)
    return pl.pallas_call(
        kernel,
        out_shape=out_shape,
        in_specs=specs,
        out_specs=[vmem] * len(out_shape) if isinstance(out_shape, list) else vmem,
        scratch_shapes=scratch,
        compiler_params=params(),
        name=name,
    )(*given)


def forward_kernel(own_ref, arrived_ref, out_ref):
    @pl.when(is_end())
    def _():
        out_ref[...] = own_ref[...]

    @pl.when(jnp.logical_not(is_end()))
    def _():
        out_ref[...] = (own_ref[...].astype(F32) + arrived_ref[...].astype(F32)).astype(BF16)


def final_kernel(base_ref, pair_ref, mirror_ref, out_ref):
    arrived = pair_ref[...].astype(F32) + mirror_ref[...].astype(F32)
    out_ref[...] = (base_ref[...] + arrived).astype(BF16)


def fast_body(n_seq, n_chan, query_in, key_in, value_in, filter_taps, skip_gain, out_weight):
    rows, width = query_in.shape
    groups = filter_taps.shape[0]
    part = groups // n_seq
    columns = out_weight.shape[1] // n_chan
    def over_seq(slots, orders):
        *going, staying = slots
        moved = []
        for k, value in enumerate(going):
            pairs = [
                (i * n_chan + j, (i ^ orders[j % 2][k]) * n_chan + j)
                for i in range(n_seq)
                for j in range(n_chan)
            ]
            moved.append(lax.ppermute(value, ("seq", "chan"), pairs))
        return moved + [staying]

    def over_chips(value, moves):
        return lax.ppermute(
            value, "chan", [(2 * a + c, 2 * b + c) for a, b in moves for c in range(2)]
        )

    def other_core(value):
        return lax.ppermute(value, "chan", [(i, i ^ 1) for i in range(n_chan)])

    other_weight = other_core(out_weight)
    mixed_in, query, skip, *packed = products(
        key_in, value_in, filter_taps, query_in, skip_gain, n_seq
    )
    arrived = over_seq(packed, FWD)
    convolved = convolve(arrived, n_seq, rows, part)
    returned = over_seq(convolved, RET)
    gated = gate(query, mixed_in, skip, returned)
    gated_other = other_core(gated)

    block = jax.ShapeDtypeStruct((rows, columns), BF16)
    block_f32 = jax.ShapeDtypeStruct((rows, columns), F32)
    one_weight = [pltpu.VMEM((width, columns), BF16), pltpu.SemaphoreType.DMA(())]
    halves = (gated, gated_other, out_weight, other_weight)

    half = run_kernel(half_kernel, "half", block_f32, one_weight, gated, out_weight, hbm=(1,))
    by_two = run_kernel(add_half_kernel, "by_two", block, [], half, gated_other, other_weight)
    first = over_chips(by_two, [(0, 1), (3, 2), (1, 3), (2, 0)])
    by_one = run_kernel(
        functools.partial(block_kernel, 1), "by_one", block, one_weight, *halves, hbm=(2,)
    )
    pair = over_chips(by_one, [(0, 1), (1, 0), (2, 3), (3, 2)])
    by_three = run_kernel(
        functools.partial(block_kernel, 3), "by_three", block, one_weight, *halves, hbm=(2,)
    )
    summed = run_kernel(forward_kernel, "forward", block, [], by_three, first)
    mirror = over_chips(summed, [(0, 3), (3, 0), (1, 2), (2, 1)])
    base = run_kernel(base_kernel, "base", block_f32, one_weight, *halves, first, hbm=(2,))
    return run_kernel(final_kernel, "final", block, [], base, pair, mirror)


def window_matrix(window, tile_size):
    reversed_window = window[:, ::-1]
    extended = jnp.concatenate(
        [reversed_window, jnp.zeros((window.shape[0], 1), window.dtype)], axis=1
    )
    repeated = jnp.tile(extended, (1, tile_size))[:, : tile_size * (2 * tile_size - 1)]
    return repeated.reshape(window.shape[0], tile_size, 2 * tile_size - 1)[:, :, tile_size - 1 :]


def accumulate(running, segment, tap_table, own_start):
    row_count, chan_width = running.shape
    group_count = tap_table.shape[0]
    tap_span = tap_table.shape[1] // 2
    group_width = chan_width // group_count
    block_rows = min(segment.shape[0], row_count)
    tile_size = math.gcd(math.gcd(block_rows, row_count), 128)
    out_tiles = row_count // tile_size
    in_tiles = block_rows // tile_size

    def one_block(step_index, current):
        block_start = step_index * block_rows
        in_blocks = lax.dynamic_slice_in_dim(segment, step_index * block_rows, block_rows, 0)
        in_blocks = in_blocks.reshape(in_tiles, tile_size, group_count, group_width)

        def add_block(previous):
            out_blocks = previous.reshape(out_tiles, tile_size, group_count, group_width)
            offset = own_start - block_start
            for lag_step in range(1 - in_tiles, out_tiles):
                tap_first = offset + lag_step * tile_size - (tile_size - 1) + tap_span
                window = lax.dynamic_slice_in_dim(tap_table, tap_first, 2 * tile_size - 1, 1)
                matrix = window_matrix(window, tile_size)
                first_out = max(0, lag_step)
                last_out = min(out_tiles, in_tiles + lag_step)
                addend = jnp.einsum(
                    "gij,qjgc->qigc",
                    matrix,
                    in_blocks[first_out - lag_step : last_out - lag_step],
                    preferred_element_type=jnp.float32,
                )
                out_blocks = out_blocks.at[first_out:last_out].add(addend)
            return out_blocks.reshape(previous.shape)

        def keep_same(previous):
            return previous

        needed = (block_start < own_start + row_count) & (block_start >= 0)
        return lax.cond(needed, add_block, keep_same, current)

    return lax.fori_loop(0, segment.shape[0] // block_rows, one_block, running)


def general_body(query_in, key_in, value_in, filter_taps, skip_gain, out_weight):
    row_count, chan_width = query_in.shape
    mixed_in = (key_in.astype(jnp.float32) * value_in.astype(jnp.float32)).astype(jnp.bfloat16)
    all_taps = lax.all_gather(filter_taps, "seq", axis=1, tiled=True)
    tap_table = jnp.concatenate([jnp.zeros_like(all_taps), all_taps], axis=1)
    seq_index = lax.axis_index("seq")
    own_start = seq_index * row_count
    zero_sum = jnp.zeros((row_count, chan_width), jnp.float32)
    convolved = accumulate(
        zero_sum, lax.all_gather(mixed_in, "seq", axis=0, tiled=True), tap_table, own_start
    )
    gated = (
        query_in.astype(jnp.float32)
        * (convolved + skip_gain[None, :] * mixed_in.astype(jnp.float32))
    ).astype(jnp.bfloat16)
    columns = lax.all_to_all(out_weight, "chan", split_axis=1, concat_axis=0, tiled=True)
    result = jnp.dot(
        lax.all_gather(gated, "chan", axis=1, tiled=True),
        columns,
        preferred_element_type=jnp.float32,
    )
    return result.astype(jnp.bfloat16)


def solution(mesh):
    n_seq, n_chan = mesh.shape["seq"], mesh.shape["chan"]

    def body(query_in, key_in, value_in, filter_taps, skip_gain, out_weight):
        rows, width = query_in.shape
        groups, span = filter_taps.shape
        part = groups // n_seq
        fits = (
            n_chan == 8
            and n_seq & (n_seq - 1) == 0
            and width == n_seq * LANES
            and part * n_seq == groups
            and part % 8 == 0
            and (part * (rows // LANES)) % 16 == 0
            and rows % (2 * LANES) == 0
            and (n_seq * rows) % (4 * LANES) == 0
            and span == rows
            and out_weight.shape[1] % (n_chan * LANES) == 0
        )
        run = functools.partial(fast_body, n_seq, n_chan) if fits else general_body
        return run(query_in, key_in, value_in, filter_taps, skip_gain, out_weight)

    placed = (
        P("seq", "chan"),
        P("seq", "chan"),
        P("seq", "chan"),
        P("chan", "seq"),
        P("chan"),
        P("chan", None),
    )
    return jax.shard_map(
        body, mesh=mesh, in_specs=placed, out_specs=P("seq", "chan"), check_vma=False
    )
```

```python
import functools
import math

import jax
import jax.numpy as jnp
from jax import lax
from jax.experimental import pallas as pl
from jax.experimental.pallas import tpu as pltpu
from jax.sharding import PartitionSpec as P

LANES = 128
GOING = ((3, 1, 2, 0), (2, 3, 1, 0))
RETURNING = GOING
OUT_PARTS = 2
BF16 = jnp.bfloat16
F32 = jnp.float32
VMEM_LIMIT = 16 * 1024 * 1024


def params():
    return pltpu.CompilerParams(vmem_limit_bytes=VMEM_LIMIT)


def in_hbm(*arrays):
    return [pltpu.with_memory_space_constraint(a, pltpu.HBM) for a in arrays]


def away(orders, k):
    return jnp.where(core_place() == 0, orders[0][k], orders[1][k])


def seq_place():
    return lax.axis_index("seq")


def chip_place():
    return lax.axis_index("chan") // 2


def core_place():
    return lax.axis_index("chan") % 2


def lanes_at(block):
    return pl.ds(pl.multiple_of(block * LANES, LANES), LANES)


def rows_at(block, size):
    return pl.ds(pl.multiple_of(block * size, size), size)


def product_kernel(n_seq, key_hbm, value_hbm, taps_hbm, query_hbm, skip_hbm, weight_hbm, *refs):
    mixed_ref, query_ref, skip_ref, weight_ref, *packed_refs = refs[: n_seq + 4]
    key_ref, value_ref, taps_ref, taps_f32, arrived = refs[n_seq + 4 :]
    rows = key_ref.shape[0]
    groups, span = taps_ref.shape
    part = groups // n_seq
    loads = [
        pltpu.make_async_copy(source, target, arrived.at[i])
        for i, (source, target) in enumerate(
            [
                (taps_hbm, taps_ref),
                (key_hbm, key_ref),
                (value_hbm, value_ref),
                (query_hbm, query_ref),
                (skip_hbm, skip_ref),
            ]
        )
    ]
    for load in loads:
        load.start()
    loads.append(load_block(2, weight_hbm, weight_ref, arrived.at[5])[1])
    loads[0].wait()
    taps_f32[...] = taps_ref[...].astype(F32)
    for slot, packed_ref in enumerate(packed_refs):
        own = taps_f32[rows_at(seq_place() ^ away(GOING, slot), part), :]
        pieces = [own[:, k * LANES : (k + 1) * LANES] for k in range(span // LANES)]
        packed_ref[rows:, :] = jnp.concatenate(pieces, axis=0).astype(BF16)
    loads[1].wait()
    loads[2].wait()
    mixed_ref[...] = (key_ref[...].astype(F32) * value_ref[...].astype(F32)).astype(BF16)
    for slot, packed_ref in enumerate(packed_refs):
        packed_ref[0:rows, :] = mixed_ref[:, lanes_at(seq_place() ^ away(GOING, slot))]
    for load in loads[3:]:
        load.wait()


def products(key_in, value_in, taps, query_in, skip_gain, out_weight, columns, n_seq):
    rows, width = key_in.shape
    groups, span = taps.shape
    tap_rows = (groups // n_seq) * (span // LANES)
    here = jax.ShapeDtypeStruct((rows, width), BF16)
    packed = jax.ShapeDtypeStruct((rows + tap_rows, LANES), BF16)
    return pl.pallas_call(
        functools.partial(product_kernel, n_seq),
        out_shape=[
            here,
            here,
            jax.ShapeDtypeStruct((1, width), F32),
            jax.ShapeDtypeStruct((width, columns), BF16),
        ]
        + [packed] * n_seq,
        in_specs=[pl.BlockSpec(memory_space=pl.ANY)] * 6,
        out_specs=[pl.BlockSpec(memory_space=pltpu.VMEM)] * (n_seq + 4),
        scratch_shapes=[
            pltpu.VMEM((rows, width), BF16),
            pltpu.VMEM((rows, width), BF16),
            pltpu.VMEM((groups, span), BF16),
            pltpu.VMEM((groups, span), F32),
            pltpu.SemaphoreType.DMA((6,)),
        ],
        compiler_params=params(),
        name="products",
    )(*in_hbm(key_in, value_in, taps, query_in, skip_gain.reshape(1, -1), out_weight))


def conv_kernel(n_seq, rows, part, *refs):
    packed_refs = refs[:n_seq]
    out_refs = refs[n_seq : 2 * n_seq]
    signal, taps, total = refs[2 * n_seq :]
    per_shard = rows // LANES
    blocks = n_seq * per_shard
    group_width = LANES // part

    for slot, packed_ref in enumerate(packed_refs):
        first = (seq_place() ^ away(GOING, slot)) * per_shard
        tap_rows = packed_ref[rows:, :].astype(F32)
        for k in range(per_shard):
            tokens = packed_ref[k * LANES : (k + 1) * LANES, :].astype(F32)
            signal[first + k] = tokens.T.astype(BF16)
            taps[first + k] = tap_rows[k * part : (k + 1) * part, :]

    below = lax.broadcasted_iota(jnp.int32, (LANES, LANES), 0)
    lane = lax.broadcasted_iota(jnp.int32, (LANES, LANES), 1)
    for g in range(part):
        here = slice(g * group_width, (g + 1) * group_width)
        before = jnp.zeros((LANES, LANES), F32)
        by_lag = []
        for e in range(blocks):
            rolled = pltpu.roll(
                jnp.broadcast_to(taps[e, g : g + 1, :], (LANES, LANES)), 0, 1, stride=1, stride_axis=0
            )
            by_lag.append(jnp.where(lane >= below, rolled, before).astype(BF16))
            before = rolled
        sums = [None] * blocks
        for e in range(0, blocks, 2):
            left = signal[0 : blocks - e, here, :].reshape((blocks - e) * group_width, LANES)
            both = jnp.dot(
                left, jnp.concatenate(by_lag[e : e + 2], axis=1), preferred_element_type=F32
            )
            for q in range(blocks - e):
                piece = both[q * group_width : (q + 1) * group_width, :]
                for k in range(2):
                    at = q + e + k
                    if at < blocks:
                        addend = piece[:, k * LANES : (k + 1) * LANES]
                        sums[at] = addend if sums[at] is None else sums[at] + addend
        for q in range(blocks):
            total[q, here, :] = sums[q]

    for slot, out_ref in enumerate(out_refs):
        first = (seq_place() ^ away(RETURNING, slot)) * per_shard
        for k in range(per_shard):
            out_ref[k * LANES : (k + 1) * LANES, :] = total[first + k].T.astype(BF16)


def convolve(packed, n_seq, rows, part):
    blocks = n_seq * rows // LANES
    vmem = pl.BlockSpec(memory_space=pltpu.VMEM)
    return pl.pallas_call(
        functools.partial(conv_kernel, n_seq, rows, part),
        out_shape=[jax.ShapeDtypeStruct((rows, LANES), BF16)] * n_seq,
        in_specs=[vmem] * n_seq,
        out_specs=[vmem] * n_seq,
        scratch_shapes=[
            pltpu.VMEM((blocks, LANES, LANES), BF16),
            pltpu.VMEM((blocks, part, LANES), F32),
            pltpu.VMEM((blocks, LANES, LANES), F32),
        ],
        compiler_params=params(),
        name="convolve",
    )(*packed)


def gate_kernel(n_seq, query_ref, mixed_ref, skip_ref, *refs):
    conv_refs, out_ref = refs[:n_seq], refs[n_seq]
    for slot, conv_ref in enumerate(conv_refs):
        lanes = lanes_at(seq_place() ^ away(RETURNING, slot))
        direct = skip_ref[:, lanes] * mixed_ref[:, lanes].astype(F32)
        out_ref[:, lanes] = (
            query_ref[:, lanes].astype(F32) * (conv_ref[...].astype(F32) + direct)
        ).astype(BF16)


def gate(query_in, mixed_in, skip_gain, parts):
    vmem = pl.BlockSpec(memory_space=pltpu.VMEM)
    return pl.pallas_call(
        functools.partial(gate_kernel, len(parts)),
        out_shape=jax.ShapeDtypeStruct(query_in.shape, BF16),
        in_specs=[vmem] * (3 + len(parts)),
        out_specs=vmem,
        compiler_params=params(),
        name="gate",
    )(query_in, mixed_in, skip_gain, *parts)


def load_block(distance, weight_hbm, weight, arrived):
    block = rows_at(2 * (chip_place() ^ distance) + core_place(), weight.shape[1])
    load = pltpu.make_async_copy(weight_hbm.at[:, block], weight, arrived)
    load.start()
    return block, load


def half_kernel(own_ref, weight, out_ref):
    out_ref[...] = jnp.dot(own_ref[...], weight[...], preferred_element_type=F32)


def add_half_kernel(half_ref, other_ref, other_weight, out_ref):
    block = rows_at(2 * (chip_place() ^ 2) + core_place(), out_ref.shape[1])
    late = jnp.dot(other_ref[...], other_weight[:, block], preferred_element_type=F32)
    out_ref[...] = (half_ref[...] + late).astype(BF16)


def both_halves(distance, own_ref, other_ref, own_weight, other_weight, weight, arrived):
    block, load = load_block(distance, own_weight, weight, arrived)
    late = jnp.dot(other_ref[...], other_weight[:, block], preferred_element_type=F32)
    load.wait()
    return late + jnp.dot(own_ref[...], weight[...], preferred_element_type=F32)


def block_kernel(distance, own_ref, other_ref, own_weight, other_weight, *refs):
    out_ref, weight, arrived = refs[-3:]
    out_ref[...] = both_halves(
        distance, own_ref, other_ref, own_weight, other_weight, weight, arrived
    ).astype(BF16)


def is_end():
    return (chip_place() == 0) | (chip_place() == 3)


def base_kernel(own_ref, other_ref, own_weight, other_weight, first_ref, out_ref, weight, arrived):
    base = both_halves(0, own_ref, other_ref, own_weight, other_weight, weight, arrived)

    @pl.when(is_end())
    def _():
        out_ref[...] = base + first_ref[...].astype(F32)

    @pl.when(jnp.logical_not(is_end()))
    def _():
        out_ref[...] = base


def run_kernel(kernel, name, out_shape, scratch, *arrays, hbm=()):
    specs, given = [], []
    for i, array in enumerate(arrays):
        space = pl.ANY if i in hbm else pltpu.VMEM
        specs.append(pl.BlockSpec(memory_space=space))
        given += in_hbm(array) if i in hbm else [array]
    vmem = pl.BlockSpec(memory_space=pltpu.VMEM)
    return pl.pallas_call(
        kernel,
        out_shape=out_shape,
        in_specs=specs,
        out_specs=[vmem] * len(out_shape) if isinstance(out_shape, list) else vmem,
        scratch_shapes=scratch,
        compiler_params=params(),
        name=name,
    )(*given)


def forward_kernel(own_ref, arrived_ref, out_ref):
    @pl.when(is_end())
    def _():
        out_ref[...] = own_ref[...]

    @pl.when(jnp.logical_not(is_end()))
    def _():
        out_ref[...] = (own_ref[...].astype(F32) + arrived_ref[...].astype(F32)).astype(BF16)


def final_kernel(base_ref, pair_ref, mirror_ref, out_hbm, out_ref, arrived):
    rows = out_ref.shape[0] // OUT_PARTS
    stores = []
    for k in range(OUT_PARTS):
        here = slice(k * rows, (k + 1) * rows)
        arrivals = pair_ref[here, :].astype(F32) + mirror_ref[here, :].astype(F32)
        out_ref[here, :] = (base_ref[here, :] + arrivals).astype(BF16)
        store = pltpu.make_async_copy(out_ref.at[here, :], out_hbm.at[here, :], arrived.at[k])
        store.start()
        stores.append(store)
    for store in stores:
        store.wait()


def finish(base, pair, mirror):
    vmem = pl.BlockSpec(memory_space=pltpu.VMEM)
    return pl.pallas_call(
        final_kernel,
        out_shape=jax.ShapeDtypeStruct(base.shape, BF16),
        in_specs=[vmem] * 3,
        out_specs=pl.BlockSpec(memory_space=pl.ANY),
        scratch_shapes=[pltpu.VMEM(base.shape, BF16), pltpu.SemaphoreType.DMA((OUT_PARTS,))],
        compiler_params=params(),
        name="final",
    )(base, pair, mirror)


def fast_body(n_seq, n_chan, query_in, key_in, value_in, filter_taps, skip_gain, out_weight):
    rows, width = query_in.shape
    groups = filter_taps.shape[0]
    part = groups // n_seq
    columns = out_weight.shape[1] // n_chan
    def over_seq(slots, orders):
        *going, staying = slots
        moved = []
        for k, value in enumerate(going):
            pairs = [
                (i * n_chan + j, (i ^ orders[j % 2][k]) * n_chan + j)
                for i in range(n_seq)
                for j in range(n_chan)
            ]
            moved.append(lax.ppermute(value, ("seq", "chan"), pairs))
        return moved + [staying]

    def over_chips(value, moves):
        return lax.ppermute(
            value, "chan", [(2 * a + c, 2 * b + c) for a, b in moves for c in range(2)]
        )

    def other_core(value):
        return lax.ppermute(value, "chan", [(i, i ^ 1) for i in range(n_chan)])

    other_weight = other_core(out_weight)
    mixed_in, query, skip, weight, *packed = products(
        key_in, value_in, filter_taps, query_in, skip_gain, out_weight, columns, n_seq
    )
    arrived = over_seq(packed, GOING)
    convolved = convolve(arrived, n_seq, rows, part)
    returned = over_seq(convolved, RETURNING)
    gated = gate(query, mixed_in, skip, returned)
    gated_other = other_core(gated)

    block = jax.ShapeDtypeStruct((rows, columns), BF16)
    block_f32 = jax.ShapeDtypeStruct((rows, columns), F32)
    one_weight = [pltpu.VMEM((width, columns), BF16), pltpu.SemaphoreType.DMA(())]
    halves = (gated, gated_other, out_weight, other_weight)

    half = run_kernel(half_kernel, "half", block_f32, [], gated, weight)
    by_two = run_kernel(add_half_kernel, "by_two", block, [], half, gated_other, other_weight)
    first = over_chips(by_two, [(0, 1), (3, 2), (1, 3), (2, 0)])
    by_one = run_kernel(
        functools.partial(block_kernel, 1), "by_one", block, one_weight, *halves, hbm=(2,)
    )
    pair = over_chips(by_one, [(0, 1), (1, 0), (2, 3), (3, 2)])
    by_three = run_kernel(
        functools.partial(block_kernel, 3), "by_three", block, one_weight, *halves, hbm=(2,)
    )
    summed = run_kernel(forward_kernel, "forward", block, [], by_three, first)
    mirror = over_chips(summed, [(0, 3), (3, 0), (1, 2), (2, 1)])
    base = run_kernel(base_kernel, "base", block_f32, one_weight, *halves, first, hbm=(2,))
    return finish(base, pair, mirror)


def window_matrix(window, tile_size):
    reversed_window = window[:, ::-1]
    extended = jnp.concatenate(
        [reversed_window, jnp.zeros((window.shape[0], 1), window.dtype)], axis=1
    )
    repeated = jnp.tile(extended, (1, tile_size))[:, : tile_size * (2 * tile_size - 1)]
    return repeated.reshape(window.shape[0], tile_size, 2 * tile_size - 1)[:, :, tile_size - 1 :]


def accumulate(running, segment, tap_table, own_start):
    row_count, chan_width = running.shape
    group_count = tap_table.shape[0]
    tap_span = tap_table.shape[1] // 2
    group_width = chan_width // group_count
    block_rows = min(segment.shape[0], row_count)
    tile_size = math.gcd(math.gcd(block_rows, row_count), 128)
    out_tiles = row_count // tile_size
    in_tiles = block_rows // tile_size

    def one_block(step_index, current):
        block_start = step_index * block_rows
        in_blocks = lax.dynamic_slice_in_dim(segment, step_index * block_rows, block_rows, 0)
        in_blocks = in_blocks.reshape(in_tiles, tile_size, group_count, group_width)

        def add_block(previous):
            out_blocks = previous.reshape(out_tiles, tile_size, group_count, group_width)
            offset = own_start - block_start
            for lag_step in range(1 - in_tiles, out_tiles):
                tap_first = offset + lag_step * tile_size - (tile_size - 1) + tap_span
                window = lax.dynamic_slice_in_dim(tap_table, tap_first, 2 * tile_size - 1, 1)
                matrix = window_matrix(window, tile_size)
                first_out = max(0, lag_step)
                last_out = min(out_tiles, in_tiles + lag_step)
                addend = jnp.einsum(
                    "gij,qjgc->qigc",
                    matrix,
                    in_blocks[first_out - lag_step : last_out - lag_step],
                    preferred_element_type=jnp.float32,
                )
                out_blocks = out_blocks.at[first_out:last_out].add(addend)
            return out_blocks.reshape(previous.shape)

        def keep_same(previous):
            return previous

        needed = (block_start < own_start + row_count) & (block_start >= 0)
        return lax.cond(needed, add_block, keep_same, current)

    return lax.fori_loop(0, segment.shape[0] // block_rows, one_block, running)


def general_body(query_in, key_in, value_in, filter_taps, skip_gain, out_weight):
    row_count, chan_width = query_in.shape
    mixed_in = (key_in.astype(jnp.float32) * value_in.astype(jnp.float32)).astype(jnp.bfloat16)
    all_taps = lax.all_gather(filter_taps, "seq", axis=1, tiled=True)
    tap_table = jnp.concatenate([jnp.zeros_like(all_taps), all_taps], axis=1)
    seq_index = lax.axis_index("seq")
    own_start = seq_index * row_count
    zero_sum = jnp.zeros((row_count, chan_width), jnp.float32)
    convolved = accumulate(
        zero_sum, lax.all_gather(mixed_in, "seq", axis=0, tiled=True), tap_table, own_start
    )
    gated = (
        query_in.astype(jnp.float32)
        * (convolved + skip_gain[None, :] * mixed_in.astype(jnp.float32))
    ).astype(jnp.bfloat16)
    columns = lax.all_to_all(out_weight, "chan", split_axis=1, concat_axis=0, tiled=True)
    result = jnp.dot(
        lax.all_gather(gated, "chan", axis=1, tiled=True),
        columns,
        preferred_element_type=jnp.float32,
    )
    return result.astype(jnp.bfloat16)


def solution(mesh):
    n_seq, n_chan = mesh.shape["seq"], mesh.shape["chan"]

    def body(query_in, key_in, value_in, filter_taps, skip_gain, out_weight):
        rows, width = query_in.shape
        groups, span = filter_taps.shape
        part = groups // n_seq
        fits = (
            n_chan == 8
            and n_seq == len(GOING[0])
            and width == n_seq * LANES
            and part * n_seq == groups
            and part % 8 == 0
            and (part * (rows // LANES)) % 16 == 0
            and rows % (2 * LANES) == 0
            and (n_seq * rows) % (4 * LANES) == 0
            and span == rows
            and out_weight.shape[1] % (n_chan * LANES) == 0
        )
        run = functools.partial(fast_body, n_seq, n_chan) if fits else general_body
        return run(query_in, key_in, value_in, filter_taps, skip_gain, out_weight)

    placed = (
        P("seq", "chan"),
        P("seq", "chan"),
        P("seq", "chan"),
        P("chan", "seq"),
        P("chan"),
        P("chan", None),
    )
    return jax.shard_map(
        body, mesh=mesh, in_specs=placed, out_specs=P("seq", "chan"), check_vma=False
    )
```

```python
import functools
import math

import jax
import jax.numpy as jnp
from jax import lax
from jax.experimental import pallas as pl
from jax.experimental.pallas import tpu as pltpu
from jax.sharding import PartitionSpec as P

LANES = 128
GOING = ((3, 1, 2, 0), (2, 3, 1, 0))
RETURNING = GOING
OUT_PARTS = 2
BF16 = jnp.bfloat16
F32 = jnp.float32
VMEM_LIMIT = 16 * 1024 * 1024


def params():
    return pltpu.CompilerParams(vmem_limit_bytes=VMEM_LIMIT)


def in_hbm(*arrays):
    return [pltpu.with_memory_space_constraint(a, pltpu.HBM) for a in arrays]


def away(orders, k):
    return jnp.where(core_place() == 0, orders[0][k], orders[1][k])


def seq_place():
    return lax.axis_index("seq")


def chip_place():
    return lax.axis_index("chan") // 2


def core_place():
    return lax.axis_index("chan") % 2


def lanes_at(block):
    return pl.ds(pl.multiple_of(block * LANES, LANES), LANES)


def rows_at(block, size):
    return pl.ds(pl.multiple_of(block * size, size), size)


def product_kernel(n_seq, key_hbm, value_hbm, taps_hbm, *refs):
    mixed_ref, *packed_refs = refs[: n_seq + 1]
    key_ref, value_ref, taps_ref, taps_f32, arrived = refs[n_seq + 1 :]
    rows = key_ref.shape[0]
    groups, span = taps_ref.shape
    part = groups // n_seq
    loads = [
        pltpu.make_async_copy(source, target, arrived.at[i])
        for i, (source, target) in enumerate(
            [
                (taps_hbm, taps_ref),
                (key_hbm, key_ref),
                (value_hbm, value_ref),
            ]
        )
    ]
    for load in loads:
        load.start()
    loads[0].wait()
    taps_f32[...] = taps_ref[...].astype(F32)
    for slot, packed_ref in enumerate(packed_refs):
        own = taps_f32[rows_at(seq_place() ^ away(GOING, slot), part), :]
        pieces = [own[:, k * LANES : (k + 1) * LANES] for k in range(span // LANES)]
        packed_ref[rows:, :] = jnp.concatenate(pieces, axis=0).astype(BF16)
    loads[1].wait()
    loads[2].wait()
    mixed_ref[...] = (key_ref[...].astype(F32) * value_ref[...].astype(F32)).astype(BF16)
    for slot, packed_ref in enumerate(packed_refs):
        packed_ref[0:rows, :] = mixed_ref[:, lanes_at(seq_place() ^ away(GOING, slot))]


def products(key_in, value_in, taps, n_seq):
    rows, width = key_in.shape
    groups, span = taps.shape
    tap_rows = (groups // n_seq) * (span // LANES)
    here = jax.ShapeDtypeStruct((rows, width), BF16)
    packed = jax.ShapeDtypeStruct((rows + tap_rows, LANES), BF16)
    return pl.pallas_call(
        functools.partial(product_kernel, n_seq),
        out_shape=[here] + [packed] * n_seq,
        in_specs=[pl.BlockSpec(memory_space=pl.ANY)] * 3,
        out_specs=[pl.BlockSpec(memory_space=pltpu.VMEM)] * (n_seq + 1),
        scratch_shapes=[
            pltpu.VMEM((rows, width), BF16),
            pltpu.VMEM((rows, width), BF16),
            pltpu.VMEM((groups, span), BF16),
            pltpu.VMEM((groups, span), F32),
            pltpu.SemaphoreType.DMA((3,)),
        ],
        compiler_params=params(),
        name="products",
    )(*in_hbm(key_in, value_in, taps))


def fetch_kernel(after_hbm, query_hbm, skip_hbm, weight_hbm, query_ref, skip_ref, weight_ref, arrived):
    loads = [
        pltpu.make_async_copy(query_hbm, query_ref, arrived.at[0]),
        pltpu.make_async_copy(skip_hbm, skip_ref, arrived.at[1]),
    ]
    for load in loads:
        load.start()
    loads.append(load_block(2, weight_hbm, weight_ref, arrived.at[2])[1])
    for load in loads:
        load.wait()


def fetch(after, query_in, skip_gain, out_weight, columns):
    vmem = pl.BlockSpec(memory_space=pltpu.VMEM)
    width = query_in.shape[1]
    return pl.pallas_call(
        fetch_kernel,
        out_shape=[
            jax.ShapeDtypeStruct(query_in.shape, BF16),
            jax.ShapeDtypeStruct((1, width), F32),
            jax.ShapeDtypeStruct((width, columns), BF16),
        ],
        in_specs=[pl.BlockSpec(memory_space=pl.ANY)] * 4,
        out_specs=[vmem] * 3,
        scratch_shapes=[pltpu.SemaphoreType.DMA((3,))],
        compiler_params=params(),
        name="fetch",
    )(after, *in_hbm(query_in, skip_gain.reshape(1, -1), out_weight))


def conv_kernel(n_seq, rows, part, *refs):
    packed_refs = refs[:n_seq]
    out_refs = refs[n_seq : 2 * n_seq]
    signal, taps, total = refs[2 * n_seq :]
    per_shard = rows // LANES
    blocks = n_seq * per_shard
    group_width = LANES // part

    for slot, packed_ref in enumerate(packed_refs):
        first = (seq_place() ^ away(GOING, slot)) * per_shard
        tap_rows = packed_ref[rows:, :].astype(F32)
        for k in range(per_shard):
            tokens = packed_ref[k * LANES : (k + 1) * LANES, :].astype(F32)
            signal[first + k] = tokens.T.astype(BF16)
            taps[first + k] = tap_rows[k * part : (k + 1) * part, :]

    below = lax.broadcasted_iota(jnp.int32, (LANES, LANES), 0)
    lane = lax.broadcasted_iota(jnp.int32, (LANES, LANES), 1)
    for g in range(part):
        here = slice(g * group_width, (g + 1) * group_width)
        before = jnp.zeros((LANES, LANES), F32)
        by_lag = []
        for e in range(blocks):
            rolled = pltpu.roll(
                jnp.broadcast_to(taps[e, g : g + 1, :], (LANES, LANES)), 0, 1, stride=1, stride_axis=0
            )
            by_lag.append(jnp.where(lane >= below, rolled, before).astype(BF16))
            before = rolled
        sums = [None] * blocks
        for e in range(0, blocks, 2):
            left = signal[0 : blocks - e, here, :].reshape((blocks - e) * group_width, LANES)
            both = jnp.dot(
                left, jnp.concatenate(by_lag[e : e + 2], axis=1), preferred_element_type=F32
            )
            for q in range(blocks - e):
                piece = both[q * group_width : (q + 1) * group_width, :]
                for k in range(2):
                    at = q + e + k
                    if at < blocks:
                        addend = piece[:, k * LANES : (k + 1) * LANES]
                        sums[at] = addend if sums[at] is None else sums[at] + addend
        for q in range(blocks):
            total[q, here, :] = sums[q]

    for slot, out_ref in enumerate(out_refs):
        first = (seq_place() ^ away(RETURNING, slot)) * per_shard
        for k in range(per_shard):
            out_ref[k * LANES : (k + 1) * LANES, :] = total[first + k].T.astype(BF16)


def convolve(packed, n_seq, rows, part):
    blocks = n_seq * rows // LANES
    vmem = pl.BlockSpec(memory_space=pltpu.VMEM)
    return pl.pallas_call(
        functools.partial(conv_kernel, n_seq, rows, part),
        out_shape=[jax.ShapeDtypeStruct((rows, LANES), BF16)] * n_seq,
        in_specs=[vmem] * n_seq,
        out_specs=[vmem] * n_seq,
        scratch_shapes=[
            pltpu.VMEM((blocks, LANES, LANES), BF16),
            pltpu.VMEM((blocks, part, LANES), F32),
            pltpu.VMEM((blocks, LANES, LANES), F32),
        ],
        compiler_params=params(),
        name="convolve",
    )(*packed)


def gate_kernel(n_seq, query_ref, mixed_ref, skip_ref, *refs):
    conv_refs, out_ref = refs[:n_seq], refs[n_seq]
    for slot, conv_ref in enumerate(conv_refs):
        lanes = lanes_at(seq_place() ^ away(RETURNING, slot))
        direct = skip_ref[:, lanes] * mixed_ref[:, lanes].astype(F32)
        out_ref[:, lanes] = (
            query_ref[:, lanes].astype(F32) * (conv_ref[...].astype(F32) + direct)
        ).astype(BF16)


def gate(query_in, mixed_in, skip_gain, parts):
    vmem = pl.BlockSpec(memory_space=pltpu.VMEM)
    return pl.pallas_call(
        functools.partial(gate_kernel, len(parts)),
        out_shape=jax.ShapeDtypeStruct(query_in.shape, BF16),
        in_specs=[vmem] * (3 + len(parts)),
        out_specs=vmem,
        compiler_params=params(),
        name="gate",
    )(query_in, mixed_in, skip_gain, *parts)


def load_block(distance, weight_hbm, weight, arrived):
    block = rows_at(2 * (chip_place() ^ distance) + core_place(), weight.shape[1])
    load = pltpu.make_async_copy(weight_hbm.at[:, block], weight, arrived)
    load.start()
    return block, load


def half_kernel(own_ref, weight, out_ref):
    out_ref[...] = jnp.dot(own_ref[...], weight[...], preferred_element_type=F32)


def add_half_kernel(half_ref, other_ref, other_weight, out_ref):
    block = rows_at(2 * (chip_place() ^ 2) + core_place(), out_ref.shape[1])
    late = jnp.dot(other_ref[...], other_weight[:, block], preferred_element_type=F32)
    out_ref[...] = (half_ref[...] + late).astype(BF16)


def both_halves(distance, own_ref, other_ref, own_weight, other_weight, weight, arrived):
    block, load = load_block(distance, own_weight, weight, arrived)
    late = jnp.dot(other_ref[...], other_weight[:, block], preferred_element_type=F32)
    load.wait()
    return late + jnp.dot(own_ref[...], weight[...], preferred_element_type=F32)


def block_kernel(distance, own_ref, other_ref, own_weight, other_weight, *refs):
    out_ref, weight, arrived = refs[-3:]
    out_ref[...] = both_halves(
        distance, own_ref, other_ref, own_weight, other_weight, weight, arrived
    ).astype(BF16)


def is_end():
    return (chip_place() == 0) | (chip_place() == 3)


def base_kernel(own_ref, other_ref, own_weight, other_weight, first_ref, out_ref, weight, arrived):
    base = both_halves(0, own_ref, other_ref, own_weight, other_weight, weight, arrived)

    @pl.when(is_end())
    def _():
        out_ref[...] = base + first_ref[...].astype(F32)

    @pl.when(jnp.logical_not(is_end()))
    def _():
        out_ref[...] = base


def run_kernel(kernel, name, out_shape, scratch, *arrays, hbm=()):
    specs, given = [], []
    for i, array in enumerate(arrays):
        space = pl.ANY if i in hbm else pltpu.VMEM
        specs.append(pl.BlockSpec(memory_space=space))
        given += in_hbm(array) if i in hbm else [array]
    vmem = pl.BlockSpec(memory_space=pltpu.VMEM)
    return pl.pallas_call(
        kernel,
        out_shape=out_shape,
        in_specs=specs,
        out_specs=[vmem] * len(out_shape) if isinstance(out_shape, list) else vmem,
        scratch_shapes=scratch,
        compiler_params=params(),
        name=name,
    )(*given)


def forward_kernel(own_ref, arrived_ref, out_ref):
    @pl.when(is_end())
    def _():
        out_ref[...] = own_ref[...]

    @pl.when(jnp.logical_not(is_end()))
    def _():
        out_ref[...] = (own_ref[...].astype(F32) + arrived_ref[...].astype(F32)).astype(BF16)


def final_kernel(base_ref, pair_ref, mirror_ref, out_hbm, out_ref, arrived):
    rows = out_ref.shape[0] // OUT_PARTS
    stores = []
    for k in range(OUT_PARTS):
        here = slice(k * rows, (k + 1) * rows)
        arrivals = pair_ref[here, :].astype(F32) + mirror_ref[here, :].astype(F32)
        out_ref[here, :] = (base_ref[here, :] + arrivals).astype(BF16)
        store = pltpu.make_async_copy(out_ref.at[here, :], out_hbm.at[here, :], arrived.at[k])
        store.start()
        stores.append(store)
    for store in stores:
        store.wait()


def finish(base, pair, mirror):
    vmem = pl.BlockSpec(memory_space=pltpu.VMEM)
    return pl.pallas_call(
        final_kernel,
        out_shape=jax.ShapeDtypeStruct(base.shape, BF16),
        in_specs=[vmem] * 3,
        out_specs=pl.BlockSpec(memory_space=pl.ANY),
        scratch_shapes=[pltpu.VMEM(base.shape, BF16), pltpu.SemaphoreType.DMA((OUT_PARTS,))],
        compiler_params=params(),
        name="final",
    )(base, pair, mirror)


def fast_body(n_seq, n_chan, query_in, key_in, value_in, filter_taps, skip_gain, out_weight):
    rows, width = query_in.shape
    groups = filter_taps.shape[0]
    part = groups // n_seq
    columns = out_weight.shape[1] // n_chan
    def over_seq(slots, orders):
        *going, staying = slots
        moved = []
        for k, value in enumerate(going):
            pairs = [
                (i * n_chan + j, (i ^ orders[j % 2][k]) * n_chan + j)
                for i in range(n_seq)
                for j in range(n_chan)
            ]
            moved.append(lax.ppermute(value, ("seq", "chan"), pairs))
        return moved + [staying]

    def over_chips(value, moves):
        return lax.ppermute(
            value, "chan", [(2 * a + c, 2 * b + c) for a, b in moves for c in range(2)]
        )

    def other_core(value):
        return lax.ppermute(value, "chan", [(i, i ^ 1) for i in range(n_chan)])

    other_weight = other_core(out_weight)
    mixed_in, *packed = products(key_in, value_in, filter_taps, n_seq)
    arrived = over_seq(packed, GOING)
    query, skip, weight = fetch(packed[-1], query_in, skip_gain, out_weight, columns)
    convolved = convolve(arrived, n_seq, rows, part)
    returned = over_seq(convolved, RETURNING)
    gated = gate(query, mixed_in, skip, returned)
    gated_other = other_core(gated)

    block = jax.ShapeDtypeStruct((rows, columns), BF16)
    block_f32 = jax.ShapeDtypeStruct((rows, columns), F32)
    one_weight = [pltpu.VMEM((width, columns), BF16), pltpu.SemaphoreType.DMA(())]
    halves = (gated, gated_other, out_weight, other_weight)

    half = run_kernel(half_kernel, "half", block_f32, [], gated, weight)
    by_two = run_kernel(add_half_kernel, "by_two", block, [], half, gated_other, other_weight)
    first = over_chips(by_two, [(0, 1), (3, 2), (1, 3), (2, 0)])
    by_one = run_kernel(
        functools.partial(block_kernel, 1), "by_one", block, one_weight, *halves, hbm=(2,)
    )
    pair = over_chips(by_one, [(0, 1), (1, 0), (2, 3), (3, 2)])
    by_three = run_kernel(
        functools.partial(block_kernel, 3), "by_three", block, one_weight, *halves, hbm=(2,)
    )
    summed = run_kernel(forward_kernel, "forward", block, [], by_three, first)
    mirror = over_chips(summed, [(0, 3), (3, 0), (1, 2), (2, 1)])
    base = run_kernel(base_kernel, "base", block_f32, one_weight, *halves, first, hbm=(2,))
    return finish(base, pair, mirror)


def window_matrix(window, tile_size):
    reversed_window = window[:, ::-1]
    extended = jnp.concatenate(
        [reversed_window, jnp.zeros((window.shape[0], 1), window.dtype)], axis=1
    )
    repeated = jnp.tile(extended, (1, tile_size))[:, : tile_size * (2 * tile_size - 1)]
    return repeated.reshape(window.shape[0], tile_size, 2 * tile_size - 1)[:, :, tile_size - 1 :]


def accumulate(running, segment, tap_table, own_start):
    row_count, chan_width = running.shape
    group_count = tap_table.shape[0]
    tap_span = tap_table.shape[1] // 2
    group_width = chan_width // group_count
    block_rows = min(segment.shape[0], row_count)
    tile_size = math.gcd(math.gcd(block_rows, row_count), 128)
    out_tiles = row_count // tile_size
    in_tiles = block_rows // tile_size

    def one_block(step_index, current):
        block_start = step_index * block_rows
        in_blocks = lax.dynamic_slice_in_dim(segment, step_index * block_rows, block_rows, 0)
        in_blocks = in_blocks.reshape(in_tiles, tile_size, group_count, group_width)

        def add_block(previous):
            out_blocks = previous.reshape(out_tiles, tile_size, group_count, group_width)
            offset = own_start - block_start
            for lag_step in range(1 - in_tiles, out_tiles):
                tap_first = offset + lag_step * tile_size - (tile_size - 1) + tap_span
                window = lax.dynamic_slice_in_dim(tap_table, tap_first, 2 * tile_size - 1, 1)
                matrix = window_matrix(window, tile_size)
                first_out = max(0, lag_step)
                last_out = min(out_tiles, in_tiles + lag_step)
                addend = jnp.einsum(
                    "gij,qjgc->qigc",
                    matrix,
                    in_blocks[first_out - lag_step : last_out - lag_step],
                    preferred_element_type=jnp.float32,
                )
                out_blocks = out_blocks.at[first_out:last_out].add(addend)
            return out_blocks.reshape(previous.shape)

        def keep_same(previous):
            return previous

        needed = (block_start < own_start + row_count) & (block_start >= 0)
        return lax.cond(needed, add_block, keep_same, current)

    return lax.fori_loop(0, segment.shape[0] // block_rows, one_block, running)


def general_body(query_in, key_in, value_in, filter_taps, skip_gain, out_weight):
    row_count, chan_width = query_in.shape
    mixed_in = (key_in.astype(jnp.float32) * value_in.astype(jnp.float32)).astype(jnp.bfloat16)
    all_taps = lax.all_gather(filter_taps, "seq", axis=1, tiled=True)
    tap_table = jnp.concatenate([jnp.zeros_like(all_taps), all_taps], axis=1)
    seq_index = lax.axis_index("seq")
    own_start = seq_index * row_count
    zero_sum = jnp.zeros((row_count, chan_width), jnp.float32)
    convolved = accumulate(
        zero_sum, lax.all_gather(mixed_in, "seq", axis=0, tiled=True), tap_table, own_start
    )
    gated = (
        query_in.astype(jnp.float32)
        * (convolved + skip_gain[None, :] * mixed_in.astype(jnp.float32))
    ).astype(jnp.bfloat16)
    columns = lax.all_to_all(out_weight, "chan", split_axis=1, concat_axis=0, tiled=True)
    result = jnp.dot(
        lax.all_gather(gated, "chan", axis=1, tiled=True),
        columns,
        preferred_element_type=jnp.float32,
    )
    return result.astype(jnp.bfloat16)


def solution(mesh):
    n_seq, n_chan = mesh.shape["seq"], mesh.shape["chan"]

    def body(query_in, key_in, value_in, filter_taps, skip_gain, out_weight):
        rows, width = query_in.shape
        groups, span = filter_taps.shape
        part = groups // n_seq
        fits = (
            n_chan == 8
            and n_seq == len(GOING[0])
            and width == n_seq * LANES
            and part * n_seq == groups
            and part % 8 == 0
            and (part * (rows // LANES)) % 16 == 0
            and rows % (2 * LANES) == 0
            and (n_seq * rows) % (4 * LANES) == 0
            and span == rows
            and out_weight.shape[1] % (n_chan * LANES) == 0
        )
        run = functools.partial(fast_body, n_seq, n_chan) if fits else general_body
        return run(query_in, key_in, value_in, filter_taps, skip_gain, out_weight)

    placed = (
        P("seq", "chan"),
        P("seq", "chan"),
        P("seq", "chan"),
        P("chan", "seq"),
        P("chan"),
        P("chan", None),
    )
    return jax.shard_map(
        body, mesh=mesh, in_specs=placed, out_specs=P("seq", "chan"), check_vma=False
    )
```

```python
import functools
import math

import jax
import jax.numpy as jnp
from jax import lax
from jax.experimental import pallas as pl
from jax.experimental.pallas import tpu as pltpu
from jax.sharding import PartitionSpec as P

LANES = 128
DISTANCES = (2, 1, 3, 0)
EARLY_PARTS = 5
GOING = ((3, 1, 2, 0), (2, 3, 1, 0))
RETURNING = GOING
BF16 = jnp.bfloat16
F32 = jnp.float32
VMEM_LIMIT = 16 * 1024 * 1024


def params():
    return pltpu.CompilerParams(vmem_limit_bytes=VMEM_LIMIT)


def in_hbm(*arrays):
    return [pltpu.with_memory_space_constraint(a, pltpu.HBM) for a in arrays]


def away(orders, k):
    return jnp.where(core_place() == 0, orders[0][k], orders[1][k])


def seq_place():
    return lax.axis_index("seq")


def chip_place():
    return lax.axis_index("chan") // 2


def core_place():
    return lax.axis_index("chan") % 2


def lanes_at(block):
    return pl.ds(pl.multiple_of(block * LANES, LANES), LANES)


def rows_at(block, size):
    return pl.ds(pl.multiple_of(block * size, size), size)


def product_kernel(n_seq, key_hbm, value_hbm, taps_hbm, *refs):
    mixed_ref, *packed_refs = refs[: n_seq + 1]
    key_ref, value_ref, taps_ref, taps_f32, arrived = refs[n_seq + 1 :]
    rows = key_ref.shape[0]
    groups, span = taps_ref.shape
    part = groups // n_seq
    loads = [
        pltpu.make_async_copy(source, target, arrived.at[i])
        for i, (source, target) in enumerate(
            [
                (taps_hbm, taps_ref),
                (key_hbm, key_ref),
                (value_hbm, value_ref),
            ]
        )
    ]
    for load in loads:
        load.start()
    loads[0].wait()
    taps_f32[...] = taps_ref[...].astype(F32)
    for slot, packed_ref in enumerate(packed_refs):
        own = taps_f32[rows_at(seq_place() ^ away(GOING, slot), part), :]
        pieces = [own[:, k * LANES : (k + 1) * LANES] for k in range(span // LANES)]
        packed_ref[rows:, :] = jnp.concatenate(pieces, axis=0).astype(BF16)
    loads[1].wait()
    loads[2].wait()
    mixed_ref[...] = (key_ref[...].astype(F32) * value_ref[...].astype(F32)).astype(BF16)
    for slot, packed_ref in enumerate(packed_refs):
        packed_ref[0:rows, :] = mixed_ref[:, lanes_at(seq_place() ^ away(GOING, slot))]


def products(key_in, value_in, taps, n_seq):
    rows, width = key_in.shape
    groups, span = taps.shape
    tap_rows = (groups // n_seq) * (span // LANES)
    here = jax.ShapeDtypeStruct((rows, width), BF16)
    packed = jax.ShapeDtypeStruct((rows + tap_rows, LANES), BF16)
    return pl.pallas_call(
        functools.partial(product_kernel, n_seq),
        out_shape=[here] + [packed] * n_seq,
        in_specs=[pl.BlockSpec(memory_space=pl.ANY)] * 3,
        out_specs=[pl.BlockSpec(memory_space=pltpu.VMEM)] * (n_seq + 1),
        scratch_shapes=[
            pltpu.VMEM((rows, width), BF16),
            pltpu.VMEM((rows, width), BF16),
            pltpu.VMEM((groups, span), BF16),
            pltpu.VMEM((groups, span), F32),
            pltpu.SemaphoreType.DMA((3,)),
        ],
        compiler_params=params(),
        name="products",
    )(*in_hbm(key_in, value_in, taps))


def fetch_kernel(after_hbm, query_hbm, skip_hbm, weight_hbm, query_ref, skip_ref, weight_ref, arrived):
    loads = [
        pltpu.make_async_copy(query_hbm, query_ref, arrived.at[0]),
        pltpu.make_async_copy(skip_hbm, skip_ref, arrived.at[1]),
    ]
    for load in loads:
        load.start()
    for i, distance in enumerate(DISTANCES):
        loads.append(load_block(distance, weight_hbm, weight_ref.at[i], arrived.at[2 + i])[1])
    for load in loads:
        load.wait()


def fetch(after, query_in, skip_gain, out_weight, columns):
    vmem = pl.BlockSpec(memory_space=pltpu.VMEM)
    width = query_in.shape[1]
    return pl.pallas_call(
        fetch_kernel,
        out_shape=[
            jax.ShapeDtypeStruct(query_in.shape, BF16),
            jax.ShapeDtypeStruct((1, width), F32),
            jax.ShapeDtypeStruct((len(DISTANCES), width, columns), BF16),
        ],
        in_specs=[pl.BlockSpec(memory_space=pl.ANY)] * 4,
        out_specs=[vmem] * 3,
        scratch_shapes=[pltpu.SemaphoreType.DMA((2 + len(DISTANCES),))],
        compiler_params=params(),
        name="fetch",
    )(after, *in_hbm(query_in, skip_gain.reshape(1, -1), out_weight))


def conv_kernel(n_seq, rows, part, *refs):
    packed_refs = refs[:n_seq]
    out_refs = refs[n_seq : 2 * n_seq]
    signal, taps, total = refs[2 * n_seq :]
    per_shard = rows // LANES
    blocks = n_seq * per_shard
    group_width = LANES // part

    for slot, packed_ref in enumerate(packed_refs):
        first = (seq_place() ^ away(GOING, slot)) * per_shard
        tap_rows = packed_ref[rows:, :].astype(F32)
        for k in range(per_shard):
            tokens = packed_ref[k * LANES : (k + 1) * LANES, :].astype(F32)
            signal[first + k] = tokens.T.astype(BF16)
            taps[first + k] = tap_rows[k * part : (k + 1) * part, :]

    below = lax.broadcasted_iota(jnp.int32, (LANES, LANES), 0)
    lane = lax.broadcasted_iota(jnp.int32, (LANES, LANES), 1)
    for g in range(part):
        here = slice(g * group_width, (g + 1) * group_width)
        before = jnp.zeros((LANES, LANES), F32)
        by_lag = []
        for e in range(blocks):
            rolled = pltpu.roll(
                jnp.broadcast_to(taps[e, g : g + 1, :], (LANES, LANES)), 0, 1, stride=1, stride_axis=0
            )
            by_lag.append(jnp.where(lane >= below, rolled, before).astype(BF16))
            before = rolled
        sums = [None] * blocks
        for e in range(0, blocks, 2):
            left = signal[0 : blocks - e, here, :].reshape((blocks - e) * group_width, LANES)
            both = jnp.dot(
                left, jnp.concatenate(by_lag[e : e + 2], axis=1), preferred_element_type=F32
            )
            for q in range(blocks - e):
                piece = both[q * group_width : (q + 1) * group_width, :]
                for k in range(2):
                    at = q + e + k
                    if at < blocks:
                        addend = piece[:, k * LANES : (k + 1) * LANES]
                        sums[at] = addend if sums[at] is None else sums[at] + addend
        for q in range(blocks):
            total[q, here, :] = sums[q]

    for slot, out_ref in enumerate(out_refs):
        first = (seq_place() ^ away(RETURNING, slot)) * per_shard
        for k in range(per_shard):
            out_ref[k * LANES : (k + 1) * LANES, :] = total[first + k].T.astype(BF16)


def convolve(packed, n_seq, rows, part):
    blocks = n_seq * rows // LANES
    vmem = pl.BlockSpec(memory_space=pltpu.VMEM)
    return pl.pallas_call(
        functools.partial(conv_kernel, n_seq, rows, part),
        out_shape=[jax.ShapeDtypeStruct((rows, LANES), BF16)] * n_seq,
        in_specs=[vmem] * n_seq,
        out_specs=[vmem] * n_seq,
        scratch_shapes=[
            pltpu.VMEM((blocks, LANES, LANES), BF16),
            pltpu.VMEM((blocks, part, LANES), F32),
            pltpu.VMEM((blocks, LANES, LANES), F32),
        ],
        compiler_params=params(),
        name="convolve",
    )(*packed)


def gate_kernel(n_seq, query_ref, mixed_ref, skip_ref, *refs):
    conv_refs, out_ref = refs[:n_seq], refs[n_seq]
    for slot, conv_ref in enumerate(conv_refs):
        lanes = lanes_at(seq_place() ^ away(RETURNING, slot))
        direct = skip_ref[:, lanes] * mixed_ref[:, lanes].astype(F32)
        out_ref[:, lanes] = (
            query_ref[:, lanes].astype(F32) * (conv_ref[...].astype(F32) + direct)
        ).astype(BF16)


def gate(query_in, mixed_in, skip_gain, parts):
    vmem = pl.BlockSpec(memory_space=pltpu.VMEM)
    return pl.pallas_call(
        functools.partial(gate_kernel, len(parts)),
        out_shape=jax.ShapeDtypeStruct(query_in.shape, BF16),
        in_specs=[vmem] * (3 + len(parts)),
        out_specs=vmem,
        compiler_params=params(),
        name="gate",
    )(query_in, mixed_in, skip_gain, *parts)


def load_block(distance, weight_hbm, weight, arrived):
    block = rows_at(2 * (chip_place() ^ distance) + core_place(), weight.shape[1])
    load = pltpu.make_async_copy(weight_hbm.at[:, block], weight, arrived)
    load.start()
    return block, load


def half_kernel(own_ref, weight, out_ref):
    out_ref[...] = jnp.dot(own_ref[...], weight[0], preferred_element_type=F32)


def add_half_kernel(half_ref, other_ref, other_weight, out_ref):
    block = rows_at(2 * (chip_place() ^ 2) + core_place(), out_ref.shape[1])
    late = jnp.dot(other_ref[...], other_weight[:, block], preferred_element_type=F32)
    out_ref[...] = (half_ref[...] + late).astype(BF16)


def both_halves(distance, own_ref, other_ref, own_weight, other_weight):
    weight = own_weight.at[DISTANCES.index(distance)]
    block = rows_at(2 * (chip_place() ^ distance) + core_place(), weight.shape[1])
    late = jnp.dot(other_ref[...], other_weight[:, block], preferred_element_type=F32)
    return late + jnp.dot(own_ref[...], weight[...], preferred_element_type=F32)


def two_piece_kernel(distance, own_ref, other_ref, own_weight, other_weight, first_ref, second_ref):
    block = both_halves(distance, own_ref, other_ref, own_weight, other_weight)
    rows = first_ref.shape[0]
    first_ref[...] = block[0:rows, :].astype(BF16)
    second_ref[...] = block[rows:, :].astype(BF16)


def after_kernel(from_ref, *refs):
    refs[-1][...] = from_ref[...]


def block_kernel(distance, own_ref, other_ref, own_weight, other_weight, *refs):
    refs[-1][...] = both_halves(distance, own_ref, other_ref, own_weight, other_weight).astype(BF16)


def is_end():
    return (chip_place() == 0) | (chip_place() == 3)


def base_kernel(own_ref, other_ref, own_weight, other_weight, first_ref, out_ref):
    base = both_halves(0, own_ref, other_ref, own_weight, other_weight)

    @pl.when(is_end())
    def _():
        out_ref[...] = base + first_ref[...].astype(F32)

    @pl.when(jnp.logical_not(is_end()))
    def _():
        out_ref[...] = base


def run_kernel(kernel, name, out_shape, scratch, *arrays, hbm=()):
    specs, given = [], []
    for i, array in enumerate(arrays):
        space = pl.ANY if i in hbm else pltpu.VMEM
        specs.append(pl.BlockSpec(memory_space=space))
        given += in_hbm(array) if i in hbm else [array]
    vmem = pl.BlockSpec(memory_space=pltpu.VMEM)
    return pl.pallas_call(
        kernel,
        out_shape=out_shape,
        in_specs=specs,
        out_specs=[vmem] * len(out_shape) if isinstance(out_shape, list) else vmem,
        scratch_shapes=scratch,
        compiler_params=params(),
        name=name,
    )(*given)


def forward_kernel(own_ref, arrived_ref, out_ref):
    @pl.when(is_end())
    def _():
        out_ref[...] = own_ref[...]

    @pl.when(jnp.logical_not(is_end()))
    def _():
        out_ref[...] = (own_ref[...].astype(F32) + arrived_ref[...].astype(F32)).astype(BF16)


def nearly_kernel(base_ref, beside_ref, mirror_ref, out_ref):
    rows = beside_ref.shape[0]
    sums = base_ref[...] + mirror_ref[...].astype(F32)
    out_ref[0:rows, :] = sums[0:rows, :] + beside_ref[...].astype(F32)
    out_ref[rows:, :] = sums[rows:, :]


def final_kernel(base_ref, late_ref, out_hbm, out_ref, arrived):
    rows = base_ref.shape[0] - late_ref.shape[0]
    out_ref[0:rows, :] = base_ref[0:rows, :].astype(BF16)
    first = pltpu.make_async_copy(out_ref.at[0:rows, :], out_hbm.at[0:rows, :], arrived.at[0])
    first.start()
    out_ref[rows:, :] = (base_ref[rows:, :] + late_ref[...].astype(F32)).astype(BF16)
    second = pltpu.make_async_copy(out_ref.at[rows:, :], out_hbm.at[rows:, :], arrived.at[1])
    second.start()
    first.wait()
    second.wait()


def finish(base, late):
    vmem = pl.BlockSpec(memory_space=pltpu.VMEM)
    return pl.pallas_call(
        final_kernel,
        out_shape=jax.ShapeDtypeStruct(base.shape, BF16),
        in_specs=[vmem] * 2,
        out_specs=pl.BlockSpec(memory_space=pl.ANY),
        scratch_shapes=[pltpu.VMEM(base.shape, BF16), pltpu.SemaphoreType.DMA((2,))],
        compiler_params=params(),
        name="final",
    )(base, late)


def fast_body(n_seq, n_chan, query_in, key_in, value_in, filter_taps, skip_gain, out_weight):
    rows, width = query_in.shape
    groups = filter_taps.shape[0]
    part = groups // n_seq
    columns = out_weight.shape[1] // n_chan
    def over_seq(slots, orders):
        *going, staying = slots
        moved = []
        for k, value in enumerate(going):
            pairs = [
                (i * n_chan + j, (i ^ orders[j % 2][k]) * n_chan + j)
                for i in range(n_seq)
                for j in range(n_chan)
            ]
            moved.append(lax.ppermute(value, ("seq", "chan"), pairs))
        return moved + [staying]

    def over_chips(value, moves):
        return lax.ppermute(
            value, "chan", [(2 * a + c, 2 * b + c) for a, b in moves for c in range(2)]
        )

    def other_core(value):
        return lax.ppermute(value, "chan", [(i, i ^ 1) for i in range(n_chan)])

    other_weight = other_core(out_weight)
    mixed_in, *packed = products(key_in, value_in, filter_taps, n_seq)
    arrived = over_seq(packed, GOING)
    query, skip, weight = fetch(packed[-1], query_in, skip_gain, out_weight, columns)
    convolved = convolve(arrived, n_seq, rows, part)
    returned = over_seq(convolved, RETURNING)
    gated = gate(query, mixed_in, skip, returned)
    gated_other = other_core(gated)

    block = jax.ShapeDtypeStruct((rows, columns), BF16)
    block_f32 = jax.ShapeDtypeStruct((rows, columns), F32)
    halves = (gated, gated_other, weight, other_weight)

    half = run_kernel(half_kernel, "half", block_f32, [], gated, weight)
    by_two = run_kernel(add_half_kernel, "by_two", block, [], half, gated_other, other_weight)
    first = over_chips(by_two, [(0, 1), (3, 2), (1, 3), (2, 0)])
    beside = [(0, 1), (1, 0), (2, 3), (3, 2)]
    early = rows * EARLY_PARTS // 8 // 16 * 16
    pieces = [jax.ShapeDtypeStruct((n, columns), BF16) for n in (early, rows - early)]
    kernel = functools.partial(two_piece_kernel, 1)
    by_one, by_one_rest = run_kernel(kernel, "by_one", pieces, [], *halves)
    pair = over_chips(by_one, beside)
    by_three = run_kernel(functools.partial(block_kernel, 3), "by_three", block, [], *halves)
    summed = run_kernel(forward_kernel, "forward", block, [], by_three, first)
    mirror = over_chips(summed, [(0, 3), (3, 0), (1, 2), (2, 1)])
    by_one_rest = run_kernel(after_kernel, "after", pieces[1], [], by_one_rest, summed, pair)
    late = over_chips(by_one_rest, beside)
    base = run_kernel(base_kernel, "base", block_f32, [], *halves, first)
    nearly = run_kernel(nearly_kernel, "nearly", block_f32, [], base, pair, mirror)
    return finish(nearly, late)


def window_matrix(window, tile_size):
    reversed_window = window[:, ::-1]
    extended = jnp.concatenate(
        [reversed_window, jnp.zeros((window.shape[0], 1), window.dtype)], axis=1
    )
    repeated = jnp.tile(extended, (1, tile_size))[:, : tile_size * (2 * tile_size - 1)]
    return repeated.reshape(window.shape[0], tile_size, 2 * tile_size - 1)[:, :, tile_size - 1 :]


def accumulate(running, segment, tap_table, own_start):
    row_count, chan_width = running.shape
    group_count = tap_table.shape[0]
    tap_span = tap_table.shape[1] // 2
    group_width = chan_width // group_count
    block_rows = min(segment.shape[0], row_count)
    tile_size = math.gcd(math.gcd(block_rows, row_count), 128)
    out_tiles = row_count // tile_size
    in_tiles = block_rows // tile_size

    def one_block(step_index, current):
        block_start = step_index * block_rows
        in_blocks = lax.dynamic_slice_in_dim(segment, step_index * block_rows, block_rows, 0)
        in_blocks = in_blocks.reshape(in_tiles, tile_size, group_count, group_width)

        def add_block(previous):
            out_blocks = previous.reshape(out_tiles, tile_size, group_count, group_width)
            offset = own_start - block_start
            for lag_step in range(1 - in_tiles, out_tiles):
                tap_first = offset + lag_step * tile_size - (tile_size - 1) + tap_span
                window = lax.dynamic_slice_in_dim(tap_table, tap_first, 2 * tile_size - 1, 1)
                matrix = window_matrix(window, tile_size)
                first_out = max(0, lag_step)
                last_out = min(out_tiles, in_tiles + lag_step)
                addend = jnp.einsum(
                    "gij,qjgc->qigc",
                    matrix,
                    in_blocks[first_out - lag_step : last_out - lag_step],
                    preferred_element_type=jnp.float32,
                )
                out_blocks = out_blocks.at[first_out:last_out].add(addend)
            return out_blocks.reshape(previous.shape)

        def keep_same(previous):
            return previous

        needed = (block_start < own_start + row_count) & (block_start >= 0)
        return lax.cond(needed, add_block, keep_same, current)

    return lax.fori_loop(0, segment.shape[0] // block_rows, one_block, running)


def general_body(query_in, key_in, value_in, filter_taps, skip_gain, out_weight):
    row_count, chan_width = query_in.shape
    mixed_in = (key_in.astype(jnp.float32) * value_in.astype(jnp.float32)).astype(jnp.bfloat16)
    all_taps = lax.all_gather(filter_taps, "seq", axis=1, tiled=True)
    tap_table = jnp.concatenate([jnp.zeros_like(all_taps), all_taps], axis=1)
    seq_index = lax.axis_index("seq")
    own_start = seq_index * row_count
    zero_sum = jnp.zeros((row_count, chan_width), jnp.float32)
    convolved = accumulate(
        zero_sum, lax.all_gather(mixed_in, "seq", axis=0, tiled=True), tap_table, own_start
    )
    gated = (
        query_in.astype(jnp.float32)
        * (convolved + skip_gain[None, :] * mixed_in.astype(jnp.float32))
    ).astype(jnp.bfloat16)
    columns = lax.all_to_all(out_weight, "chan", split_axis=1, concat_axis=0, tiled=True)
    result = jnp.dot(
        lax.all_gather(gated, "chan", axis=1, tiled=True),
        columns,
        preferred_element_type=jnp.float32,
    )
    return result.astype(jnp.bfloat16)


def solution(mesh):
    n_seq, n_chan = mesh.shape["seq"], mesh.shape["chan"]

    def body(query_in, key_in, value_in, filter_taps, skip_gain, out_weight):
        rows, width = query_in.shape
        groups, span = filter_taps.shape
        part = groups // n_seq
        fits = (
            n_chan == 8
            and n_seq == len(GOING[0])
            and width == n_seq * LANES
            and part * n_seq == groups
            and part % 8 == 0
            and (part * (rows // LANES)) % 16 == 0
            and rows % (2 * LANES) == 0
            and (n_seq * rows) % (4 * LANES) == 0
            and span == rows
            and out_weight.shape[1] % (n_chan * LANES) == 0
        )
        run = functools.partial(fast_body, n_seq, n_chan) if fits else general_body
        return run(query_in, key_in, value_in, filter_taps, skip_gain, out_weight)

    placed = (
        P("seq", "chan"),
        P("seq", "chan"),
        P("seq", "chan"),
        P("chan", "seq"),
        P("chan"),
        P("chan", None),
    )
    return jax.shard_map(
        body, mesh=mesh, in_specs=placed, out_specs=P("seq", "chan"), check_vma=False
    )
```

```python
import functools
import math

import jax
import jax.numpy as jnp
from jax import lax
from jax.experimental import pallas as pl
from jax.experimental.pallas import tpu as pltpu
from jax.sharding import PartitionSpec as P

LANES = 128
DISTANCES = (2, 1, 3, 0)
EARLY_PARTS = 4
LEAD_PARTS = 4
GOING = ((3, 1, 2, 0), (2, 3, 1, 0))
RETURNING = GOING
BF16 = jnp.bfloat16
F32 = jnp.float32
VMEM_LIMIT = 16 * 1024 * 1024


def params():
    return pltpu.CompilerParams(vmem_limit_bytes=VMEM_LIMIT)


def in_hbm(*arrays):
    return [pltpu.with_memory_space_constraint(a, pltpu.HBM) for a in arrays]


def away(orders, k):
    return jnp.where(core_place() == 0, orders[0][k], orders[1][k])


def seq_place():
    return lax.axis_index("seq")


def chip_place():
    return lax.axis_index("chan") // 2


def core_place():
    return lax.axis_index("chan") % 2


def lanes_at(block):
    return pl.ds(pl.multiple_of(block * LANES, LANES), LANES)


def rows_at(block, size):
    return pl.ds(pl.multiple_of(block * size, size), size)


def product_kernel(n_seq, key_hbm, value_hbm, taps_hbm, *refs):
    mixed_ref, *packed_refs = refs[: n_seq + 1]
    key_ref, value_ref, taps_ref, taps_f32, arrived = refs[n_seq + 1 :]
    rows = key_ref.shape[0]
    groups, span = taps_ref.shape
    part = groups // n_seq
    loads = [
        pltpu.make_async_copy(source, target, arrived.at[i])
        for i, (source, target) in enumerate(
            [
                (taps_hbm, taps_ref),
                (key_hbm, key_ref),
                (value_hbm, value_ref),
            ]
        )
    ]
    for load in loads:
        load.start()
    loads[0].wait()
    taps_f32[...] = taps_ref[...].astype(F32)
    for slot, packed_ref in enumerate(packed_refs):
        own = taps_f32[rows_at(seq_place() ^ away(GOING, slot), part), :]
        pieces = [own[:, k * LANES : (k + 1) * LANES] for k in range(span // LANES)]
        packed_ref[rows:, :] = jnp.concatenate(pieces, axis=0).astype(BF16)
    loads[1].wait()
    loads[2].wait()
    mixed_ref[...] = (key_ref[...].astype(F32) * value_ref[...].astype(F32)).astype(BF16)
    for slot, packed_ref in enumerate(packed_refs):
        packed_ref[0:rows, :] = mixed_ref[:, lanes_at(seq_place() ^ away(GOING, slot))]


def products(key_in, value_in, taps, n_seq):
    rows, width = key_in.shape
    groups, span = taps.shape
    tap_rows = (groups // n_seq) * (span // LANES)
    here = jax.ShapeDtypeStruct((rows, width), BF16)
    packed = jax.ShapeDtypeStruct((rows + tap_rows, LANES), BF16)
    return pl.pallas_call(
        functools.partial(product_kernel, n_seq),
        out_shape=[here] + [packed] * n_seq,
        in_specs=[pl.BlockSpec(memory_space=pl.ANY)] * 3,
        out_specs=[pl.BlockSpec(memory_space=pltpu.VMEM)] * (n_seq + 1),
        scratch_shapes=[
            pltpu.VMEM((rows, width), BF16),
            pltpu.VMEM((rows, width), BF16),
            pltpu.VMEM((groups, span), BF16),
            pltpu.VMEM((groups, span), F32),
            pltpu.SemaphoreType.DMA((3,)),
        ],
        compiler_params=params(),
        name="products",
    )(*in_hbm(key_in, value_in, taps))


def fetch_kernel(after_hbm, query_hbm, skip_hbm, weight_hbm, query_ref, skip_ref, weight_ref, arrived):
    loads = [
        pltpu.make_async_copy(query_hbm, query_ref, arrived.at[0]),
        pltpu.make_async_copy(skip_hbm, skip_ref, arrived.at[1]),
    ]
    for load in loads:
        load.start()
    for i, distance in enumerate(DISTANCES):
        loads.append(load_block(distance, weight_hbm, weight_ref.at[i], arrived.at[2 + i])[1])
    for load in loads:
        load.wait()


def fetch(after, query_in, skip_gain, out_weight, columns):
    vmem = pl.BlockSpec(memory_space=pltpu.VMEM)
    width = query_in.shape[1]
    return pl.pallas_call(
        fetch_kernel,
        out_shape=[
            jax.ShapeDtypeStruct(query_in.shape, BF16),
            jax.ShapeDtypeStruct((1, width), F32),
            jax.ShapeDtypeStruct((len(DISTANCES), width, columns), BF16),
        ],
        in_specs=[pl.BlockSpec(memory_space=pl.ANY)] * 4,
        out_specs=[vmem] * 3,
        scratch_shapes=[pltpu.SemaphoreType.DMA((2 + len(DISTANCES),))],
        compiler_params=params(),
        name="fetch",
    )(after, *in_hbm(query_in, skip_gain.reshape(1, -1), out_weight))


def conv_kernel(n_seq, rows, part, *refs):
    packed_refs = refs[:n_seq]
    out_refs = refs[n_seq : 2 * n_seq]
    signal, taps, total = refs[2 * n_seq :]
    per_shard = rows // LANES
    blocks = n_seq * per_shard
    group_width = LANES // part

    for slot, packed_ref in enumerate(packed_refs):
        first = (seq_place() ^ away(GOING, slot)) * per_shard
        tap_rows = packed_ref[rows:, :].astype(F32)
        for k in range(per_shard):
            tokens = packed_ref[k * LANES : (k + 1) * LANES, :].astype(F32)
            signal[first + k] = tokens.T.astype(BF16)
            taps[first + k] = tap_rows[k * part : (k + 1) * part, :]

    below = lax.broadcasted_iota(jnp.int32, (LANES, LANES), 0)
    lane = lax.broadcasted_iota(jnp.int32, (LANES, LANES), 1)
    for g in range(part):
        here = slice(g * group_width, (g + 1) * group_width)
        before = jnp.zeros((LANES, LANES), F32)
        by_lag = []
        for e in range(blocks):
            rolled = pltpu.roll(
                jnp.broadcast_to(taps[e, g : g + 1, :], (LANES, LANES)), 0, 1, stride=1, stride_axis=0
            )
            by_lag.append(jnp.where(lane >= below, rolled, before).astype(BF16))
            before = rolled
        sums = [None] * blocks
        for e in range(0, blocks, 2):
            left = signal[0 : blocks - e, here, :].reshape((blocks - e) * group_width, LANES)
            both = jnp.dot(
                left, jnp.concatenate(by_lag[e : e + 2], axis=1), preferred_element_type=F32
            )
            for q in range(blocks - e):
                piece = both[q * group_width : (q + 1) * group_width, :]
                for k in range(2):
                    at = q + e + k
                    if at < blocks:
                        addend = piece[:, k * LANES : (k + 1) * LANES]
                        sums[at] = addend if sums[at] is None else sums[at] + addend
        for q in range(blocks):
            total[q, here, :] = sums[q]

    for slot, out_ref in enumerate(out_refs):
        first = (seq_place() ^ away(RETURNING, slot)) * per_shard
        for k in range(per_shard):
            out_ref[k * LANES : (k + 1) * LANES, :] = total[first + k].T.astype(BF16)


def convolve(packed, n_seq, rows, part):
    blocks = n_seq * rows // LANES
    vmem = pl.BlockSpec(memory_space=pltpu.VMEM)
    return pl.pallas_call(
        functools.partial(conv_kernel, n_seq, rows, part),
        out_shape=[jax.ShapeDtypeStruct((rows, LANES), BF16)] * n_seq,
        in_specs=[vmem] * n_seq,
        out_specs=[vmem] * n_seq,
        scratch_shapes=[
            pltpu.VMEM((blocks, LANES, LANES), BF16),
            pltpu.VMEM((blocks, part, LANES), F32),
            pltpu.VMEM((blocks, LANES, LANES), F32),
        ],
        compiler_params=params(),
        name="convolve",
    )(*packed)


def gate_kernel(n_seq, query_ref, mixed_ref, skip_ref, *refs):
    conv_refs, out_ref = refs[:n_seq], refs[n_seq]
    for slot, conv_ref in enumerate(conv_refs):
        lanes = lanes_at(seq_place() ^ away(RETURNING, slot))
        direct = skip_ref[:, lanes] * mixed_ref[:, lanes].astype(F32)
        out_ref[:, lanes] = (
            query_ref[:, lanes].astype(F32) * (conv_ref[...].astype(F32) + direct)
        ).astype(BF16)


def gate(query_in, mixed_in, skip_gain, parts):
    vmem = pl.BlockSpec(memory_space=pltpu.VMEM)
    return pl.pallas_call(
        functools.partial(gate_kernel, len(parts)),
        out_shape=jax.ShapeDtypeStruct(query_in.shape, BF16),
        in_specs=[vmem] * (3 + len(parts)),
        out_specs=vmem,
        compiler_params=params(),
        name="gate",
    )(query_in, mixed_in, skip_gain, *parts)


def load_block(distance, weight_hbm, weight, arrived):
    block = rows_at(2 * (chip_place() ^ distance) + core_place(), weight.shape[1])
    load = pltpu.make_async_copy(weight_hbm.at[:, block], weight, arrived)
    load.start()
    return block, load


def half_kernel(own_ref, weight, out_ref):
    out_ref[...] = jnp.dot(own_ref[...], weight[0], preferred_element_type=F32)


def add_half_kernel(half_ref, other_ref, other_weight, *out_refs):
    block = rows_at(2 * (chip_place() ^ 2) + core_place(), half_ref.shape[1])
    late = jnp.dot(other_ref[...], other_weight[:, block], preferred_element_type=F32)
    sums = (half_ref[...] + late).astype(BF16)
    start = 0
    for out_ref in out_refs:
        out_ref[...] = sums[start : start + out_ref.shape[0], :]
        start += out_ref.shape[0]


def both_halves(distance, own_ref, other_ref, own_weight, other_weight):
    weight = own_weight.at[DISTANCES.index(distance)]
    block = rows_at(2 * (chip_place() ^ distance) + core_place(), weight.shape[1])
    late = jnp.dot(other_ref[...], other_weight[:, block], preferred_element_type=F32)
    return late + jnp.dot(own_ref[...], weight[...], preferred_element_type=F32)


def two_piece_kernel(distance, own_ref, other_ref, own_weight, other_weight, first_ref, second_ref):
    block = both_halves(distance, own_ref, other_ref, own_weight, other_weight)
    rows = first_ref.shape[0]
    first_ref[...] = block[0:rows, :].astype(BF16)
    second_ref[...] = block[rows:, :].astype(BF16)


def after_kernel(from_ref, *refs):
    refs[-1][...] = from_ref[...]


def block_kernel(distance, own_ref, other_ref, own_weight, other_weight, *refs):
    refs[-1][...] = both_halves(distance, own_ref, other_ref, own_weight, other_weight).astype(BF16)


def is_end():
    return (chip_place() == 0) | (chip_place() == 3)


def base_kernel(own_ref, other_ref, own_weight, other_weight, *refs):
    first_refs, out_ref = refs[:-1], refs[-1]
    base = both_halves(0, own_ref, other_ref, own_weight, other_weight)

    @pl.when(is_end())
    def _():
        first = jnp.concatenate([first_ref[...].astype(F32) for first_ref in first_refs], axis=0)
        out_ref[...] = base + first

    @pl.when(jnp.logical_not(is_end()))
    def _():
        out_ref[...] = base


def run_kernel(kernel, name, out_shape, scratch, *arrays, hbm=()):
    specs, given = [], []
    for i, array in enumerate(arrays):
        space = pl.ANY if i in hbm else pltpu.VMEM
        specs.append(pl.BlockSpec(memory_space=space))
        given += in_hbm(array) if i in hbm else [array]
    vmem = pl.BlockSpec(memory_space=pltpu.VMEM)
    return pl.pallas_call(
        kernel,
        out_shape=out_shape,
        in_specs=specs,
        out_specs=[vmem] * len(out_shape) if isinstance(out_shape, list) else vmem,
        scratch_shapes=scratch,
        compiler_params=params(),
        name=name,
    )(*given)


def forward_kernel(start, own_ref, arrived_ref, out_ref):
    own = own_ref[start : start + out_ref.shape[0], :]

    @pl.when(is_end())
    def _():
        out_ref[...] = own

    @pl.when(jnp.logical_not(is_end()))
    def _():
        out_ref[...] = (own.astype(F32) + arrived_ref[...].astype(F32)).astype(BF16)


def nearly_kernel(base_ref, beside_ref, *refs):
    mirror_refs, out_ref = refs[:-1], refs[-1]
    start = 0
    for mirror_ref in mirror_refs:
        here = slice(start, start + mirror_ref.shape[0])
        out_ref[here, :] = base_ref[here, :] + mirror_ref[...].astype(F32)
        start += mirror_ref.shape[0]
    out_ref[0 : beside_ref.shape[0], :] += beside_ref[...].astype(F32)


def final_kernel(base_ref, late_ref, out_hbm, out_ref, arrived):
    rows = base_ref.shape[0] - late_ref.shape[0]
    out_ref[0:rows, :] = base_ref[0:rows, :].astype(BF16)
    first = pltpu.make_async_copy(out_ref.at[0:rows, :], out_hbm.at[0:rows, :], arrived.at[0])
    first.start()
    out_ref[rows:, :] = (base_ref[rows:, :] + late_ref[...].astype(F32)).astype(BF16)
    second = pltpu.make_async_copy(out_ref.at[rows:, :], out_hbm.at[rows:, :], arrived.at[1])
    second.start()
    first.wait()
    second.wait()


def finish(base, late):
    vmem = pl.BlockSpec(memory_space=pltpu.VMEM)
    return pl.pallas_call(
        final_kernel,
        out_shape=jax.ShapeDtypeStruct(base.shape, BF16),
        in_specs=[vmem] * 2,
        out_specs=pl.BlockSpec(memory_space=pl.ANY),
        scratch_shapes=[pltpu.VMEM(base.shape, BF16), pltpu.SemaphoreType.DMA((2,))],
        compiler_params=params(),
        name="final",
    )(base, late)


def fast_body(n_seq, n_chan, query_in, key_in, value_in, filter_taps, skip_gain, out_weight):
    rows, width = query_in.shape
    groups = filter_taps.shape[0]
    part = groups // n_seq
    columns = out_weight.shape[1] // n_chan
    def over_seq(slots, orders):
        *going, staying = slots
        moved = []
        for k, value in enumerate(going):
            pairs = [
                (i * n_chan + j, (i ^ orders[j % 2][k]) * n_chan + j)
                for i in range(n_seq)
                for j in range(n_chan)
            ]
            moved.append(lax.ppermute(value, ("seq", "chan"), pairs))
        return moved + [staying]

    def over_chips(value, moves):
        return lax.ppermute(
            value, "chan", [(2 * a + c, 2 * b + c) for a, b in moves for c in range(2)]
        )

    def other_core(value):
        return lax.ppermute(value, "chan", [(i, i ^ 1) for i in range(n_chan)])

    other_weight = other_core(out_weight)
    mixed_in, *packed = products(key_in, value_in, filter_taps, n_seq)
    arrived = over_seq(packed, GOING)
    query, skip, weight = fetch(packed[-1], query_in, skip_gain, out_weight, columns)
    convolved = convolve(arrived, n_seq, rows, part)
    returned = over_seq(convolved, RETURNING)
    gated = gate(query, mixed_in, skip, returned)
    gated_other = other_core(gated)

    block = jax.ShapeDtypeStruct((rows, columns), BF16)
    block_f32 = jax.ShapeDtypeStruct((rows, columns), F32)
    halves = (gated, gated_other, weight, other_weight)

    half = run_kernel(half_kernel, "half", block_f32, [], gated, weight)
    lead = rows * LEAD_PARTS // 8 // 16 * 16
    parts = [jax.ShapeDtypeStruct((n, columns), BF16) for n in (lead, rows - lead)]
    by_two = run_kernel(add_half_kernel, "by_two", parts, [], half, gated_other, other_weight)
    first = [over_chips(part, [(0, 1), (3, 2), (1, 3), (2, 0)]) for part in by_two]
    beside = [(0, 1), (1, 0), (2, 3), (3, 2)]
    early = rows * EARLY_PARTS // 8 // 16 * 16
    pieces = [jax.ShapeDtypeStruct((n, columns), BF16) for n in (early, rows - early)]
    kernel = functools.partial(two_piece_kernel, 1)
    by_one, by_one_rest = run_kernel(kernel, "by_one", pieces, [], *halves)
    pair = over_chips(by_one, beside)
    by_three = run_kernel(functools.partial(block_kernel, 3), "by_three", block, [], *halves)
    mirror = []
    for part, start, arrived in zip(parts, (0, lead), first):
        kernel = functools.partial(forward_kernel, start)
        summed = run_kernel(kernel, "forward", part, [], by_three, arrived)
        mirror.append(over_chips(summed, [(0, 3), (3, 0), (1, 2), (2, 1)]))
    by_one_rest = run_kernel(after_kernel, "after", pieces[1], [], by_one_rest, summed, pair)
    late = over_chips(by_one_rest, beside)
    base = run_kernel(base_kernel, "base", block_f32, [], *halves, *first)
    nearly = run_kernel(nearly_kernel, "nearly", block_f32, [], base, pair, *mirror)
    return finish(nearly, late)


def window_matrix(window, tile_size):
    reversed_window = window[:, ::-1]
    extended = jnp.concatenate(
        [reversed_window, jnp.zeros((window.shape[0], 1), window.dtype)], axis=1
    )
    repeated = jnp.tile(extended, (1, tile_size))[:, : tile_size * (2 * tile_size - 1)]
    return repeated.reshape(window.shape[0], tile_size, 2 * tile_size - 1)[:, :, tile_size - 1 :]


def accumulate(running, segment, tap_table, own_start):
    row_count, chan_width = running.shape
    group_count = tap_table.shape[0]
    tap_span = tap_table.shape[1] // 2
    group_width = chan_width // group_count
    block_rows = min(segment.shape[0], row_count)
    tile_size = math.gcd(math.gcd(block_rows, row_count), 128)
    out_tiles = row_count // tile_size
    in_tiles = block_rows // tile_size

    def one_block(step_index, current):
        block_start = step_index * block_rows
        in_blocks = lax.dynamic_slice_in_dim(segment, step_index * block_rows, block_rows, 0)
        in_blocks = in_blocks.reshape(in_tiles, tile_size, group_count, group_width)

        def add_block(previous):
            out_blocks = previous.reshape(out_tiles, tile_size, group_count, group_width)
            offset = own_start - block_start
            for lag_step in range(1 - in_tiles, out_tiles):
                tap_first = offset + lag_step * tile_size - (tile_size - 1) + tap_span
                window = lax.dynamic_slice_in_dim(tap_table, tap_first, 2 * tile_size - 1, 1)
                matrix = window_matrix(window, tile_size)
                first_out = max(0, lag_step)
                last_out = min(out_tiles, in_tiles + lag_step)
                addend = jnp.einsum(
                    "gij,qjgc->qigc",
                    matrix,
                    in_blocks[first_out - lag_step : last_out - lag_step],
                    preferred_element_type=jnp.float32,
                )
                out_blocks = out_blocks.at[first_out:last_out].add(addend)
            return out_blocks.reshape(previous.shape)

        def keep_same(previous):
            return previous

        needed = (block_start < own_start + row_count) & (block_start >= 0)
        return lax.cond(needed, add_block, keep_same, current)

    return lax.fori_loop(0, segment.shape[0] // block_rows, one_block, running)


def general_body(query_in, key_in, value_in, filter_taps, skip_gain, out_weight):
    row_count, chan_width = query_in.shape
    mixed_in = (key_in.astype(jnp.float32) * value_in.astype(jnp.float32)).astype(jnp.bfloat16)
    all_taps = lax.all_gather(filter_taps, "seq", axis=1, tiled=True)
    tap_table = jnp.concatenate([jnp.zeros_like(all_taps), all_taps], axis=1)
    seq_index = lax.axis_index("seq")
    own_start = seq_index * row_count
    zero_sum = jnp.zeros((row_count, chan_width), jnp.float32)
    convolved = accumulate(
        zero_sum, lax.all_gather(mixed_in, "seq", axis=0, tiled=True), tap_table, own_start
    )
    gated = (
        query_in.astype(jnp.float32)
        * (convolved + skip_gain[None, :] * mixed_in.astype(jnp.float32))
    ).astype(jnp.bfloat16)
    columns = lax.all_to_all(out_weight, "chan", split_axis=1, concat_axis=0, tiled=True)
    result = jnp.dot(
        lax.all_gather(gated, "chan", axis=1, tiled=True),
        columns,
        preferred_element_type=jnp.float32,
    )
    return result.astype(jnp.bfloat16)


def solution(mesh):
    n_seq, n_chan = mesh.shape["seq"], mesh.shape["chan"]

    def body(query_in, key_in, value_in, filter_taps, skip_gain, out_weight):
        rows, width = query_in.shape
        groups, span = filter_taps.shape
        part = groups // n_seq
        fits = (
            n_chan == 8
            and n_seq == len(GOING[0])
            and width == n_seq * LANES
            and part * n_seq == groups
            and part % 8 == 0
            and (part * (rows // LANES)) % 16 == 0
            and rows % (2 * LANES) == 0
            and (n_seq * rows) % (4 * LANES) == 0
            and span == rows
            and out_weight.shape[1] % (n_chan * LANES) == 0
        )
        run = functools.partial(fast_body, n_seq, n_chan) if fits else general_body
        return run(query_in, key_in, value_in, filter_taps, skip_gain, out_weight)

    placed = (
        P("seq", "chan"),
        P("seq", "chan"),
        P("seq", "chan"),
        P("chan", "seq"),
        P("chan"),
        P("chan", None),
    )
    return jax.shard_map(
        body, mesh=mesh, in_specs=placed, out_specs=P("seq", "chan"), check_vma=False
    )
```

```python
import functools
import math

import jax
import jax.numpy as jnp
from jax import lax
from jax.experimental import pallas as pl
from jax.experimental.pallas import tpu as pltpu
from jax.sharding import PartitionSpec as P

LANES = 128
DISTANCES = (2, 1, 3, 0)
EARLY_PARTS = 6
GOING = ((3, 1, 2, 0), (2, 3, 1, 0))
RETURNING = GOING
BF16 = jnp.bfloat16
F32 = jnp.float32
VMEM_LIMIT = 16 * 1024 * 1024


def params():
    return pltpu.CompilerParams(vmem_limit_bytes=VMEM_LIMIT)


def in_hbm(*arrays):
    return [pltpu.with_memory_space_constraint(a, pltpu.HBM) for a in arrays]


def away(orders, k):
    return jnp.where(core_place() == 0, orders[0][k], orders[1][k])


def seq_place():
    return lax.axis_index("seq")


def chip_place():
    return lax.axis_index("chan") // 2


def core_place():
    return lax.axis_index("chan") % 2


def lanes_at(block):
    return pl.ds(pl.multiple_of(block * LANES, LANES), LANES)


def rows_at(block, size):
    return pl.ds(pl.multiple_of(block * size, size), size)


def product_kernel(n_seq, key_hbm, value_hbm, taps_hbm, *refs):
    mixed_ref, *packed_refs = refs[: n_seq + 1]
    key_ref, value_ref, taps_ref, taps_f32, arrived = refs[n_seq + 1 :]
    rows = key_ref.shape[0]
    groups, span = taps_ref.shape
    part = groups // n_seq
    loads = [
        pltpu.make_async_copy(source, target, arrived.at[i])
        for i, (source, target) in enumerate(
            [
                (taps_hbm, taps_ref),
                (key_hbm, key_ref),
                (value_hbm, value_ref),
            ]
        )
    ]
    for load in loads:
        load.start()
    loads[0].wait()
    taps_f32[...] = taps_ref[...].astype(F32)
    for slot, packed_ref in enumerate(packed_refs):
        own = taps_f32[rows_at(seq_place() ^ away(GOING, slot), part), :]
        pieces = [own[:, k * LANES : (k + 1) * LANES] for k in range(span // LANES)]
        packed_ref[rows:, :] = jnp.concatenate(pieces, axis=0).astype(BF16)
    loads[1].wait()
    loads[2].wait()
    mixed_ref[...] = (key_ref[...].astype(F32) * value_ref[...].astype(F32)).astype(BF16)
    for slot, packed_ref in enumerate(packed_refs):
        packed_ref[0:rows, :] = mixed_ref[:, lanes_at(seq_place() ^ away(GOING, slot))]


def products(key_in, value_in, taps, n_seq):
    rows, width = key_in.shape
    groups, span = taps.shape
    tap_rows = (groups // n_seq) * (span // LANES)
    here = jax.ShapeDtypeStruct((rows, width), BF16)
    packed = jax.ShapeDtypeStruct((rows + tap_rows, LANES), BF16)
    return pl.pallas_call(
        functools.partial(product_kernel, n_seq),
        out_shape=[here] + [packed] * n_seq,
        in_specs=[pl.BlockSpec(memory_space=pl.ANY)] * 3,
        out_specs=[pl.BlockSpec(memory_space=pltpu.VMEM)] * (n_seq + 1),
        scratch_shapes=[
            pltpu.VMEM((rows, width), BF16),
            pltpu.VMEM((rows, width), BF16),
            pltpu.VMEM((groups, span), BF16),
            pltpu.VMEM((groups, span), F32),
            pltpu.SemaphoreType.DMA((3,)),
        ],
        compiler_params=params(),
        name="products",
    )(*in_hbm(key_in, value_in, taps))


def fetch_kernel(after_hbm, query_hbm, skip_hbm, weight_hbm, query_ref, skip_ref, weight_ref, arrived):
    loads = [
        pltpu.make_async_copy(query_hbm, query_ref, arrived.at[0]),
        pltpu.make_async_copy(skip_hbm, skip_ref, arrived.at[1]),
    ]
    for load in loads:
        load.start()
    for i, distance in enumerate(DISTANCES):
        loads.append(load_block(distance, weight_hbm, weight_ref.at[i], arrived.at[2 + i])[1])
    for load in loads:
        load.wait()


def fetch(after, query_in, skip_gain, out_weight, columns):
    vmem = pl.BlockSpec(memory_space=pltpu.VMEM)
    width = query_in.shape[1]
    return pl.pallas_call(
        fetch_kernel,
        out_shape=[
            jax.ShapeDtypeStruct(query_in.shape, BF16),
            jax.ShapeDtypeStruct((1, width), F32),
            jax.ShapeDtypeStruct((len(DISTANCES), width, columns), BF16),
        ],
        in_specs=[pl.BlockSpec(memory_space=pl.ANY)] * 4,
        out_specs=[vmem] * 3,
        scratch_shapes=[pltpu.SemaphoreType.DMA((2 + len(DISTANCES),))],
        compiler_params=params(),
        name="fetch",
    )(after, *in_hbm(query_in, skip_gain.reshape(1, -1), out_weight))


def conv_kernel(n_seq, rows, part, *refs):
    packed_refs = refs[:n_seq]
    out_refs = refs[n_seq : 2 * n_seq]
    signal, taps, total = refs[2 * n_seq :]
    per_shard = rows // LANES
    blocks = n_seq * per_shard
    group_width = LANES // part

    for slot, packed_ref in enumerate(packed_refs):
        first = (seq_place() ^ away(GOING, slot)) * per_shard
        tap_rows = packed_ref[rows:, :].astype(F32)
        for k in range(per_shard):
            tokens = packed_ref[k * LANES : (k + 1) * LANES, :].astype(F32)
            signal[first + k] = tokens.T.astype(BF16)
            taps[first + k] = tap_rows[k * part : (k + 1) * part, :]

    below = lax.broadcasted_iota(jnp.int32, (LANES, LANES), 0)
    lane = lax.broadcasted_iota(jnp.int32, (LANES, LANES), 1)
    for g in range(part):
        here = slice(g * group_width, (g + 1) * group_width)
        before = jnp.zeros((LANES, LANES), F32)
        by_lag = []
        for e in range(blocks):
            rolled = pltpu.roll(
                jnp.broadcast_to(taps[e, g : g + 1, :], (LANES, LANES)), 0, 1, stride=1, stride_axis=0
            )
            by_lag.append(jnp.where(lane >= below, rolled, before).astype(BF16))
            before = rolled
        sums = [None] * blocks
        for e in range(0, blocks, 2):
            left = signal[0 : blocks - e, here, :].reshape((blocks - e) * group_width, LANES)
            both = jnp.dot(
                left, jnp.concatenate(by_lag[e : e + 2], axis=1), preferred_element_type=F32
            )
            for q in range(blocks - e):
                piece = both[q * group_width : (q + 1) * group_width, :]
                for k in range(2):
                    at = q + e + k
                    if at < blocks:
                        addend = piece[:, k * LANES : (k + 1) * LANES]
                        sums[at] = addend if sums[at] is None else sums[at] + addend
        for q in range(blocks):
            total[q, here, :] = sums[q]

    for slot, out_ref in enumerate(out_refs):
        first = (seq_place() ^ away(RETURNING, slot)) * per_shard
        for k in range(per_shard):
            out_ref[k * LANES : (k + 1) * LANES, :] = total[first + k].T.astype(BF16)


def convolve(packed, n_seq, rows, part):
    blocks = n_seq * rows // LANES
    vmem = pl.BlockSpec(memory_space=pltpu.VMEM)
    return pl.pallas_call(
        functools.partial(conv_kernel, n_seq, rows, part),
        out_shape=[jax.ShapeDtypeStruct((rows, LANES), BF16)] * n_seq,
        in_specs=[vmem] * n_seq,
        out_specs=[vmem] * n_seq,
        scratch_shapes=[
            pltpu.VMEM((blocks, LANES, LANES), BF16),
            pltpu.VMEM((blocks, part, LANES), F32),
            pltpu.VMEM((blocks, LANES, LANES), F32),
        ],
        compiler_params=params(),
        name="convolve",
    )(*packed)


def gate_kernel(n_seq, query_ref, mixed_ref, skip_ref, *refs):
    conv_refs, out_ref = refs[:n_seq], refs[n_seq]
    for slot, conv_ref in enumerate(conv_refs):
        lanes = lanes_at(seq_place() ^ away(RETURNING, slot))
        direct = skip_ref[:, lanes] * mixed_ref[:, lanes].astype(F32)
        out_ref[:, lanes] = (
            query_ref[:, lanes].astype(F32) * (conv_ref[...].astype(F32) + direct)
        ).astype(BF16)


def gate(query_in, mixed_in, skip_gain, parts):
    vmem = pl.BlockSpec(memory_space=pltpu.VMEM)
    return pl.pallas_call(
        functools.partial(gate_kernel, len(parts)),
        out_shape=jax.ShapeDtypeStruct(query_in.shape, BF16),
        in_specs=[vmem] * (3 + len(parts)),
        out_specs=vmem,
        compiler_params=params(),
        name="gate",
    )(query_in, mixed_in, skip_gain, *parts)


def load_block(distance, weight_hbm, weight, arrived):
    block = rows_at(2 * (chip_place() ^ distance) + core_place(), weight.shape[1])
    load = pltpu.make_async_copy(weight_hbm.at[:, block], weight, arrived)
    load.start()
    return block, load


def half_kernel(own_ref, weight, out_ref):
    out_ref[...] = jnp.dot(own_ref[...], weight[0], preferred_element_type=F32)


def add_half_kernel(half_ref, other_ref, other_weight, out_ref):
    block = rows_at(2 * (chip_place() ^ 2) + core_place(), out_ref.shape[1])
    late = jnp.dot(other_ref[...], other_weight[:, block], preferred_element_type=F32)
    out_ref[...] = (half_ref[...] + late).astype(BF16)


def both_halves(distance, own_ref, other_ref, own_weight, other_weight):
    weight = own_weight.at[DISTANCES.index(distance)]
    block = rows_at(2 * (chip_place() ^ distance) + core_place(), weight.shape[1])
    late = jnp.dot(other_ref[...], other_weight[:, block], preferred_element_type=F32)
    return late + jnp.dot(own_ref[...], weight[...], preferred_element_type=F32)


def two_piece_kernel(distance, own_ref, other_ref, own_weight, other_weight, _, first_ref, second_ref):
    block = both_halves(distance, own_ref, other_ref, own_weight, other_weight)
    rows = first_ref.shape[0]
    first_ref[...] = block[0:rows, :].astype(BF16)
    second_ref[...] = block[rows:, :].astype(BF16)


def after_kernel(from_ref, *refs):
    refs[-1][...] = from_ref[...]


def block_kernel(distance, own_ref, other_ref, own_weight, other_weight, *refs):
    refs[-1][...] = both_halves(distance, own_ref, other_ref, own_weight, other_weight).astype(BF16)


def is_end():
    return (chip_place() == 0) | (chip_place() == 3)


def base_kernel(own_ref, other_ref, own_weight, other_weight, first_ref, out_ref):
    base = both_halves(0, own_ref, other_ref, own_weight, other_weight)

    @pl.when(is_end())
    def _():
        out_ref[...] = base + first_ref[...].astype(F32)

    @pl.when(jnp.logical_not(is_end()))
    def _():
        out_ref[...] = base


def run_kernel(kernel, name, out_shape, scratch, *arrays, hbm=()):
    specs, given = [], []
    for i, array in enumerate(arrays):
        space = pl.ANY if i in hbm else pltpu.VMEM
        specs.append(pl.BlockSpec(memory_space=space))
        given += in_hbm(array) if i in hbm else [array]
    vmem = pl.BlockSpec(memory_space=pltpu.VMEM)
    return pl.pallas_call(
        kernel,
        out_shape=out_shape,
        in_specs=specs,
        out_specs=[vmem] * len(out_shape) if isinstance(out_shape, list) else vmem,
        scratch_shapes=scratch,
        compiler_params=params(),
        name=name,
    )(*given)


def forward_kernel(own_ref, arrived_ref, out_ref):
    @pl.when(is_end())
    def _():
        out_ref[...] = own_ref[...]

    @pl.when(jnp.logical_not(is_end()))
    def _():
        out_ref[...] = (own_ref[...].astype(F32) + arrived_ref[...].astype(F32)).astype(BF16)


def nearly_kernel(base_ref, beside_ref, mirror_ref, out_ref):
    rows = beside_ref.shape[0]
    sums = base_ref[...] + mirror_ref[...].astype(F32)
    out_ref[0:rows, :] = sums[0:rows, :] + beside_ref[...].astype(F32)
    out_ref[rows:, :] = sums[rows:, :]


def final_kernel(base_ref, late_ref, out_hbm, out_ref, arrived):
    rows = base_ref.shape[0] - late_ref.shape[0]
    out_ref[0:rows, :] = base_ref[0:rows, :].astype(BF16)
    first = pltpu.make_async_copy(out_ref.at[0:rows, :], out_hbm.at[0:rows, :], arrived.at[0])
    first.start()
    out_ref[rows:, :] = (base_ref[rows:, :] + late_ref[...].astype(F32)).astype(BF16)
    second = pltpu.make_async_copy(out_ref.at[rows:, :], out_hbm.at[rows:, :], arrived.at[1])
    second.start()
    first.wait()
    second.wait()


def finish(base, late):
    vmem = pl.BlockSpec(memory_space=pltpu.VMEM)
    return pl.pallas_call(
        final_kernel,
        out_shape=jax.ShapeDtypeStruct(base.shape, BF16),
        in_specs=[vmem] * 2,
        out_specs=pl.BlockSpec(memory_space=pl.ANY),
        scratch_shapes=[pltpu.VMEM(base.shape, BF16), pltpu.SemaphoreType.DMA((2,))],
        compiler_params=params(),
        name="final",
    )(base, late)


def fast_body(n_seq, n_chan, query_in, key_in, value_in, filter_taps, skip_gain, out_weight):
    rows, width = query_in.shape
    groups = filter_taps.shape[0]
    part = groups // n_seq
    columns = out_weight.shape[1] // n_chan
    def over_seq(slots, orders):
        *going, staying = slots
        moved = []
        for k, value in enumerate(going):
            pairs = [
                (i * n_chan + j, (i ^ orders[j % 2][k]) * n_chan + j)
                for i in range(n_seq)
                for j in range(n_chan)
            ]
            moved.append(lax.ppermute(value, ("seq", "chan"), pairs))
        return moved + [staying]

    def over_chips(value, moves):
        return lax.ppermute(
            value, "chan", [(2 * a + c, 2 * b + c) for a, b in moves for c in range(2)]
        )

    def other_core(value):
        return lax.ppermute(value, "chan", [(i, i ^ 1) for i in range(n_chan)])

    other_weight = other_core(out_weight)
    mixed_in, *packed = products(key_in, value_in, filter_taps, n_seq)
    arrived = over_seq(packed, GOING)
    query, skip, weight = fetch(packed[-1], query_in, skip_gain, out_weight, columns)
    convolved = convolve(arrived, n_seq, rows, part)
    returned = over_seq(convolved, RETURNING)
    gated = gate(query, mixed_in, skip, returned)
    gated_other = other_core(gated)

    block = jax.ShapeDtypeStruct((rows, columns), BF16)
    block_f32 = jax.ShapeDtypeStruct((rows, columns), F32)
    halves = (gated, gated_other, weight, other_weight)

    half = run_kernel(half_kernel, "half", block_f32, [], gated, weight)
    by_two = run_kernel(add_half_kernel, "by_two", block, [], half, gated_other, other_weight)
    first = over_chips(by_two, [(0, 1), (3, 2), (1, 3), (2, 0)])
    beside = [(0, 1), (1, 0), (2, 3), (3, 2)]
    early = rows * EARLY_PARTS // 8 // 16 * 16
    pieces = [jax.ShapeDtypeStruct((n, columns), BF16) for n in (early, rows - early)]
    by_three = run_kernel(functools.partial(block_kernel, 3), "by_three", block, [], *halves)
    kernel = functools.partial(two_piece_kernel, 1)
    by_one, by_one_rest = run_kernel(kernel, "by_one", pieces, [], *halves, by_three)
    pair = over_chips(by_one, beside)
    summed = run_kernel(forward_kernel, "forward", block, [], by_three, first)
    mirror = over_chips(summed, [(0, 3), (3, 0), (1, 2), (2, 1)])
    by_one_rest = run_kernel(after_kernel, "after", pieces[1], [], by_one_rest, summed, pair)
    late = over_chips(by_one_rest, beside)
    base = run_kernel(base_kernel, "base", block_f32, [], *halves, first)
    nearly = run_kernel(nearly_kernel, "nearly", block_f32, [], base, pair, mirror)
    return finish(nearly, late)


def window_matrix(window, tile_size):
    reversed_window = window[:, ::-1]
    extended = jnp.concatenate(
        [reversed_window, jnp.zeros((window.shape[0], 1), window.dtype)], axis=1
    )
    repeated = jnp.tile(extended, (1, tile_size))[:, : tile_size * (2 * tile_size - 1)]
    return repeated.reshape(window.shape[0], tile_size, 2 * tile_size - 1)[:, :, tile_size - 1 :]


def accumulate(running, segment, tap_table, own_start):
    row_count, chan_width = running.shape
    group_count = tap_table.shape[0]
    tap_span = tap_table.shape[1] // 2
    group_width = chan_width // group_count
    block_rows = min(segment.shape[0], row_count)
    tile_size = math.gcd(math.gcd(block_rows, row_count), 128)
    out_tiles = row_count // tile_size
    in_tiles = block_rows // tile_size

    def one_block(step_index, current):
        block_start = step_index * block_rows
        in_blocks = lax.dynamic_slice_in_dim(segment, step_index * block_rows, block_rows, 0)
        in_blocks = in_blocks.reshape(in_tiles, tile_size, group_count, group_width)

        def add_block(previous):
            out_blocks = previous.reshape(out_tiles, tile_size, group_count, group_width)
            offset = own_start - block_start
            for lag_step in range(1 - in_tiles, out_tiles):
                tap_first = offset + lag_step * tile_size - (tile_size - 1) + tap_span
                window = lax.dynamic_slice_in_dim(tap_table, tap_first, 2 * tile_size - 1, 1)
                matrix = window_matrix(window, tile_size)
                first_out = max(0, lag_step)
                last_out = min(out_tiles, in_tiles + lag_step)
                addend = jnp.einsum(
                    "gij,qjgc->qigc",
                    matrix,
                    in_blocks[first_out - lag_step : last_out - lag_step],
                    preferred_element_type=jnp.float32,
                )
                out_blocks = out_blocks.at[first_out:last_out].add(addend)
            return out_blocks.reshape(previous.shape)

        def keep_same(previous):
            return previous

        needed = (block_start < own_start + row_count) & (block_start >= 0)
        return lax.cond(needed, add_block, keep_same, current)

    return lax.fori_loop(0, segment.shape[0] // block_rows, one_block, running)


def general_body(query_in, key_in, value_in, filter_taps, skip_gain, out_weight):
    row_count, chan_width = query_in.shape
    mixed_in = (key_in.astype(jnp.float32) * value_in.astype(jnp.float32)).astype(jnp.bfloat16)
    all_taps = lax.all_gather(filter_taps, "seq", axis=1, tiled=True)
    tap_table = jnp.concatenate([jnp.zeros_like(all_taps), all_taps], axis=1)
    seq_index = lax.axis_index("seq")
    own_start = seq_index * row_count
    zero_sum = jnp.zeros((row_count, chan_width), jnp.float32)
    convolved = accumulate(
        zero_sum, lax.all_gather(mixed_in, "seq", axis=0, tiled=True), tap_table, own_start
    )
    gated = (
        query_in.astype(jnp.float32)
        * (convolved + skip_gain[None, :] * mixed_in.astype(jnp.float32))
    ).astype(jnp.bfloat16)
    columns = lax.all_to_all(out_weight, "chan", split_axis=1, concat_axis=0, tiled=True)
    result = jnp.dot(
        lax.all_gather(gated, "chan", axis=1, tiled=True),
        columns,
        preferred_element_type=jnp.float32,
    )
    return result.astype(jnp.bfloat16)


def solution(mesh):
    n_seq, n_chan = mesh.shape["seq"], mesh.shape["chan"]

    def body(query_in, key_in, value_in, filter_taps, skip_gain, out_weight):
        rows, width = query_in.shape
        groups, span = filter_taps.shape
        part = groups // n_seq
        fits = (
            n_chan == 8
            and n_seq == len(GOING[0])
            and width == n_seq * LANES
            and part * n_seq == groups
            and part % 8 == 0
            and (part * (rows // LANES)) % 16 == 0
            and rows % (2 * LANES) == 0
            and (n_seq * rows) % (4 * LANES) == 0
            and span == rows
            and out_weight.shape[1] % (n_chan * LANES) == 0
        )
        run = functools.partial(fast_body, n_seq, n_chan) if fits else general_body
        return run(query_in, key_in, value_in, filter_taps, skip_gain, out_weight)

    placed = (
        P("seq", "chan"),
        P("seq", "chan"),
        P("seq", "chan"),
        P("chan", "seq"),
        P("chan"),
        P("chan", None),
    )
    return jax.shard_map(
        body, mesh=mesh, in_specs=placed, out_specs=P("seq", "chan"), check_vma=False
    )
```

```python
import functools
import math

import jax
import jax.numpy as jnp
from jax import lax
from jax.experimental import pallas as pl
from jax.experimental.pallas import tpu as pltpu
from jax.sharding import PartitionSpec as P

LANES = 128
DISTANCES = (2, 1, 3, 0)
EARLY_PARTS = 5
GOING = ((3, 1, 2, 0), (2, 3, 1, 0))
RETURNING = GOING
BF16 = jnp.bfloat16
F32 = jnp.float32
VMEM_LIMIT = 16 * 1024 * 1024


def params():
    return pltpu.CompilerParams(vmem_limit_bytes=VMEM_LIMIT)


def in_hbm(*arrays):
    return [pltpu.with_memory_space_constraint(a, pltpu.HBM) for a in arrays]


def away(orders, k):
    return jnp.where(core_place() == 0, orders[0][k], orders[1][k])


def seq_place():
    return lax.axis_index("seq")


def chip_place():
    return lax.axis_index("chan") // 2


def core_place():
    return lax.axis_index("chan") % 2


def lanes_at(block):
    return pl.ds(pl.multiple_of(block * LANES, LANES), LANES)


def rows_at(block, size):
    return pl.ds(pl.multiple_of(block * size, size), size)


def product_kernel(n_seq, key_hbm, value_hbm, taps_hbm, *refs):
    mixed_ref, *packed_refs = refs[: n_seq + 1]
    key_ref, value_ref, taps_ref, taps_f32, arrived = refs[n_seq + 1 :]
    rows = key_ref.shape[0]
    groups, span = taps_ref.shape
    part = groups // n_seq
    loads = [
        pltpu.make_async_copy(source, target, arrived.at[i])
        for i, (source, target) in enumerate(
            [
                (taps_hbm, taps_ref),
                (key_hbm, key_ref),
                (value_hbm, value_ref),
            ]
        )
    ]
    for load in loads:
        load.start()
    loads[0].wait()
    taps_f32[...] = taps_ref[...].astype(F32)
    for slot, packed_ref in enumerate(packed_refs):
        own = taps_f32[rows_at(seq_place() ^ away(GOING, slot), part), :]
        pieces = [own[:, k * LANES : (k + 1) * LANES] for k in range(span // LANES)]
        packed_ref[rows:, :] = jnp.concatenate(pieces, axis=0).astype(BF16)
    loads[1].wait()
    loads[2].wait()
    mixed_ref[...] = (key_ref[...].astype(F32) * value_ref[...].astype(F32)).astype(BF16)
    for slot, packed_ref in enumerate(packed_refs):
        packed_ref[0:rows, :] = mixed_ref[:, lanes_at(seq_place() ^ away(GOING, slot))]


def products(key_in, value_in, taps, n_seq):
    rows, width = key_in.shape
    groups, span = taps.shape
    tap_rows = (groups // n_seq) * (span // LANES)
    here = jax.ShapeDtypeStruct((rows, width), BF16)
    packed = jax.ShapeDtypeStruct((rows + tap_rows, LANES), BF16)
    return pl.pallas_call(
        functools.partial(product_kernel, n_seq),
        out_shape=[here] + [packed] * n_seq,
        in_specs=[pl.BlockSpec(memory_space=pl.ANY)] * 3,
        out_specs=[pl.BlockSpec(memory_space=pltpu.VMEM)] * (n_seq + 1),
        scratch_shapes=[
            pltpu.VMEM((rows, width), BF16),
            pltpu.VMEM((rows, width), BF16),
            pltpu.VMEM((groups, span), BF16),
            pltpu.VMEM((groups, span), F32),
            pltpu.SemaphoreType.DMA((3,)),
        ],
        compiler_params=params(),
        name="products",
    )(*in_hbm(key_in, value_in, taps))


def fetch_kernel(after_hbm, query_hbm, skip_hbm, weight_hbm, query_ref, skip_ref, weight_ref, arrived):
    loads = [
        pltpu.make_async_copy(query_hbm, query_ref, arrived.at[0]),
        pltpu.make_async_copy(skip_hbm, skip_ref, arrived.at[1]),
    ]
    for load in loads:
        load.start()
    for i, distance in enumerate(DISTANCES):
        loads.append(load_block(distance, weight_hbm, weight_ref.at[i], arrived.at[2 + i])[1])
    for load in loads:
        load.wait()


def fetch(after, query_in, skip_gain, out_weight, columns):
    vmem = pl.BlockSpec(memory_space=pltpu.VMEM)
    width = query_in.shape[1]
    return pl.pallas_call(
        fetch_kernel,
        out_shape=[
            jax.ShapeDtypeStruct(query_in.shape, BF16),
            jax.ShapeDtypeStruct((1, width), F32),
            jax.ShapeDtypeStruct((len(DISTANCES), width, columns), BF16),
        ],
        in_specs=[pl.BlockSpec(memory_space=pl.ANY)] * 4,
        out_specs=[vmem] * 3,
        scratch_shapes=[pltpu.SemaphoreType.DMA((2 + len(DISTANCES),))],
        compiler_params=params(),
        name="fetch",
    )(after, *in_hbm(query_in, skip_gain.reshape(1, -1), out_weight))


def conv_kernel(n_seq, rows, part, *refs):
    packed_refs = refs[:n_seq]
    out_refs = refs[n_seq : 2 * n_seq]
    signal, taps, total = refs[2 * n_seq :]
    per_shard = rows // LANES
    blocks = n_seq * per_shard
    group_width = LANES // part

    for slot, packed_ref in enumerate(packed_refs):
        first = (seq_place() ^ away(GOING, slot)) * per_shard
        tap_rows = packed_ref[rows:, :].astype(F32)
        for k in range(per_shard):
            tokens = packed_ref[k * LANES : (k + 1) * LANES, :]
            signal[first + k] = tokens.T
            taps[first + k] = tap_rows[k * part : (k + 1) * part, :]

    below = lax.broadcasted_iota(jnp.int32, (LANES, LANES), 0)
    lane = lax.broadcasted_iota(jnp.int32, (LANES, LANES), 1)
    for g in range(part):
        here = slice(g * group_width, (g + 1) * group_width)
        before = jnp.zeros((LANES, LANES), F32)
        by_lag = []
        for e in range(blocks):
            rolled = pltpu.roll(
                jnp.broadcast_to(taps[e, g : g + 1, :], (LANES, LANES)), 0, 1, stride=1, stride_axis=0
            )
            by_lag.append(jnp.where(lane >= below, rolled, before).astype(BF16))
            before = rolled
        sums = [None] * blocks
        for e in range(0, blocks, 2):
            left = signal[0 : blocks - e, here, :].reshape((blocks - e) * group_width, LANES)
            both = jnp.dot(
                left, jnp.concatenate(by_lag[e : e + 2], axis=1), preferred_element_type=F32
            )
            for q in range(blocks - e):
                piece = both[q * group_width : (q + 1) * group_width, :]
                for k in range(2):
                    at = q + e + k
                    if at < blocks:
                        addend = piece[:, k * LANES : (k + 1) * LANES]
                        sums[at] = addend if sums[at] is None else sums[at] + addend
        for q in range(blocks):
            total[q, here, :] = sums[q]

    for slot, out_ref in enumerate(out_refs):
        first = (seq_place() ^ away(RETURNING, slot)) * per_shard
        for k in range(per_shard):
            out_ref[k * LANES : (k + 1) * LANES, :] = total[first + k].astype(BF16).T


def convolve(packed, n_seq, rows, part):
    blocks = n_seq * rows // LANES
    vmem = pl.BlockSpec(memory_space=pltpu.VMEM)
    return pl.pallas_call(
        functools.partial(conv_kernel, n_seq, rows, part),
        out_shape=[jax.ShapeDtypeStruct((rows, LANES), BF16)] * n_seq,
        in_specs=[vmem] * n_seq,
        out_specs=[vmem] * n_seq,
        scratch_shapes=[
            pltpu.VMEM((blocks, LANES, LANES), BF16),
            pltpu.VMEM((blocks, part, LANES), F32),
            pltpu.VMEM((blocks, LANES, LANES), F32),
        ],
        compiler_params=params(),
        name="convolve",
    )(*packed)


def gate_kernel(n_seq, query_ref, mixed_ref, skip_ref, *refs):
    conv_refs, out_ref = refs[:n_seq], refs[n_seq]
    for slot, conv_ref in enumerate(conv_refs):
        lanes = lanes_at(seq_place() ^ away(RETURNING, slot))
        direct = skip_ref[:, lanes] * mixed_ref[:, lanes].astype(F32)
        out_ref[:, lanes] = (
            query_ref[:, lanes].astype(F32) * (conv_ref[...].astype(F32) + direct)
        ).astype(BF16)


def gate(query_in, mixed_in, skip_gain, parts):
    vmem = pl.BlockSpec(memory_space=pltpu.VMEM)
    return pl.pallas_call(
        functools.partial(gate_kernel, len(parts)),
        out_shape=jax.ShapeDtypeStruct(query_in.shape, BF16),
        in_specs=[vmem] * (3 + len(parts)),
        out_specs=vmem,
        compiler_params=params(),
        name="gate",
    )(query_in, mixed_in, skip_gain, *parts)


def load_block(distance, weight_hbm, weight, arrived):
    block = rows_at(2 * (chip_place() ^ distance) + core_place(), weight.shape[1])
    load = pltpu.make_async_copy(weight_hbm.at[:, block], weight, arrived)
    load.start()
    return block, load


def half_kernel(own_ref, weight, out_ref):
    out_ref[...] = jnp.dot(own_ref[...], weight[0], preferred_element_type=F32)


def add_half_kernel(half_ref, other_ref, other_weight, out_ref):
    block = rows_at(2 * (chip_place() ^ 2) + core_place(), out_ref.shape[1])
    late = jnp.dot(other_ref[...], other_weight[:, block], preferred_element_type=F32)
    out_ref[...] = (half_ref[...] + late).astype(BF16)


def both_halves(distance, own_ref, other_ref, own_weight, other_weight):
    weight = own_weight.at[DISTANCES.index(distance)]
    block = rows_at(2 * (chip_place() ^ distance) + core_place(), weight.shape[1])
    late = jnp.dot(other_ref[...], other_weight[:, block], preferred_element_type=F32)
    return late + jnp.dot(own_ref[...], weight[...], preferred_element_type=F32)


def two_piece_kernel(distance, own_ref, other_ref, own_weight, other_weight, first_ref, second_ref):
    block = both_halves(distance, own_ref, other_ref, own_weight, other_weight)
    rows = first_ref.shape[0]
    first_ref[...] = block[0:rows, :].astype(BF16)
    second_ref[...] = block[rows:, :].astype(BF16)


def after_kernel(from_ref, *refs):
    refs[-1][...] = from_ref[...]


def block_kernel(distance, own_ref, other_ref, own_weight, other_weight, *refs):
    refs[-1][...] = both_halves(distance, own_ref, other_ref, own_weight, other_weight).astype(BF16)


def is_end():
    return (chip_place() == 0) | (chip_place() == 3)


def base_kernel(own_ref, other_ref, own_weight, other_weight, first_ref, out_ref):
    base = both_halves(0, own_ref, other_ref, own_weight, other_weight)

    @pl.when(is_end())
    def _():
        out_ref[...] = base + first_ref[...].astype(F32)

    @pl.when(jnp.logical_not(is_end()))
    def _():
        out_ref[...] = base


def run_kernel(kernel, name, out_shape, scratch, *arrays, hbm=()):
    specs, given = [], []
    for i, array in enumerate(arrays):
        space = pl.ANY if i in hbm else pltpu.VMEM
        specs.append(pl.BlockSpec(memory_space=space))
        given += in_hbm(array) if i in hbm else [array]
    vmem = pl.BlockSpec(memory_space=pltpu.VMEM)
    return pl.pallas_call(
        kernel,
        out_shape=out_shape,
        in_specs=specs,
        out_specs=[vmem] * len(out_shape) if isinstance(out_shape, list) else vmem,
        scratch_shapes=scratch,
        compiler_params=params(),
        name=name,
    )(*given)


def forward_kernel(own_ref, arrived_ref, out_ref):
    @pl.when(is_end())
    def _():
        out_ref[...] = own_ref[...]

    @pl.when(jnp.logical_not(is_end()))
    def _():
        out_ref[...] = (own_ref[...].astype(F32) + arrived_ref[...].astype(F32)).astype(BF16)


def nearly_kernel(base_ref, beside_ref, mirror_ref, out_ref):
    rows = beside_ref.shape[0]
    sums = base_ref[...] + mirror_ref[...].astype(F32)
    out_ref[0:rows, :] = sums[0:rows, :] + beside_ref[...].astype(F32)
    out_ref[rows:, :] = sums[rows:, :]


def final_kernel(base_ref, late_ref, out_hbm, out_ref, arrived):
    rows = base_ref.shape[0] - late_ref.shape[0]
    out_ref[0:rows, :] = base_ref[0:rows, :].astype(BF16)
    first = pltpu.make_async_copy(out_ref.at[0:rows, :], out_hbm.at[0:rows, :], arrived.at[0])
    first.start()
    out_ref[rows:, :] = (base_ref[rows:, :] + late_ref[...].astype(F32)).astype(BF16)
    second = pltpu.make_async_copy(out_ref.at[rows:, :], out_hbm.at[rows:, :], arrived.at[1])
    second.start()
    first.wait()
    second.wait()


def finish(base, late):
    vmem = pl.BlockSpec(memory_space=pltpu.VMEM)
    return pl.pallas_call(
        final_kernel,
        out_shape=jax.ShapeDtypeStruct(base.shape, BF16),
        in_specs=[vmem] * 2,
        out_specs=pl.BlockSpec(memory_space=pl.ANY),
        scratch_shapes=[pltpu.VMEM(base.shape, BF16), pltpu.SemaphoreType.DMA((2,))],
        compiler_params=params(),
        name="final",
    )(base, late)


def fast_body(n_seq, n_chan, query_in, key_in, value_in, filter_taps, skip_gain, out_weight):
    rows, width = query_in.shape
    groups = filter_taps.shape[0]
    part = groups // n_seq
    columns = out_weight.shape[1] // n_chan
    def over_seq(slots, orders):
        *going, staying = slots
        moved = []
        for k, value in enumerate(going):
            pairs = [
                (i * n_chan + j, (i ^ orders[j % 2][k]) * n_chan + j)
                for i in range(n_seq)
                for j in range(n_chan)
            ]
            moved.append(lax.ppermute(value, ("seq", "chan"), pairs))
        return moved + [staying]

    def over_chips(value, moves):
        return lax.ppermute(
            value, "chan", [(2 * a + c, 2 * b + c) for a, b in moves for c in range(2)]
        )

    def other_core(value):
        return lax.ppermute(value, "chan", [(i, i ^ 1) for i in range(n_chan)])

    other_weight = other_core(out_weight)
    mixed_in, *packed = products(key_in, value_in, filter_taps, n_seq)
    arrived = over_seq(packed, GOING)
    query, skip, weight = fetch(packed[-1], query_in, skip_gain, out_weight, columns)
    convolved = convolve(arrived, n_seq, rows, part)
    returned = over_seq(convolved, RETURNING)
    gated = gate(query, mixed_in, skip, returned)
    gated_other = other_core(gated)

    block = jax.ShapeDtypeStruct((rows, columns), BF16)
    block_f32 = jax.ShapeDtypeStruct((rows, columns), F32)
    halves = (gated, gated_other, weight, other_weight)

    half = run_kernel(half_kernel, "half", block_f32, [], gated, weight)
    by_two = run_kernel(add_half_kernel, "by_two", block, [], half, gated_other, other_weight)
    first = over_chips(by_two, [(0, 1), (3, 2), (1, 3), (2, 0)])
    beside = [(0, 1), (1, 0), (2, 3), (3, 2)]
    early = rows * EARLY_PARTS // 8 // 16 * 16
    pieces = [jax.ShapeDtypeStruct((n, columns), BF16) for n in (early, rows - early)]
    kernel = functools.partial(two_piece_kernel, 1)
    by_one, by_one_rest = run_kernel(kernel, "by_one", pieces, [], *halves)
    pair = over_chips(by_one, beside)
    by_three = run_kernel(functools.partial(block_kernel, 3), "by_three", block, [], *halves)
    summed = run_kernel(forward_kernel, "forward", block, [], by_three, first)
    mirror = over_chips(summed, [(0, 3), (3, 0), (1, 2), (2, 1)])
    by_one_rest = run_kernel(after_kernel, "after", pieces[1], [], by_one_rest, summed, pair)
    late = over_chips(by_one_rest, beside)
    base = run_kernel(base_kernel, "base", block_f32, [], *halves, first)
    nearly = run_kernel(nearly_kernel, "nearly", block_f32, [], base, pair, mirror)
    return finish(nearly, late)


def window_matrix(window, tile_size):
    reversed_window = window[:, ::-1]
    extended = jnp.concatenate(
        [reversed_window, jnp.zeros((window.shape[0], 1), window.dtype)], axis=1
    )
    repeated = jnp.tile(extended, (1, tile_size))[:, : tile_size * (2 * tile_size - 1)]
    return repeated.reshape(window.shape[0], tile_size, 2 * tile_size - 1)[:, :, tile_size - 1 :]


def accumulate(running, segment, tap_table, own_start):
    row_count, chan_width = running.shape
    group_count = tap_table.shape[0]
    tap_span = tap_table.shape[1] // 2
    group_width = chan_width // group_count
    block_rows = min(segment.shape[0], row_count)
    tile_size = math.gcd(math.gcd(block_rows, row_count), 128)
    out_tiles = row_count // tile_size
    in_tiles = block_rows // tile_size

    def one_block(step_index, current):
        block_start = step_index * block_rows
        in_blocks = lax.dynamic_slice_in_dim(segment, step_index * block_rows, block_rows, 0)
        in_blocks = in_blocks.reshape(in_tiles, tile_size, group_count, group_width)

        def add_block(previous):
            out_blocks = previous.reshape(out_tiles, tile_size, group_count, group_width)
            offset = own_start - block_start
            for lag_step in range(1 - in_tiles, out_tiles):
                tap_first = offset + lag_step * tile_size - (tile_size - 1) + tap_span
                window = lax.dynamic_slice_in_dim(tap_table, tap_first, 2 * tile_size - 1, 1)
                matrix = window_matrix(window, tile_size)
                first_out = max(0, lag_step)
                last_out = min(out_tiles, in_tiles + lag_step)
                addend = jnp.einsum(
                    "gij,qjgc->qigc",
                    matrix,
                    in_blocks[first_out - lag_step : last_out - lag_step],
                    preferred_element_type=jnp.float32,
                )
                out_blocks = out_blocks.at[first_out:last_out].add(addend)
            return out_blocks.reshape(previous.shape)

        def keep_same(previous):
            return previous

        needed = (block_start < own_start + row_count) & (block_start >= 0)
        return lax.cond(needed, add_block, keep_same, current)

    return lax.fori_loop(0, segment.shape[0] // block_rows, one_block, running)


def general_body(query_in, key_in, value_in, filter_taps, skip_gain, out_weight):
    row_count, chan_width = query_in.shape
    mixed_in = (key_in.astype(jnp.float32) * value_in.astype(jnp.float32)).astype(jnp.bfloat16)
    all_taps = lax.all_gather(filter_taps, "seq", axis=1, tiled=True)
    tap_table = jnp.concatenate([jnp.zeros_like(all_taps), all_taps], axis=1)
    seq_index = lax.axis_index("seq")
    own_start = seq_index * row_count
    zero_sum = jnp.zeros((row_count, chan_width), jnp.float32)
    convolved = accumulate(
        zero_sum, lax.all_gather(mixed_in, "seq", axis=0, tiled=True), tap_table, own_start
    )
    gated = (
        query_in.astype(jnp.float32)
        * (convolved + skip_gain[None, :] * mixed_in.astype(jnp.float32))
    ).astype(jnp.bfloat16)
    columns = lax.all_to_all(out_weight, "chan", split_axis=1, concat_axis=0, tiled=True)
    result = jnp.dot(
        lax.all_gather(gated, "chan", axis=1, tiled=True),
        columns,
        preferred_element_type=jnp.float32,
    )
    return result.astype(jnp.bfloat16)


def solution(mesh):
    n_seq, n_chan = mesh.shape["seq"], mesh.shape["chan"]

    def body(query_in, key_in, value_in, filter_taps, skip_gain, out_weight):
        rows, width = query_in.shape
        groups, span = filter_taps.shape
        part = groups // n_seq
        fits = (
            n_chan == 8
            and n_seq == len(GOING[0])
            and width == n_seq * LANES
            and part * n_seq == groups
            and part % 8 == 0
            and (part * (rows // LANES)) % 16 == 0
            and rows % (2 * LANES) == 0
            and (n_seq * rows) % (4 * LANES) == 0
            and span == rows
            and out_weight.shape[1] % (n_chan * LANES) == 0
        )
        run = functools.partial(fast_body, n_seq, n_chan) if fits else general_body
        return run(query_in, key_in, value_in, filter_taps, skip_gain, out_weight)

    placed = (
        P("seq", "chan"),
        P("seq", "chan"),
        P("seq", "chan"),
        P("chan", "seq"),
        P("chan"),
        P("chan", None),
    )
    return jax.shard_map(
        body, mesh=mesh, in_specs=placed, out_specs=P("seq", "chan"), check_vma=False
    )
```
